32 devices in a mesh: groups: 2 (over x), wide: 8 (over z, y), narrow: 2 (over core).
Axes of the slice: x: 2, y: 2, z: 4, core: 2. Of those that a mesh axis runs over, the one named last changes fastest.
Arguments:
- queries: bfloat16 [64, 6144], P(('groups', 'wide'), 'narrow'), parts along dimension 0
- new_keys: bfloat16 [64, 1024], P(('groups', 'wide'), 'narrow'), parts along dimension 0, may hold values from -6 to 6
- new_values: bfloat16 [64, 1024], P(('groups', 'wide'), 'narrow'), parts along dimension 0, may hold values from -6 to 6
- key_cache: bfloat16 [64, 512, 1024], P(('groups', 'wide'), None, 'narrow'), parts along dimension 0
- value_cache: bfloat16 [64, 512, 1024], P(('groups', 'wide'), None, 'narrow'), parts along dimension 0, may hold values from -6 to 6
- lengths: int32 [64], P(('groups', 'wide')), parts along dimension 0, may hold values from 32 to 512, as said below
- assignment: int32 [64], P(('groups', 'wide')), parts along dimension 0, may hold values from 0 to 31, as said below
- tokens: bfloat16 [64, 6144], P(('groups', 'wide')), parts along dimension 0, may hold values from -6 to 6
- norm_gain: float32 [6144], replicated, may hold values from 0.25 to 1.75
- routes: int32 [64, 2], P('groups'), parts along dimension 0, may hold values from 0 to 7, all different within a row; in each aligned block of 32 rows (0 to 31, 32 to 63, ...) at most 16 rows name the same one
- route_logits: float32 [64, 2], P('groups'), parts along dimension 0, may hold values from -6 to 6
- w_gate: bfloat16 [2, 6144, 8192], P('narrow', None, 'wide'), may hold values from -0.078125 to 0.078125
- w_up: bfloat16 [2, 6144, 8192], P('narrow', None, 'wide'), may hold values from -0.078125 to 0.078125
- w_down: bfloat16 [2, 8192, 6144], P('narrow', 'wide'), may hold values from -0.0625 to 0.0625
Outputs:
- context: bfloat16 [64, 6144], P(('groups', 'wide'), 'narrow'), parts along dimension 0
- mixed_out: bfloat16 [64, 6144], P(('groups', 'wide')), parts along dimension 0
The draws below stay inside these ranges and needn't reach their ends.
There are 2 independent parts, one for each index of `groups`. The reference program is written for one: setup_inputs(seed, part) draws one part's arguments, and reference() takes and returns one part's arrays. A program takes and returns all parts, laid end to end along the dimension named above; an argument that names none is the same for every part. Nothing has to cross between parts.
Inputs may be any that keep to these rules, and one draw needn't show every extreme that they name: `assignment`: the requests of the micro-batch in some order, each once. `lengths`: some slot has exactly 512 and some exactly 32 positions. `routes`: each row names two different experts; no expert is named by more than 16 rows, a bound that some block reaches.
All inputs are finite; a program needn't handle non-finite values.
Results may differ from the reference program's by a relative error of at most 0.0049.
Values may be sent and summed in bfloat16 or wider, within the bound.
No kernel may reach another device: no remote copies, remote signals or barrier semaphores. Data moves between devices by JAX's collectives and lax.ppermute only.
A program may use at most 128 MiB of HBM per device.

```python
import math
import jax
import jax.numpy as jnp
import numpy as np
from jax import lax

D = 6144
HQ = 48
KVH = 8
HD = 128
EXPERTS = 8
FFW = 8192
CTX = 512
EXP_WIN = 2
REQS = 32
CAP = 16


def base_keys(key):
    return jax.random.normal(jax.random.fold_in(key, 11), (REQS, CTX, KVH * HD), jnp.float32)


def slot_order(key):
    return jax.random.permutation(jax.random.fold_in(key, 13), REQS).astype(jnp.int32)


def draw_key_cache(key, part):
    shared = base_keys(key)
    return shared.astype(jnp.bfloat16)


def draw_queries(key, part):
    key = jax.random.fold_in(key, 5)
    entries = jax.random.normal(key, (REQS, HQ * HD), jnp.float32)
    return entries.astype(jnp.bfloat16)


def draw_lengths(key, part):
    key = jax.random.fold_in(key, 7)
    drawn = jax.random.randint(jax.random.fold_in(key, 1), (REQS,), CTX // 16, CTX + 1, jnp.int32)
    longest = jax.random.randint(jax.random.fold_in(key, 2), (), 0, REQS, jnp.int32)
    drawn = drawn.at[longest].set(CTX)
    drawn = drawn.at[(longest + 1) % REQS].set(CTX // 16)
    return drawn


def draw_assignment(key, part):
    return slot_order(key)


def steps_of(rng, shape, cuts, low, largest):
    gain, own = 1.0, jax.random.fold_in(rng, 6)
    for axis_at, parts in cuts:
        draws = jnp.exp(jax.random.uniform(jax.random.fold_in(own, axis_at), (parts,), jnp.float32, low / len(cuts), largest / len(cuts)))
        gain = gain * jnp.repeat(draws, shape[axis_at] // parts).reshape([-1 if axis == axis_at else 1 for axis in range(len(shape))])
    return gain


def shared_out(key, own, number, rows, amount, top, bound, slope):
    order = jax.random.permutation(key, amount)
    crowded, usual = portions_of(amount, rows * top, bound, slope, True), portions_of(amount, rows * top, bound, slope, False)
    places = jnp.arange(amount)

    def named(tallies, rotation):
        used = int((tallies > 0).sum())
        fixed = max(1, used // 4)
        shifted = fixed + (places - fixed + rotation * (used - fixed)) % max(1, amount - fixed)
        return jnp.zeros((amount,), jnp.int32).at[order[jnp.where(places < fixed, places, shifted)]].set(jnp.asarray(tallies, jnp.int32))

    tallies = jnp.where(number % 4 == 0, named(crowded, number // 4), named(usual, number - number // 4 - 1))
    mixed = jax.random.permutation(jax.random.fold_in(own, 3), amount)
    source_of, taker = mixed[0:amount // 2 * 2:2], mixed[1:amount // 2 * 2:2]
    room = jnp.minimum(tallies[source_of] - 1, bound - tallies[taker]) // 2
    room = jnp.where((source_of == order[0]) | (taker == order[0]) | (tallies[taker] == 0), 0, jnp.maximum(room, 0))
    shifted = jax.random.randint(jax.random.fold_in(own, 4), (amount // 2,), 0, 1 << 20) % (room + 1)
    tallies = tallies.at[source_of].add(-shifted).at[taker].add(shifted)
    members = jnp.searchsorted(jnp.cumsum(tallies), jnp.arange(rows * top), side="right").astype(jnp.int32)
    grid = members.reshape(top, rows).T
    grid = grid[jax.random.permutation(jax.random.fold_in(own, 1), rows)]
    rotation = jax.random.randint(jax.random.fold_in(own, 2), (rows, 1), 0, top)
    return jnp.take_along_axis(grid, (jnp.arange(top)[None, :] + rotation) % top, axis=1)


def portions_of(amount, total, most, slope, full):
    loads = [(1 << 20) // math.isqrt(standing ** slope) + 1 for standing in range(1, amount + 1)]
    largest = most if full else min(most, max(-(-total // amount), total * loads[0] // sum(loads)))
    least = 1 if total - largest >= amount - 1 else 0
    holding, surplus = [largest] + [least] * (amount - 1), total - largest - least * (amount - 1)
    while surplus > 0:
        free = [i for i in range(1, amount) if holding[i] < largest] or [i for i in range(1, amount) if holding[i] < most]
        whole, budget = sum([loads[i] for i in free]), surplus
        for i in free:
            addition = min(most - holding[i], max(1, budget * loads[i] // whole), surplus)
            holding[i] = holding[i] + addition
            surplus = surplus - addition
    return np.array(holding)


def gaussian(own_key, extent, spread, limit, split=(), held_as=jnp.bfloat16):
    values = jax.random.normal(own_key, extent, jnp.float32) * spread
    if len(split) > 0:
        values = steps_of(own_key, extent, split, -0.22, 0.18) * values
    return jnp.clip(values, min=-limit, max=limit).astype(held_as)


def setup_inputs(seed: int = 0, part: int = 0) -> dict:
    streams_of = jax.random.split(jax.random.key(seed), 15)
    part_splits = jax.random.split(jax.random.fold_in(streams_of[14], part), 15)
    queries = draw_queries(jax.random.fold_in(jax.random.fold_in(streams_of[14], part), 71), part)
    new_keys = gaussian(part_splits[1], (REQS, KVH * HD), 1.0, 6.0, ((0, 8), (1, 2)))
    new_values = gaussian(part_splits[2], (REQS, KVH * HD), 1.0, 6.0, ((0, 8), (1, 2)))
    key_cache = draw_key_cache(jax.random.fold_in(jax.random.fold_in(streams_of[14], part), 71), part)
    value_cache = gaussian(part_splits[4], (REQS, CTX, KVH * HD), 1.0, 6.0, ((0, 8), (2, 2)))
    lengths = draw_lengths(jax.random.fold_in(jax.random.fold_in(streams_of[14], part), 71), part)
    assignment = draw_assignment(jax.random.fold_in(jax.random.fold_in(streams_of[14], part), 71), part)
    tokens = gaussian(part_splits[7], (REQS, D), 1.0, 6.0, ((0, 8),))
    norm_gain = jnp.clip(1.0 + 0.15 * jax.random.normal(streams_of[8], (D,), jnp.float32), 0.25, 1.75)
    routes_keys = jax.random.split(jax.random.fold_in(part_splits[9], 1), REQS // REQS)
    routes_turns = jax.random.permutation(jax.random.fold_in(part_splits[9], 3), REQS // REQS)
    routes = jax.vmap(lambda own, number: shared_out(jax.random.fold_in(part_splits[9], 2), own, number, REQS, EXPERTS, 2, CAP, 2))(routes_keys, routes_turns).reshape((REQS, 2))
    route_logits = gaussian(part_splits[10], (REQS, 2), 2.0, 6.0, (), jnp.float32)
    w_gate = gaussian(streams_of[11], (EXP_WIN, D, FFW), D ** -0.5, 0.078125, ((0, 2), (2, 8)))
    w_up = gaussian(streams_of[12], (EXP_WIN, D, FFW), D ** -0.5, 0.078125, ((0, 2), (2, 8)))
    w_down = gaussian(streams_of[13], (EXP_WIN, FFW, D), FFW ** -0.5, 0.0625, ((0, 2), (1, 8)))
    return dict(queries=queries, new_keys=new_keys, new_values=new_values, key_cache=key_cache, value_cache=value_cache, lengths=lengths, assignment=assignment, tokens=tokens, norm_gain=norm_gain, routes=routes, route_logits=route_logits, w_gate=w_gate, w_up=w_up, w_down=w_down)


def expert_weights(routes, route_logits, expert):
    first_prob = 1.0 / (1.0 + jnp.exp(route_logits[:, 1] - route_logits[:, 0]))
    second_prob = 1.0 - first_prob
    chosen = (routes == expert).astype(jnp.float32)
    return chosen[:, 0] * first_prob + chosen[:, 1] * second_prob

def reference(queries, new_keys, new_values, key_cache, value_cache, lengths, assignment, tokens, norm_gain, routes, route_logits, w_gate, w_up, w_down):
    head_group = HQ // KVH
    score_scale = HD ** (-0.5)
    slot_queries = jnp.take(queries, assignment, axis=0).astype(jnp.float32).reshape(REQS, KVH, head_group, HD)
    slot_keys = jnp.take(new_keys, assignment, axis=0).astype(jnp.float32).reshape(REQS, KVH, HD)
    slot_values = jnp.take(new_values, assignment, axis=0).astype(jnp.float32).reshape(REQS, KVH, HD)
    cache_keys = key_cache.astype(jnp.float32).reshape(REQS, CTX, KVH, HD)
    cache_values = value_cache.astype(jnp.float32).reshape(REQS, CTX, KVH, HD)
    scores = jnp.einsum('rgjd,rtgd->rgjt', slot_queries, cache_keys) * score_scale
    own_score = jnp.einsum('rgjd,rgd->rgj', slot_queries, slot_keys) * score_scale
    positions = jnp.arange(CTX, dtype=jnp.int32)
    is_valid = positions[None, :] < lengths[:, None]
    scores = jnp.where(is_valid[:, None, None, :], scores, -jnp.inf)
    row_max = jnp.maximum(lax.optimization_barrier(jnp.max(scores, axis=-1)), own_score)
    weights = jnp.exp(scores - row_max[..., None])
    own_weight = jnp.exp(own_score - row_max)
    denominator = lax.optimization_barrier(jnp.sum(weights, axis=-1)) + own_weight
    attn_probs = (weights / denominator[..., None]).astype(jnp.bfloat16)
    own_prob = (own_weight / denominator).astype(jnp.bfloat16)
    mixed_heads = jnp.einsum('rgjt,rtgd->rgjd', attn_probs.astype(jnp.float32), cache_values)
    mixed_heads = mixed_heads + own_prob.astype(jnp.float32)[..., None] * slot_values[:, :, None, :]
    context = mixed_heads.reshape(REQS, HQ * HD).astype(jnp.bfloat16)
    values = tokens.astype(jnp.float32)
    normed = (values * lax.rsqrt(lax.optimization_barrier(jnp.mean(values * values, axis=-1, keepdims=True)) + 1e-05) * norm_gain).astype(jnp.bfloat16)
    expert_sum = jnp.zeros((REQS, D), jnp.float32)
    for expert in range(EXP_WIN):
        weight = expert_weights(routes, route_logits, expert)
        gate_out = jnp.dot(normed, w_gate[expert], preferred_element_type=jnp.float32)
        up_out = jnp.dot(normed, w_up[expert], preferred_element_type=jnp.float32)
        hidden = (weight[:, None] * jax.nn.silu(gate_out) * up_out).astype(jnp.bfloat16)
        expert_sum = expert_sum + jnp.dot(hidden, w_down[expert], preferred_element_type=jnp.float32)
    mixed_out = (values + expert_sum).astype(jnp.bfloat16)
    return (context, mixed_out)
```

```python
import jax
import jax.numpy as jnp
from jax import lax
from jax.sharding import PartitionSpec as P

HQ = 48
KVH = 8
HD = 128
CTX = 512


def partner(index, step):
    return index ^ step


def swap(block, axis, count, step):
    return lax.ppermute(block, axis, [(i, partner(i, step)) for i in range(count)])


def expert_weights(routes, route_logits, expert):
    first_prob = 1.0 / (1.0 + jnp.exp(route_logits[:, 1] - route_logits[:, 0]))
    second_prob = 1.0 - first_prob
    chosen = (routes == expert).astype(jnp.float32)
    return chosen[:, 0] * first_prob + chosen[:, 1] * second_prob


def attention(query_rows, key_rows, value_rows, key_cache, value_cache, lengths):
    head_group = HQ // KVH
    slot_count = key_cache.shape[0]
    kv_local = key_cache.shape[2] // HD
    score_scale = HD ** (-0.5)
    query_heads = query_rows.reshape(slot_count, kv_local, head_group, HD)
    own_keys = key_rows.reshape(slot_count, kv_local, HD)
    own_values = value_rows.reshape(slot_count, kv_local, HD)
    cache_keys = key_cache.reshape(slot_count, CTX, kv_local, HD)
    cache_values = value_cache.reshape(slot_count, CTX, kv_local, HD)
    own_score = (
        jnp.einsum("rgjd,rgd->rgj", query_heads, own_keys, preferred_element_type=jnp.float32)
        * score_scale
    )
    scores = (
        jnp.einsum("rgjd,rtgd->rgjt", query_heads, cache_keys, preferred_element_type=jnp.float32)
        * score_scale
    )
    positions = jnp.arange(CTX, dtype=jnp.int32)
    is_valid = positions[None, :] < lengths[:, None]
    scores = jnp.where(is_valid[:, None, None, :], scores, -jnp.inf)
    row_max = jnp.maximum(jnp.max(scores, axis=-1), own_score)
    weights = jnp.exp(scores - row_max[..., None])
    own_weight = jnp.exp(own_score - row_max)
    denominator = jnp.sum(weights, axis=-1) + own_weight
    attn_probs = (weights / denominator[..., None]).astype(jnp.bfloat16)
    own_prob = (own_weight / denominator).astype(jnp.bfloat16)
    mixed_heads = jnp.einsum(
        "rgjt,rtgd->rgjd", attn_probs, cache_values, preferred_element_type=jnp.float32
    )
    mixed_heads = (
        mixed_heads
        + own_prob.astype(jnp.float32)[..., None] * own_values.astype(jnp.float32)[:, :, None, :]
    )
    return mixed_heads.reshape(slot_count, kv_local * head_group * HD).astype(jnp.bfloat16)


def make_local(wide):
    def local(
        queries,
        new_keys,
        new_values,
        key_cache,
        value_cache,
        lengths,
        assignment,
        tokens,
        norm_gain,
        routes,
        route_logits,
        w_gate,
        w_up,
        w_down,
    ):
        rows = tokens.shape[0]
        width = tokens.shape[1]
        half = width // 2
        me = lax.axis_index("wide")
        core = lax.axis_index("narrow")
        blocks = jnp.stack([partner(me, step) for step in range(wide)])

        token_rows = jnp.concatenate(
            [tokens] + [swap(tokens, "wide", wide, step) for step in range(1, wide)], axis=0
        )
        mine = jnp.concatenate([queries, new_keys, new_values], axis=1)
        fetched = jnp.concatenate(
            [mine] + [swap(mine, "wide", wide, step) for step in range(1, wide)], axis=0
        )

        values = token_rows.astype(jnp.float32)
        normed = (
            values
            * lax.rsqrt(jnp.mean(values * values, axis=-1, keepdims=True) + 1e-05)
            * norm_gain
        ).astype(jnp.bfloat16)
        weight_all = expert_weights(routes, route_logits, core)
        weight_all = jnp.take(weight_all.reshape(wide, rows), blocks, axis=0).reshape(-1)
        gate_out = jnp.dot(normed, w_gate[0], preferred_element_type=jnp.float32)
        up_out = jnp.dot(normed, w_up[0], preferred_element_type=jnp.float32)
        hidden = (weight_all[:, None] * jax.nn.silu(gate_out) * up_out).astype(jnp.bfloat16)
        terms = jnp.dot(hidden, w_down[0], preferred_element_type=jnp.float32)

        given = lax.dynamic_slice_in_dim(terms, (1 - core) * half, half, 1)
        kept = lax.dynamic_slice_in_dim(terms, core * half, half, 1)
        terms = kept + swap(given.astype(jnp.bfloat16), "narrow", 2, 1).astype(jnp.float32)
        sent = terms.astype(jnp.bfloat16)
        total = terms[:rows]
        for step in range(1, wide):
            block = sent[step * rows : (step + 1) * rows]
            total = total + swap(block, "wide", wide, step).astype(jnp.float32)
        own = lax.dynamic_slice_in_dim(tokens, core * half, half, 1).astype(jnp.float32)
        piece = (own + total).astype(jnp.bfloat16)
        other = swap(piece, "narrow", 2, 1)
        first = jnp.where(core == 0, piece, other)
        second = jnp.where(core == 0, other, piece)
        mixed_out = jnp.concatenate([first, second], axis=1)

        place = assignment // rows
        found = partner(place, me) * rows + assignment % rows
        slots = jnp.take(fetched, found, axis=0)
        q_width, k_width = queries.shape[1], new_keys.shape[1]
        context = attention(
            slots[:, :q_width],
            slots[:, q_width : q_width + k_width],
            slots[:, q_width + k_width :],
            key_cache,
            value_cache,
            lengths,
        )
        return (context, mixed_out)

    return local


def solution(mesh):
    placed = (
        P(("groups", "wide"), "narrow"),
        P(("groups", "wide"), "narrow"),
        P(("groups", "wide"), "narrow"),
        P(("groups", "wide"), None, "narrow"),
        P(("groups", "wide"), None, "narrow"),
        P(("groups", "wide")),
        P(("groups", "wide")),
        P(("groups", "wide"), None),
        P(),
        P("groups", None),
        P("groups", None),
        P("narrow", None, "wide"),
        P("narrow", None, "wide"),
        P("narrow", "wide", None),
    )
    return jax.shard_map(
        make_local(mesh.shape["wide"]),
        mesh=mesh,
        in_specs=placed,
        out_specs=(P(("groups", "wide"), "narrow"), P(("groups", "wide"), None)),
        check_vma=False,
    )
```

```python
import jax
import jax.numpy as jnp
from jax import lax
from jax.sharding import PartitionSpec as P

HQ = 48
KVH = 8
HD = 128
CTX = 512


def swap(block, axis, count, step):
    return lax.ppermute(block, axis, [(i, i ^ step) for i in range(count)])


def spread(block, wide):
    copies = jnp.broadcast_to(block[None], (wide,) + block.shape)
    return lax.all_to_all(copies, "wide", 0, 0, tiled=True).reshape(-1, block.shape[1])


def expert_weights(routes, route_logits, expert):
    first_prob = 1.0 / (1.0 + jnp.exp(route_logits[:, 1] - route_logits[:, 0]))
    second_prob = 1.0 - first_prob
    chosen = (routes == expert).astype(jnp.float32)
    return chosen[:, 0] * first_prob + chosen[:, 1] * second_prob


def attention(query_rows, key_rows, value_rows, key_cache, value_cache, lengths):
    head_group = HQ // KVH
    slot_count = key_cache.shape[0]
    kv_local = key_cache.shape[2] // HD
    score_scale = HD ** (-0.5)
    query_heads = query_rows.reshape(slot_count, kv_local, head_group, HD)
    own_keys = key_rows.reshape(slot_count, kv_local, HD)
    own_values = value_rows.reshape(slot_count, kv_local, HD)
    cache_keys = key_cache.reshape(slot_count, CTX, kv_local, HD)
    cache_values = value_cache.reshape(slot_count, CTX, kv_local, HD)
    own_score = (
        jnp.einsum("rgjd,rgd->rgj", query_heads, own_keys, preferred_element_type=jnp.float32)
        * score_scale
    )
    scores = (
        jnp.einsum("rgjd,rtgd->rgjt", query_heads, cache_keys, preferred_element_type=jnp.float32)
        * score_scale
    )
    positions = jnp.arange(CTX, dtype=jnp.int32)
    is_valid = positions[None, :] < lengths[:, None]
    scores = jnp.where(is_valid[:, None, None, :], scores, -jnp.inf)
    row_max = jnp.maximum(jnp.max(scores, axis=-1), own_score)
    weights = jnp.exp(scores - row_max[..., None])
    own_weight = jnp.exp(own_score - row_max)
    denominator = jnp.sum(weights, axis=-1) + own_weight
    attn_probs = (weights / denominator[..., None]).astype(jnp.bfloat16)
    own_prob = (own_weight / denominator).astype(jnp.bfloat16)
    mixed_heads = jnp.einsum(
        "rgjt,rtgd->rgjd", attn_probs, cache_values, preferred_element_type=jnp.float32
    )
    mixed_heads = (
        mixed_heads
        + own_prob.astype(jnp.float32)[..., None] * own_values.astype(jnp.float32)[:, :, None, :]
    )
    return mixed_heads.reshape(slot_count, kv_local * head_group * HD).astype(jnp.bfloat16)


def make_local(wide):
    def local(
        queries,
        new_keys,
        new_values,
        key_cache,
        value_cache,
        lengths,
        assignment,
        tokens,
        norm_gain,
        routes,
        route_logits,
        w_gate,
        w_up,
        w_down,
    ):
        rows = tokens.shape[0]
        width = tokens.shape[1]
        half = width // 2
        me = lax.axis_index("wide")
        core = lax.axis_index("narrow")
        part = lax.dynamic_slice_in_dim(tokens, core * half, half, 1)
        part_rows = spread(part, wide)
        other_rows = swap(part_rows, "narrow", 2, 1)
        token_rows = jnp.concatenate(
            [
                jnp.where(core == 0, part_rows, other_rows),
                jnp.where(core == 0, other_rows, part_rows),
            ],
            axis=1,
        )
        mine = jnp.concatenate([queries, new_keys, new_values], axis=1)
        fetched = spread(mine, wide)

        values = token_rows.astype(jnp.float32)
        normed = (
            values
            * lax.rsqrt(jnp.mean(values * values, axis=-1, keepdims=True) + 1e-05)
            * norm_gain
        ).astype(jnp.bfloat16)
        weight_all = expert_weights(routes, route_logits, core)
        gate_out = jnp.dot(normed, w_gate[0], preferred_element_type=jnp.float32)
        up_out = jnp.dot(normed, w_up[0], preferred_element_type=jnp.float32)
        hidden = (weight_all[:, None] * jax.nn.silu(gate_out) * up_out).astype(jnp.bfloat16)
        terms = jnp.dot(hidden, w_down[0], preferred_element_type=jnp.float32)

        given = lax.dynamic_slice_in_dim(terms, (1 - core) * half, half, 1)
        kept = lax.dynamic_slice_in_dim(terms, core * half, half, 1)
        terms = kept + swap(given.astype(jnp.bfloat16), "narrow", 2, 1).astype(jnp.float32)
        sent = terms.astype(jnp.bfloat16)
        pieces = lax.all_to_all(sent.reshape(wide, rows, half), "wide", 0, 0, tiled=True)
        total = jnp.sum(pieces.astype(jnp.float32), axis=0)
        own = lax.dynamic_slice_in_dim(tokens, core * half, half, 1).astype(jnp.float32)
        piece = (own + total).astype(jnp.bfloat16)
        other = swap(piece, "narrow", 2, 1)
        first = jnp.where(core == 0, piece, other)
        second = jnp.where(core == 0, other, piece)
        mixed_out = jnp.concatenate([first, second], axis=1)

        slots = jnp.take(fetched, assignment, axis=0)
        q_width, k_width = queries.shape[1], new_keys.shape[1]
        context = attention(
            slots[:, :q_width],
            slots[:, q_width : q_width + k_width],
            slots[:, q_width + k_width :],
            key_cache,
            value_cache,
            lengths,
        )
        return (context, mixed_out)

    return local


def solution(mesh):
    placed = (
        P(("groups", "wide"), "narrow"),
        P(("groups", "wide"), "narrow"),
        P(("groups", "wide"), "narrow"),
        P(("groups", "wide"), None, "narrow"),
        P(("groups", "wide"), None, "narrow"),
        P(("groups", "wide")),
        P(("groups", "wide")),
        P(("groups", "wide"), None),
        P(),
        P("groups", None),
        P("groups", None),
        P("narrow", None, "wide"),
        P("narrow", None, "wide"),
        P("narrow", "wide", None),
    )
    return jax.shard_map(
        make_local(mesh.shape["wide"]),
        mesh=mesh,
        in_specs=placed,
        out_specs=(P(("groups", "wide"), "narrow"), P(("groups", "wide"), None)),
        check_vma=False,
    )
```

```python
import functools
import math

import jax
import jax.numpy as jnp
from jax import lax
from jax.experimental import pallas as pl
from jax.experimental.pallas import tpu as pltpu
from jax.sharding import PartitionSpec as P

HQ = 48
KVH = 8
HD = 128
GROUP = HQ // KVH
SCALE = HD ** (-0.5)
TILE = 256
CUTS = 4
MIB = 1024 * 1024


def steps_of(wide):
    return [wide >> (i + 1) for i in range(int(math.log2(wide)))]


def swap(block, axis, count, step):
    return lax.ppermute(block, axis, [(i, i ^ step) for i in range(count)])


def owner_of(place, me, steps):
    found = me
    for bit, step in enumerate(steps):
        found = found ^ (((place >> bit) & 1) * step)
    return found


def place_of(owner, me, steps):
    differ = owner ^ me
    found = 0
    for bit, step in enumerate(steps):
        shift = int(math.log2(step))
        found = found | (((differ >> shift) & 1) << bit)
    return found


def call(kernel, outs, ins, scratch=(), flops=0, size=0, limit=16, smem=(), far=()):
    spaces = [pltpu.SMEM if i in smem else pl.ANY if i in far else pltpu.VMEM for i in range(len(ins))]
    return pl.pallas_call(
        kernel,
        name=getattr(kernel, "func", kernel).__name__,
        out_shape=outs,
        in_specs=[pl.BlockSpec(memory_space=space) for space in spaces],
        out_specs=jax.tree.map(lambda _: pl.BlockSpec(memory_space=pltpu.VMEM), outs),
        scratch_shapes=list(scratch),
        compiler_params=pltpu.CompilerParams(vmem_limit_bytes=limit * MIB),
        cost_estimate=pl.CostEstimate(flops=flops, bytes_accessed=size, transcendentals=0),
    )(*ins)


def row_copies(source, target, sems, first):
    rows = target.shape[0] // CUTS
    return [
        pltpu.make_async_copy(
            source.at[0, pl.ds(pl.multiple_of(first + i * rows, rows), rows), :],
            target.at[pl.ds(i * rows, rows), :],
            sems.at[i],
        )
        for i in range(CUTS)
    ]


def column_copies(source, target, sems, first):
    columns = target.shape[1] // CUTS
    return [
        pltpu.make_async_copy(
            source.at[0, :, pl.ds(pl.multiple_of(first + i * columns, columns), columns)],
            target.at[:, pl.ds(i * columns, columns)],
            sems.at[i],
        )
        for i in range(CUTS)
    ]


def load(other, source, after, target, sems):
    core = lax.axis_index("narrow")
    side = 1 - core if other else core
    copies = row_copies(source, target, sems, side * target.shape[0])
    for copy in copies:
        copy.start()
    for copy in copies:
        copy.wait()


def shape(dims, dtype):
    return jax.ShapeDtypeStruct(dims, dtype)


def near(array):
    return pltpu.with_memory_space_constraint(array, pltpu.VMEM)


def distant(array):
    return pltpu.with_memory_space_constraint(array, pltpu.HBM)


def prepare(far_tokens, far_gain, far_query, far_key, far_value, out_ref, heads_ref, *held):
    *near_refs, packed, sems = held
    far_refs = (far_tokens, far_gain, far_query, far_key, far_value)
    copies = [
        pltpu.make_async_copy(far, ref, sems.at[i])
        for i, (far, ref) in enumerate(zip(far_refs, near_refs))
    ]
    for copy in copies:
        copy.start()
    for copy in copies:
        copy.wait()
    tokens_ref, gain_ref, *head_refs = near_refs
    half = out_ref.shape[1]
    core = lax.axis_index("narrow")
    values = tokens_ref[...].astype(jnp.float32)
    scale = lax.rsqrt(jnp.mean(values * values, axis=-1, keepdims=True) + 1e-05)
    normed = (values * scale * gain_ref[...]).astype(jnp.bfloat16)
    out_ref[...] = jnp.where(core == 0, normed[:, :half], normed[:, half:])
    rows = tokens_ref.shape[0]
    at = 0
    each = heads_ref.shape[0] // rows
    for ref in head_refs:
        block = ref[...].astype(jnp.float32)
        for head in range(ref.shape[1] // HD):
            packed[pl.ds(at, rows, stride=each), :] = block[:, head * HD : (head + 1) * HD]
            at += 1
    heads_ref[...] = packed[...].astype(jnp.bfloat16)


def grow(own_ref, got_ref, after, out_ref):
    both = [own_ref[...].astype(jnp.float32), got_ref[...].astype(jnp.float32)]
    out_ref[...] = jnp.concatenate(both, axis=0).astype(jnp.bfloat16)


def gate_first(x_ref, gate_ref, up_ref, far_up, gate_out, up_out, up_rest, sems):
    core = lax.axis_index("narrow")
    copies = row_copies(far_up, up_rest, sems, (1 - core) * up_rest.shape[0])
    for copy in copies:
        copy.start()
    tile = min(TILE, gate_ref.shape[1])

    @pl.loop(0, gate_ref.shape[1] // tile)
    def _(i):
        columns = pl.ds(pl.multiple_of(i * tile, tile), tile)
        x = x_ref[...]
        gate_out[:, columns] = jnp.dot(x, gate_ref[:, columns], preferred_element_type=jnp.float32)
        up_out[:, columns] = jnp.dot(x, up_ref[:, columns], preferred_element_type=jnp.float32)

    for copy in copies:
        copy.wait()


def gate_second(
    steps,
    rows,
    x_ref,
    gate_ref,
    up_ref,
    gate_part,
    up_part,
    routes_ref,
    logits_ref,
    far_down,
    hidden_out,
    given_out,
    down_own,
    down_other,
    sems,
):
    count, depth = x_ref.shape
    core = lax.axis_index("narrow")
    me = lax.axis_index("wide")
    other_copies = column_copies(far_down, down_other, sems.at[0], (1 - core) * depth)
    own_copies = column_copies(far_down, down_own, sems.at[1], core * depth)
    for copy in other_copies + own_copies:
        copy.start()
    tile = min(TILE, gate_ref.shape[1])

    logits = logits_ref[...]
    first = 1.0 / (1.0 + jnp.exp(logits[1:2] - logits[0:1]))
    second = 1.0 - first
    chosen = (routes_ref[...] == core).astype(jnp.float32)
    weight_row = chosen[0:1] * first + chosen[1:2] * second
    row = lax.broadcasted_iota(jnp.int32, (count, count), 0)
    column = lax.broadcasted_iota(jnp.int32, (count, count), 1)
    shift = int(math.log2(rows))
    token = (owner_of(row >> shift, me, steps) << shift) | (row & (rows - 1))
    weight = jnp.sum(jnp.where(token == column, weight_row, 0.0), axis=1, keepdims=True)

    @pl.loop(0, gate_ref.shape[1] // tile)
    def _(i):
        columns = pl.ds(pl.multiple_of(i * tile, tile), tile)
        x = x_ref[...]
        gate = gate_part[:, columns] + jnp.dot(
            x, gate_ref[:, columns], preferred_element_type=jnp.float32
        )
        up = up_part[:, columns] + jnp.dot(
            x, up_ref[:, columns], preferred_element_type=jnp.float32
        )
        hidden_out[:, columns] = (weight * (gate * jax.nn.sigmoid(gate)) * up).astype(jnp.bfloat16)

    span = depth // CUTS
    for cut, copy in enumerate(other_copies):
        copy.wait()
        columns = slice(cut * span, (cut + 1) * span)
        given_out[:, columns] = jnp.dot(
            hidden_out[...], down_other[:, columns], preferred_element_type=jnp.float32
        ).astype(jnp.bfloat16)
    for copy in own_copies:
        copy.wait()


def down_first(hidden_ref, down_ref, out_ref):
    @pl.loop(0, out_ref.shape[1] // TILE)
    def _(i):
        columns = pl.ds(pl.multiple_of(i * TILE, TILE), TILE)
        out_ref[:, columns] = jnp.dot(
            hidden_ref[...], down_ref[:, columns], preferred_element_type=jnp.float32
        )


def combine(terms_ref, taken_ref, after, kept_ref, sent_ref):
    total = terms_ref[...] + taken_ref[...].astype(jnp.float32)
    kept = kept_ref.shape[0]
    kept_ref[...] = total[:kept]
    sent_ref[...] = total[kept:].astype(jnp.bfloat16)


def finish(terms_ref, taken_ref, tokens_ref, out_ref):
    half = out_ref.shape[1]
    core = lax.axis_index("narrow")
    own = tokens_ref[...].astype(jnp.float32)
    own = jnp.where(core == 0, own[:, :half], own[:, half:])
    total = terms_ref[...] + taken_ref[...].astype(jnp.float32)
    out_ref[...] = (own + total).astype(jnp.bfloat16)


def join(own_ref, other_ref, out_ref):
    half = own_ref.shape[1]
    core = lax.axis_index("narrow")
    own, other = own_ref[...], other_ref[...]
    out_ref[:, :half] = jnp.where(core == 0, own, other)
    out_ref[:, half:] = jnp.where(core == 0, other, own)


def attend(
    steps, taking, near_ref, far_ref, keys_ref, values_ref, lengths_ref, place_ref, after, out_ref
):
    slots, span, width = keys_ref.shape
    rows = slots
    kv_local = width // HD
    heads = kv_local * GROUP
    each = heads + 2 * kv_local
    me = lax.axis_index("wide")
    shift = int(math.log2(rows))
    half = near_ref.shape[0]
    head_of = lax.broadcasted_iota(jnp.int32, (heads, 1), 0)
    positions = lax.broadcasted_iota(jnp.int32, (heads, span), 1)

    def by_group(pieces):
        result = pieces[0]
        for g in range(1, kv_local):
            result = jnp.where(head_of >= g * GROUP, pieces[g], result)
        return result

    for order, slot in enumerate(taking):
        request = place_ref[slot]
        at = (place_of(request >> shift, me, steps) << shift) | (request & (rows - 1))
        at = at * each
        inside = pl.ds(pl.multiple_of(jnp.where(at < half, at, at - half), each), each)
        block = jnp.where(at < half, near_ref[inside, :], far_ref[inside, :])
        query = block[:heads]
        own = block[heads:].astype(jnp.float32)
        own_key = by_group([own[g : g + 1] for g in range(kv_local)])
        own_value = by_group([own[kv_local + g : kv_local + g + 1] for g in range(kv_local)])
        own_score = jnp.sum(query.astype(jnp.float32) * own_key, axis=1, keepdims=True) * SCALE
        scores = by_group(
            [
                lax.dot_general(
                    query,
                    keys_ref[slot, :, g * HD : (g + 1) * HD],
                    (((1,), (1,)), ((), ())),
                    preferred_element_type=jnp.float32,
                )
                for g in range(kv_local)
            ]
        )
        scores = jnp.where(positions < lengths_ref[slot], scores * SCALE, -jnp.inf)
        row_max = jnp.maximum(jnp.max(scores, axis=1, keepdims=True), own_score)
        weights = jnp.exp(scores - row_max)
        own_weight = jnp.exp(own_score - row_max)
        total = jnp.sum(weights, axis=1, keepdims=True) + own_weight
        probs = (weights / total).astype(jnp.bfloat16)
        own_prob = (own_weight / total).astype(jnp.bfloat16).astype(jnp.float32)
        mixed = by_group(
            [
                jnp.dot(
                    probs,
                    values_ref[slot, :, g * HD : (g + 1) * HD],
                    preferred_element_type=jnp.float32,
                )
                for g in range(kv_local)
            ]
        )
        out_ref[order * heads : (order + 1) * heads, :] = mixed + own_prob * own_value


def lay_out(heads, pieces, out_ref, held):
    at = 0
    for piece in pieces:
        held[at : at + piece.shape[0], :] = piece[...]
        at += piece.shape[0]
    for head in range(heads):
        out_ref[:, head * HD : (head + 1) * HD] = held[
            pl.ds(head, out_ref.shape[0], stride=heads), :
        ].astype(jnp.bfloat16)


def attend_last(steps, taking, heads, *refs):
    *ins, early, out_ref, late, held = refs
    attend(steps, taking, *ins, late)
    lay_out(heads, [early, late], out_ref, held)


def make_local(wide):
    steps = steps_of(wide)

    def local(
        queries,
        new_keys,
        new_values,
        key_cache,
        value_cache,
        lengths,
        assignment,
        tokens,
        norm_gain,
        routes,
        route_logits,
        w_gate,
        w_up,
        w_down,
    ):
        rows, width = tokens.shape
        half = width // 2
        units = w_gate.shape[2]
        count = rows * wide
        each = (queries.shape[1] + 2 * new_keys.shape[1]) // HD
        core = lax.axis_index("narrow")
        bf16, f32 = jnp.bfloat16, jnp.float32
        heads_local = queries.shape[1] // HD
        dma = pltpu.SemaphoreType.DMA
        piece_bytes = 2 * half * units

        firsts = [tokens, norm_gain[None], queries, new_keys, new_values]
        x, heads = call(
            prepare,
            [shape((rows, half), bf16), shape((rows * each, HD), bf16)],
            [distant(a) for a in firsts],
            [pltpu.VMEM(a.shape, a.dtype) for a in firsts]
            + [pltpu.VMEM((rows * each, HD), f32), dma((len(firsts),))],
            size=100000,
            far=range(len(firsts)),
        )

        def loaded(weights, other, after):
            return call(
                functools.partial(load, other),
                pltpu.VMEM((half, units), bf16),
                [distant(weights), after],
                [dma((CUTS,))],
                size=piece_bytes,
                far=(0, 1),
            )

        pieces = []
        far_heads = None
        for order, step in enumerate(steps):
            got = swap(x, "wide", wide, step)
            got_heads = swap(heads, "wide", wide, step)
            if order < 3:
                pieces.append(loaded((w_gate, w_up, w_gate)[order], order == 2, x))
            x = call(
                grow,
                shape((2 * x.shape[0], half), bf16),
                [x, got, near(pieces[-1])],
                size=8 * x.size,
                far=(2,),
            )
            if order < len(steps) - 1:
                heads = jnp.concatenate([heads, got_heads], axis=0)
            else:
                far_heads = got_heads

        product = 2 * count * half * units
        other_x = swap(x, "narrow", 2, 1)
        part = shape((count, units), f32)
        gate_part, up_part, up_rest = call(
            gate_first,
            [part, part, pltpu.VMEM((half, units), bf16)],
            [x, near(pieces[0]), near(pieces[1]), distant(w_up)],
            [dma((CUTS,))],
            flops=2 * product,
            size=3 * piece_bytes,
            far=(3,),
        )
        hidden, given, down_piece = call(
            functools.partial(gate_second, steps, rows),
            [shape((count, units), bf16), shape((count, half), bf16), pltpu.VMEM((units, half), bf16)],
            [
                other_x,
                near(pieces[2]),
                near(up_rest),
                gate_part,
                up_part,
                routes.T,
                route_logits.T,
                distant(w_down),
            ],
            [pltpu.VMEM((units, half), bf16), dma((2, CUTS))],
            flops=3 * product,
            size=4 * piece_bytes,
            far=(7,),
        )
        taken = swap(given, "narrow", 2, 1)
        terms = call(
            down_first,
            shape((count, half), f32),
            [hidden, near(down_piece)],
            flops=product,
            size=piece_bytes,
        )

        caches = [near(key_cache), near(value_cache), lengths, assignment]
        slots = queries.shape[0]
        early = None
        context = None
        after = hidden
        for order, step in enumerate(reversed(steps)):
            kept = terms.shape[0] // 2
            terms, sent = call(
                combine,
                [shape((kept, half), f32), shape((kept, half), bf16)],
                [terms, taken, after],
                size=terms.size * 8,
                far=(2,),
            )
            taken = swap(sent, "wide", wide, step)
            if order == 0:
                early = call(
                    functools.partial(attend, steps, list(range(slots // 2))),
                    shape((slots // 2 * heads_local, HD), f32),
                    [heads, far_heads, *caches, sent],
                    flops=2 * key_cache.size * GROUP,
                    size=2 * key_cache.size,
                    smem=(4, 5),
                    far=(6,),
                )
                after = early
            elif order == 1:
                context = call(
                    functools.partial(attend_last, steps, list(range(slots // 2, slots)), heads_local),
                    shape(queries.shape, bf16),
                    [heads, far_heads, *caches, sent, early],
                    [
                        pltpu.VMEM(((slots - slots // 2) * heads_local, HD), f32),
                        pltpu.VMEM((slots * heads_local, HD), f32),
                    ],
                    flops=2 * key_cache.size * GROUP,
                    size=2 * key_cache.size,
                    smem=(4, 5),
                    far=(6,),
                )
                after = distant(context)

        piece = call(finish, shape((rows, half), bf16), [terms, taken, tokens], size=terms.size * 8)
        other = swap(piece, "narrow", 2, 1)
        mixed_out = call(join, shape((rows, width), bf16), [piece, other], size=terms.size * 4)
        return (context, mixed_out)

    return local


def solution(mesh):
    placed = (
        P(("groups", "wide"), "narrow"),
        P(("groups", "wide"), "narrow"),
        P(("groups", "wide"), "narrow"),
        P(("groups", "wide"), None, "narrow"),
        P(("groups", "wide"), None, "narrow"),
        P(("groups", "wide")),
        P(("groups", "wide")),
        P(("groups", "wide"), None),
        P(),
        P("groups", None),
        P("groups", None),
        P("narrow", None, "wide"),
        P("narrow", None, "wide"),
        P("narrow", "wide", None),
    )
    return jax.shard_map(
        make_local(mesh.shape["wide"]),
        mesh=mesh,
        in_specs=placed,
        out_specs=(P(("groups", "wide"), "narrow"), P(("groups", "wide"), None)),
        check_vma=False,
    )
```

```python
import functools
import math

import jax
import jax.numpy as jnp
from jax import lax
from jax.experimental import pallas as pl
from jax.experimental.pallas import tpu as pltpu
from jax.sharding import PartitionSpec as P

HQ = 48
KVH = 8
HD = 128
GROUP = HQ // KVH
SCALE = HD ** (-0.5)
TILE = 256
WIDE_TILE = 768
CUTS = 4
MIB = 1024 * 1024


def steps_of(wide):
    return [wide >> (i + 1) for i in range(int(math.log2(wide)))]


def swap(block, axis, count, step):
    return lax.ppermute(block, axis, [(i, i ^ step) for i in range(count)])


def owner_of(place, me, steps):
    found = me
    for bit, step in enumerate(steps):
        found = found ^ (((place >> bit) & 1) * step)
    return found


def place_of(owner, me, steps):
    differ = owner ^ me
    found = 0
    for bit, step in enumerate(steps):
        shift = int(math.log2(step))
        found = found | (((differ >> shift) & 1) << bit)
    return found


def call(kernel, outs, ins, scratch=(), flops=0, size=0, limit=16, smem=(), far=()):
    spaces = [pltpu.SMEM if i in smem else pl.ANY if i in far else pltpu.VMEM for i in range(len(ins))]
    return pl.pallas_call(
        kernel,
        name=getattr(kernel, "func", kernel).__name__,
        out_shape=outs,
        in_specs=[pl.BlockSpec(memory_space=space) for space in spaces],
        out_specs=jax.tree.map(lambda _: pl.BlockSpec(memory_space=pltpu.VMEM), outs),
        scratch_shapes=list(scratch),
        compiler_params=pltpu.CompilerParams(vmem_limit_bytes=limit * MIB),
        cost_estimate=pl.CostEstimate(flops=flops, bytes_accessed=size, transcendentals=0),
    )(*ins)


def column_copies(source, target, sems, first):
    columns = target.shape[1] // CUTS
    return [
        pltpu.make_async_copy(
            source.at[0, :, pl.ds(pl.multiple_of(first + i * columns, columns), columns)],
            target.at[:, pl.ds(i * columns, columns)],
            sems.at[i],
        )
        for i in range(CUTS)
    ]


def shape(dims, dtype):
    return jax.ShapeDtypeStruct(dims, dtype)


def near(array):
    return pltpu.with_memory_space_constraint(array, pltpu.VMEM)


def distant(array):
    return pltpu.with_memory_space_constraint(array, pltpu.HBM)


def prepare(far_tokens, far_gain, far_query, far_key, far_value, out_ref, heads_ref, *held):
    *near_refs, packed, sems = held
    far_refs = (far_tokens, far_gain, far_query, far_key, far_value)
    copies = [
        pltpu.make_async_copy(far, ref, sems.at[i])
        for i, (far, ref) in enumerate(zip(far_refs, near_refs))
    ]
    for copy in copies:
        copy.start()
    for copy in copies:
        copy.wait()
    tokens_ref, gain_ref, *head_refs = near_refs
    half = out_ref.shape[1]
    core = lax.axis_index("narrow")
    values = tokens_ref[...].astype(jnp.float32)
    scale = lax.rsqrt(jnp.mean(values * values, axis=-1, keepdims=True) + 1e-05)
    normed = (values * scale * gain_ref[...]).astype(jnp.bfloat16)
    out_ref[...] = jnp.where(core == 0, normed[:, :half], normed[:, half:])
    rows = tokens_ref.shape[0]
    at = 0
    each = heads_ref.shape[0] // rows
    for ref in head_refs:
        block = ref[...].astype(jnp.float32)
        for head in range(ref.shape[1] // HD):
            packed[pl.ds(at, rows, stride=each), :] = block[:, head * HD : (head + 1) * HD]
            at += 1
    heads_ref[...] = packed[...].astype(jnp.bfloat16)


def stacked(own_ref, got_ref):
    both = [own_ref[...].astype(jnp.float32), got_ref[...].astype(jnp.float32)]
    return jnp.concatenate(both, axis=0).astype(jnp.bfloat16)


def grow(own_ref, got_ref, *refs):
    refs[-1][...] = stacked(own_ref, got_ref)


def grow_both(own_ref, got_ref, own_heads, got_heads, *refs):
    refs[-2][...] = stacked(own_ref, got_ref)
    refs[-1][...] = stacked(own_heads, got_heads)


def gate_all(
    steps,
    rows,
    x_ref,
    other_ref,
    gate_ref,
    up_ref,
    routes_ref,
    logits_ref,
    far_down,
    hidden_out,
    given_out,
    down_own,
    down_other,
    sems,
):
    count, depth = x_ref.shape
    core = lax.axis_index("narrow")
    me = lax.axis_index("wide")
    other_copies = column_copies(far_down, down_other, sems.at[0], (1 - core) * depth)
    own_copies = column_copies(far_down, down_own, sems.at[1], core * depth)
    for copy in other_copies + own_copies:
        copy.start()
    tile = min(TILE, gate_ref.shape[2])
    own = pl.ds(pl.multiple_of(core * depth, depth), depth)
    other = pl.ds(pl.multiple_of((1 - core) * depth, depth), depth)

    logits = logits_ref[...]
    first = 1.0 / (1.0 + jnp.exp(logits[1:2] - logits[0:1]))
    second = 1.0 - first
    chosen = (routes_ref[...] == core).astype(jnp.float32)
    weight_row = chosen[0:1] * first + chosen[1:2] * second
    row = lax.broadcasted_iota(jnp.int32, (count, count), 0)
    column = lax.broadcasted_iota(jnp.int32, (count, count), 1)
    shift = int(math.log2(rows))
    token = (owner_of(row >> shift, me, steps) << shift) | (row & (rows - 1))
    weight = jnp.sum(jnp.where(token == column, weight_row, 0.0), axis=1, keepdims=True)

    @pl.loop(0, gate_ref.shape[2] // tile)
    def _(i):
        columns = pl.ds(pl.multiple_of(i * tile, tile), tile)
        x, y = x_ref[...], other_ref[...]
        gate = jnp.dot(x, gate_ref[0, own, columns], preferred_element_type=jnp.float32)
        gate += jnp.dot(y, gate_ref[0, other, columns], preferred_element_type=jnp.float32)
        up = jnp.dot(x, up_ref[0, own, columns], preferred_element_type=jnp.float32)
        up += jnp.dot(y, up_ref[0, other, columns], preferred_element_type=jnp.float32)
        hidden_out[:, columns] = (weight * (gate * jax.nn.sigmoid(gate)) * up).astype(jnp.bfloat16)

    span = depth // CUTS
    for cut, copy in enumerate(other_copies):
        copy.wait()
        columns = slice(cut * span, (cut + 1) * span)
        given_out[:, columns] = jnp.dot(
            hidden_out[...], down_other[:, columns], preferred_element_type=jnp.float32
        ).astype(jnp.bfloat16)
    for copy in own_copies:
        copy.wait()


def down_first(hidden_ref, down_ref, out_ref):
    @pl.loop(0, out_ref.shape[1] // WIDE_TILE)
    def _(i):
        columns = pl.ds(pl.multiple_of(i * WIDE_TILE, WIDE_TILE), WIDE_TILE)
        out_ref[:, columns] = jnp.dot(
            hidden_ref[...], down_ref[:, columns], preferred_element_type=jnp.float32
        )


def combine(terms_ref, taken_ref, after, kept_ref, sent_ref):
    total = terms_ref[...] + taken_ref[...].astype(jnp.float32)
    kept = kept_ref.shape[0]
    kept_ref[...] = total[:kept]
    sent_ref[...] = total[kept:].astype(jnp.bfloat16)


def part_last(terms_ref, taken_ref, after, kept_ref, sent_ref):
    total = (terms_ref[...] + taken_ref[...].astype(jnp.float32)).astype(jnp.bfloat16)
    kept = kept_ref.shape[0]
    kept_ref[...] = total[:kept]
    sent_ref[...] = total[kept:]


def finish(kept_ref, taken_ref, other_kept, other_taken, tokens_ref, out_ref):
    half = kept_ref.shape[1]
    core = lax.axis_index("narrow")
    own = kept_ref[...].astype(jnp.float32) + taken_ref[...].astype(jnp.float32)
    other = other_kept[...].astype(jnp.float32) + other_taken[...].astype(jnp.float32)
    tokens = tokens_ref[...].astype(jnp.float32)
    first = tokens[:, :half] + jnp.where(core == 0, own, other)
    second = tokens[:, half:] + jnp.where(core == 0, other, own)
    out_ref[:, :half] = first.astype(jnp.bfloat16)
    out_ref[:, half:] = second.astype(jnp.bfloat16)


def attend(
    steps, taking, near_ref, far_ref, keys_ref, values_ref, lengths_ref, place_ref, after, out_ref
):
    slots, span, width = keys_ref.shape
    rows = slots
    kv_local = width // HD
    heads = kv_local * GROUP
    each = heads + 2 * kv_local
    me = lax.axis_index("wide")
    shift = int(math.log2(rows))
    half = near_ref.shape[0]
    head_of = lax.broadcasted_iota(jnp.int32, (heads, 1), 0)
    positions = lax.broadcasted_iota(jnp.int32, (heads, span), 1)

    def by_group(pieces):
        result = pieces[0]
        for g in range(1, kv_local):
            result = jnp.where(head_of >= g * GROUP, pieces[g], result)
        return result

    for order, slot in enumerate(taking):
        request = place_ref[slot]
        at = (place_of(request >> shift, me, steps) << shift) | (request & (rows - 1))
        at = at * each
        inside = pl.ds(pl.multiple_of(jnp.where(at < half, at, at - half), each), each)
        block = jnp.where(at < half, near_ref[inside, :], far_ref[inside, :])
        query = block[:heads]
        own = block[heads:].astype(jnp.float32)
        own_key = by_group([own[g : g + 1] for g in range(kv_local)])
        own_value = by_group([own[kv_local + g : kv_local + g + 1] for g in range(kv_local)])
        own_score = jnp.sum(query.astype(jnp.float32) * own_key, axis=1, keepdims=True) * SCALE
        scores = by_group(
            [
                lax.dot_general(
                    query,
                    keys_ref[slot, :, g * HD : (g + 1) * HD],
                    (((1,), (1,)), ((), ())),
                    preferred_element_type=jnp.float32,
                )
                for g in range(kv_local)
            ]
        )
        scores = jnp.where(positions < lengths_ref[slot], scores * SCALE, -jnp.inf)
        row_max = jnp.maximum(jnp.max(scores, axis=1, keepdims=True), own_score)
        weights = jnp.exp(scores - row_max)
        own_weight = jnp.exp(own_score - row_max)
        total = jnp.sum(weights, axis=1, keepdims=True) + own_weight
        probs = (weights / total).astype(jnp.bfloat16)
        own_prob = (own_weight / total).astype(jnp.bfloat16).astype(jnp.float32)
        mixed = by_group(
            [
                jnp.dot(
                    probs,
                    values_ref[slot, :, g * HD : (g + 1) * HD],
                    preferred_element_type=jnp.float32,
                )
                for g in range(kv_local)
            ]
        )
        out_ref[order * heads : (order + 1) * heads, :] = mixed + own_prob * own_value


def lay_out(heads, pieces, out_ref, held):
    at = 0
    for piece in pieces:
        held[at : at + piece.shape[0], :] = piece[...]
        at += piece.shape[0]
    for head in range(heads):
        out_ref[:, head * HD : (head + 1) * HD] = held[
            pl.ds(head, out_ref.shape[0], stride=heads), :
        ].astype(jnp.bfloat16)


def attend_last(steps, taking, heads, *refs):
    *ins, early, out_ref, late, held = refs
    attend(steps, taking, *ins, late)
    lay_out(heads, [early, late], out_ref, held)


def make_local(wide):
    steps = steps_of(wide)

    def local(
        queries,
        new_keys,
        new_values,
        key_cache,
        value_cache,
        lengths,
        assignment,
        tokens,
        norm_gain,
        routes,
        route_logits,
        w_gate,
        w_up,
        w_down,
    ):
        rows, width = tokens.shape
        half = width // 2
        units = w_gate.shape[2]
        count = rows * wide
        each = (queries.shape[1] + 2 * new_keys.shape[1]) // HD
        core = lax.axis_index("narrow")
        bf16, f32 = jnp.bfloat16, jnp.float32
        heads_local = queries.shape[1] // HD
        dma = pltpu.SemaphoreType.DMA
        piece_bytes = 2 * half * units

        firsts = [tokens, norm_gain[None], queries, new_keys, new_values]
        x, heads = call(
            prepare,
            [shape((rows, half), bf16), shape((rows * each, HD), bf16)],
            [distant(a) for a in firsts],
            [pltpu.VMEM(a.shape, a.dtype) for a in firsts]
            + [pltpu.VMEM((rows * each, HD), f32), dma((len(firsts),))],
            size=100000,
            far=range(len(firsts)),
        )

        for order, step in enumerate(steps):
            ins = [x, swap(x, "wide", wide, step)]
            outs = [shape((2 * x.shape[0], half), bf16)]
            if order > 0:
                ins += [heads, swap(heads, "wide", wide, steps[order - 1])]
                outs += [shape((2 * heads.shape[0], HD), bf16)]
            far = (len(ins),)
            ins += [distant(w_gate)]
            if order == 0:
                x = call(grow, outs[0], ins, size=8 * x.size, far=far)
            else:
                x, heads = call(grow_both, outs, ins, size=8 * (x.size + heads.size), far=far)
        far_heads = swap(heads, "wide", wide, steps[-1])

        product = 2 * count * half * units
        other_x = swap(x, "narrow", 2, 1)
        hidden, given, down_piece = call(
            functools.partial(gate_all, steps, rows),
            [shape((count, units), bf16), shape((count, half), bf16), pltpu.VMEM((units, half), bf16)],
            [
                x,
                other_x,
                near(w_gate),
                near(w_up),
                routes.T,
                route_logits.T,
                distant(w_down),
            ],
            [pltpu.VMEM((units, half), bf16), dma((2, CUTS))],
            flops=5 * product,
            size=6 * piece_bytes,
            far=(6,),
        )
        taken = swap(given, "narrow", 2, 1)
        terms = call(
            down_first,
            shape((count, half), f32),
            [hidden, near(down_piece)],
            flops=product,
            size=piece_bytes,
        )

        caches = [near(key_cache), near(value_cache), lengths, assignment]
        slots = queries.shape[0]
        early = None
        context = None
        after = hidden
        for order, step in enumerate(reversed(steps)):
            kept = terms.shape[0] // 2
            last = order == len(steps) - 1
            terms, sent = call(
                part_last if last else combine,
                [shape((kept, half), bf16 if last else f32), shape((kept, half), bf16)],
                [terms, taken, after],
                size=terms.size * 8,
                far=(2,),
            )
            taken = swap(sent, "wide", wide, step)
            if order == 0:
                early = call(
                    functools.partial(attend, steps, list(range(slots // 2))),
                    shape((slots // 2 * heads_local, HD), f32),
                    [heads, far_heads, *caches, sent],
                    flops=2 * key_cache.size * GROUP,
                    size=2 * key_cache.size,
                    smem=(4, 5),
                    far=(6,),
                )
                after = early
            elif order == 1:
                context = call(
                    functools.partial(attend_last, steps, list(range(slots // 2, slots)), heads_local),
                    shape(queries.shape, bf16),
                    [heads, far_heads, *caches, sent, early],
                    [
                        pltpu.VMEM(((slots - slots // 2) * heads_local, HD), f32),
                        pltpu.VMEM((slots * heads_local, HD), f32),
                    ],
                    flops=2 * key_cache.size * GROUP,
                    size=2 * key_cache.size,
                    smem=(4, 5),
                    far=(6,),
                )
                after = distant(context)

        crossed = [(i, ((i >> 1) ^ steps[0]) * 2 + (1 - (i & 1))) for i in range(2 * wide)]
        other_taken = lax.ppermute(sent, ("wide", "narrow"), crossed)
        other_kept = swap(terms, "narrow", 2, 1)
        mixed_out = call(
            finish,
            shape((rows, width), bf16),
            [terms, taken, other_kept, other_taken, tokens],
            size=terms.size * 8,
        )
        return (context, mixed_out)

    return local


def solution(mesh):
    placed = (
        P(("groups", "wide"), "narrow"),
        P(("groups", "wide"), "narrow"),
        P(("groups", "wide"), "narrow"),
        P(("groups", "wide"), None, "narrow"),
        P(("groups", "wide"), None, "narrow"),
        P(("groups", "wide")),
        P(("groups", "wide")),
        P(("groups", "wide"), None),
        P(),
        P("groups", None),
        P("groups", None),
        P("narrow", None, "wide"),
        P("narrow", None, "wide"),
        P("narrow", "wide", None),
    )
    return jax.shard_map(
        make_local(mesh.shape["wide"]),
        mesh=mesh,
        in_specs=placed,
        out_specs=(P(("groups", "wide"), "narrow"), P(("groups", "wide"), None)),
        check_vma=False,
    )
```

```python
import functools
import math

import jax
import jax.numpy as jnp
from jax import lax
from jax.experimental import pallas as pl
from jax.experimental.pallas import tpu as pltpu
from jax.sharding import PartitionSpec as P

HQ = 48
KVH = 8
HD = 128
GROUP = HQ // KVH
SCALE = HD ** (-0.5)
TILE = 256
WIDE_TILE = 768
CUTS = 4
MIB = 1024 * 1024


def steps_of(wide):
    return [wide >> (i + 1) for i in range(int(math.log2(wide)))]


def swap(block, axis, count, step):
    return lax.ppermute(block, axis, [(i, i ^ step) for i in range(count)])


def owner_of(place, me, steps):
    found = me
    for bit, step in enumerate(steps):
        found = found ^ (((place >> bit) & 1) * step)
    return found


def place_of(owner, me, steps):
    differ = owner ^ me
    found = 0
    for bit, step in enumerate(steps):
        shift = int(math.log2(step))
        found = found | (((differ >> shift) & 1) << bit)
    return found


def call(kernel, outs, ins, scratch=(), flops=0, size=0, limit=4, smem=(), far=()):
    spaces = [pltpu.SMEM if i in smem else pl.ANY if i in far else pltpu.VMEM for i in range(len(ins))]
    return pl.pallas_call(
        kernel,
        name=getattr(kernel, "func", kernel).__name__,
        out_shape=outs,
        in_specs=[pl.BlockSpec(memory_space=space) for space in spaces],
        out_specs=jax.tree.map(lambda _: pl.BlockSpec(memory_space=pltpu.VMEM), outs),
        scratch_shapes=list(scratch),
        compiler_params=pltpu.CompilerParams(vmem_limit_bytes=limit * MIB),
        cost_estimate=pl.CostEstimate(flops=flops, bytes_accessed=size, transcendentals=0),
    )(*ins)


def column_copies(source, target, sems, first):
    columns = target.shape[1] // CUTS
    return [
        pltpu.make_async_copy(
            source.at[0, :, pl.ds(pl.multiple_of(first + i * columns, columns), columns)],
            target.at[:, pl.ds(i * columns, columns)],
            sems.at[i],
        )
        for i in range(CUTS)
    ]


def shape(dims, dtype):
    return jax.ShapeDtypeStruct(dims, dtype)


def near(array):
    return pltpu.with_memory_space_constraint(array, pltpu.VMEM)


def distant(array):
    return pltpu.with_memory_space_constraint(array, pltpu.HBM)


def prepare(far_tokens, far_gain, far_query, far_key, far_value, out_ref, both_ref, *held):
    *near_refs, packed, sems = held
    far_refs = (far_tokens, far_gain, far_query, far_key, far_value)
    copies = [
        pltpu.make_async_copy(far, ref, sems.at[i])
        for i, (far, ref) in enumerate(zip(far_refs, near_refs))
    ]
    for copy in copies:
        copy.start()
    for copy in copies:
        copy.wait()
    tokens_ref, gain_ref, *head_refs = near_refs
    rows, half = out_ref.shape
    core = lax.axis_index("narrow")
    values = tokens_ref[...].astype(jnp.float32)
    scale = lax.rsqrt(jnp.mean(values * values, axis=-1, keepdims=True) + 1e-05)
    normed = values * scale * gain_ref[...]
    normed = jnp.where(core == 0, normed[:, :half], normed[:, half:])
    out_ref[...] = normed.astype(jnp.bfloat16)
    pieces = half // HD
    for piece in range(pieces):
        packed[pl.ds(piece, rows, stride=pieces), :] = normed[:, piece * HD : (piece + 1) * HD]
    at = rows * pieces
    each = (both_ref.shape[0] - at) // rows
    for ref in head_refs:
        block = ref[...].astype(jnp.float32)
        for head in range(ref.shape[1] // HD):
            packed[pl.ds(at, rows, stride=each), :] = block[:, head * HD : (head + 1) * HD]
            at += 1
    both_ref[...] = packed[...].astype(jnp.bfloat16)


def stacked(refs):
    return jnp.concatenate([ref[...].astype(jnp.float32) for ref in refs], axis=0)


def gather_line(own_ref, far_both, next_ref, last_ref, own_both, *refs):
    *_, out_ref, heads_ref, packed = refs
    rows, half = own_ref.shape
    pieces = half // HD
    tokens = rows * pieces
    packed[...] = far_both[:tokens, :].astype(jnp.float32)
    far = [packed[pl.ds(piece, rows, stride=pieces), :] for piece in range(pieces)]
    far = jnp.concatenate(far, axis=1)
    own, near_rows, last = (r[...].astype(jnp.float32) for r in (own_ref, next_ref, last_ref))
    out_ref[...] = jnp.concatenate([own, far, near_rows, last], axis=0).astype(jnp.bfloat16)
    count = heads_ref.shape[0] // 2
    heads_ref[:count, :] = own_both[tokens:, :]
    heads_ref[count:, :] = far_both[tokens:, :]


def grow_both(own_ref, got_ref, own_heads, got_heads, *refs):
    refs[-2][...] = stacked([own_ref, got_ref]).astype(jnp.bfloat16)
    refs[-1][...] = stacked([own_heads, got_heads]).astype(jnp.bfloat16)


def shares(steps, rows, far_routes, far_logits, *refs):
    *_, out_ref, routes_ref, logits_ref, sems = refs
    copies = [
        pltpu.make_async_copy(far_routes, routes_ref, sems.at[0]),
        pltpu.make_async_copy(far_logits, logits_ref, sems.at[1]),
    ]
    for copy in copies:
        copy.start()
    for copy in copies:
        copy.wait()
    count = out_ref.shape[0]
    core = lax.axis_index("narrow")
    me = lax.axis_index("wide")
    logits = logits_ref[...]
    first = 1.0 / (1.0 + jnp.exp(logits[1:2] - logits[0:1]))
    second = 1.0 - first
    chosen = (routes_ref[...] == core).astype(jnp.float32)
    weight_row = chosen[0:1] * first + chosen[1:2] * second
    row = lax.broadcasted_iota(jnp.int32, (count, count), 0)
    column = lax.broadcasted_iota(jnp.int32, (count, count), 1)
    shift = int(math.log2(rows))
    token = (owner_of(row >> shift, me, steps) << shift) | (row & (rows - 1))
    weight = jnp.sum(jnp.where(token == column, weight_row, 0.0), axis=1, keepdims=True)
    out_ref[...] = jnp.broadcast_to(weight, out_ref.shape)


def gate_all(
    x_ref,
    other_ref,
    gate_ref,
    up_ref,
    share_ref,
    far_down,
    hidden_out,
    down_own,
    down_other,
    sems,
):
    count, depth = x_ref.shape
    core = lax.axis_index("narrow")
    other_copies = column_copies(far_down, down_other, sems.at[0], (1 - core) * depth)
    own_copies = column_copies(far_down, down_own, sems.at[1], core * depth)
    for copy in other_copies + own_copies:
        copy.start()
    tile = min(TILE, gate_ref.shape[2])
    own = pl.ds(pl.multiple_of(core * depth, depth), depth)
    other = pl.ds(pl.multiple_of((1 - core) * depth, depth), depth)

    weight = share_ref[:, 0:1]

    @pl.loop(0, gate_ref.shape[2] // tile)
    def _(i):
        columns = pl.ds(pl.multiple_of(i * tile, tile), tile)
        x, y = x_ref[...], other_ref[...]
        gate = jnp.dot(x, gate_ref[0, own, columns], preferred_element_type=jnp.float32)
        gate += jnp.dot(y, gate_ref[0, other, columns], preferred_element_type=jnp.float32)
        up = jnp.dot(x, up_ref[0, own, columns], preferred_element_type=jnp.float32)
        up += jnp.dot(y, up_ref[0, other, columns], preferred_element_type=jnp.float32)
        hidden_out[:, columns] = (weight * (gate * jax.nn.sigmoid(gate)) * up).astype(jnp.bfloat16)

    for copy in other_copies + own_copies:
        copy.wait()


def down(hidden_ref, down_ref, after, out_ref):
    @pl.loop(0, out_ref.shape[1] // WIDE_TILE)
    def _(i):
        columns = pl.ds(pl.multiple_of(i * WIDE_TILE, WIDE_TILE), WIDE_TILE)
        out_ref[:, columns] = jnp.dot(
            hidden_ref[...], down_ref[:, columns], preferred_element_type=jnp.float32
        ).astype(out_ref.dtype)


def combine(terms_ref, taken_ref, after, kept_ref, sent_ref):
    total = terms_ref[...] + taken_ref[...].astype(jnp.float32)
    kept = kept_ref.shape[0]
    kept_ref[...] = total[:kept]
    sent_ref[...] = total[kept:].astype(jnp.bfloat16)


def part_line(terms_ref, taken_ref, after, kept_ref, far_ref, next_ref, last_ref):
    total = terms_ref[...] + taken_ref[...].astype(jnp.float32)
    rows = kept_ref.shape[0]
    kept_ref[...] = total[:rows]
    for i, ref in enumerate((far_ref, next_ref, last_ref)):
        ref[...] = total[(i + 1) * rows : (i + 2) * rows].astype(jnp.bfloat16)


def finish(kept_ref, far_ref, next_ref, last_ref, tokens_ref, after, out_ref):
    half = kept_ref.shape[1]
    core = lax.axis_index("narrow")
    own = tokens_ref[...].astype(jnp.float32)
    own = jnp.where(core == 0, own[:, :half], own[:, half:])
    total = kept_ref[...]
    for ref in (far_ref, next_ref, last_ref):
        total = total + ref[...].astype(jnp.float32)
    out_ref[...] = (own + total).astype(jnp.bfloat16)


def join(own_ref, other_ref, out_ref):
    half = own_ref.shape[1]
    core = lax.axis_index("narrow")
    own, other = own_ref[...], other_ref[...]
    out_ref[:, :half] = jnp.where(core == 0, own, other)
    out_ref[:, half:] = jnp.where(core == 0, other, own)


def attend(
    steps, taking, near_ref, far_ref, keys_ref, values_ref, lengths_ref, place_ref, after, out_ref
):
    slots, span, width = keys_ref.shape
    rows = slots
    kv_local = width // HD
    heads = kv_local * GROUP
    each = heads + 2 * kv_local
    me = lax.axis_index("wide")
    shift = int(math.log2(rows))
    half = near_ref.shape[0]
    head_of = lax.broadcasted_iota(jnp.int32, (heads, 1), 0)
    positions = lax.broadcasted_iota(jnp.int32, (heads, span), 1)

    def by_group(pieces):
        result = pieces[0]
        for g in range(1, kv_local):
            result = jnp.where(head_of >= g * GROUP, pieces[g], result)
        return result

    for order, slot in enumerate(taking):
        request = place_ref[slot]
        at = (place_of(request >> shift, me, steps) << shift) | (request & (rows - 1))
        at = at * each
        inside = pl.ds(pl.multiple_of(jnp.where(at < half, at, at - half), each), each)
        block = jnp.where(at < half, near_ref[inside, :], far_ref[inside, :])
        query = block[:heads]
        own = block[heads:].astype(jnp.float32)
        own_key = by_group([own[g : g + 1] for g in range(kv_local)])
        own_value = by_group([own[kv_local + g : kv_local + g + 1] for g in range(kv_local)])
        own_score = jnp.sum(query.astype(jnp.float32) * own_key, axis=1, keepdims=True) * SCALE
        scores = by_group(
            [
                lax.dot_general(
                    query,
                    keys_ref[slot, :, g * HD : (g + 1) * HD],
                    (((1,), (1,)), ((), ())),
                    preferred_element_type=jnp.float32,
                )
                for g in range(kv_local)
            ]
        )
        scores = jnp.where(positions < lengths_ref[slot], scores * SCALE, -jnp.inf)
        row_max = jnp.maximum(jnp.max(scores, axis=1, keepdims=True), own_score)
        weights = jnp.exp(scores - row_max)
        own_weight = jnp.exp(own_score - row_max)
        total = jnp.sum(weights, axis=1, keepdims=True) + own_weight
        probs = (weights / total).astype(jnp.bfloat16)
        own_prob = (own_weight / total).astype(jnp.bfloat16).astype(jnp.float32)
        mixed = by_group(
            [
                jnp.dot(
                    probs,
                    values_ref[slot, :, g * HD : (g + 1) * HD],
                    preferred_element_type=jnp.float32,
                )
                for g in range(kv_local)
            ]
        )
        out_ref[order * heads : (order + 1) * heads, :] = mixed + own_prob * own_value


def lay_out(heads, pieces, out_ref, held):
    at = 0
    for piece in pieces:
        held[at : at + piece.shape[0], :] = piece[...]
        at += piece.shape[0]
    for head in range(heads):
        out_ref[:, head * HD : (head + 1) * HD] = held[
            pl.ds(head, out_ref.shape[0], stride=heads), :
        ].astype(jnp.bfloat16)


def attend_last(steps, taking, heads, *refs):
    *ins, early, out_ref, late, held = refs
    attend(steps, taking, *ins, late)
    lay_out(heads, [early, late], out_ref, held)


def make_local(wide):
    steps = steps_of(wide)

    def local(
        queries,
        new_keys,
        new_values,
        key_cache,
        value_cache,
        lengths,
        assignment,
        tokens,
        norm_gain,
        routes,
        route_logits,
        w_gate,
        w_up,
        w_down,
    ):
        rows, width = tokens.shape
        half = width // 2
        units = w_gate.shape[2]
        count = rows * wide
        each = (queries.shape[1] + 2 * new_keys.shape[1]) // HD
        core = lax.axis_index("narrow")
        bf16, f32 = jnp.bfloat16, jnp.float32
        heads_local = queries.shape[1] // HD
        dma = pltpu.SemaphoreType.DMA
        piece_bytes = 2 * half * units

        firsts = [tokens, norm_gain[None], queries, new_keys, new_values]
        both_rows = rows * (half // HD + each)
        weights = [distant(w_gate), distant(w_up)]
        x, both = call(
            prepare,
            [shape((rows, half), bf16), shape((both_rows, HD), bf16)],
            [distant(a) for a in firsts],
            [pltpu.VMEM(a.shape, a.dtype) for a in firsts]
            + [pltpu.VMEM((both_rows, HD), f32), dma((len(firsts),))],
            size=100000,
            far=range(len(firsts)),
        )
        line = [swap(both, "wide", wide, steps[0])]
        line += [swap(x, "wide", wide, step) for step in (steps[1], steps[0] ^ steps[1])]
        share = call(
            functools.partial(shares, steps, rows),
            shape((count, HD), f32),
            [distant(routes.T), distant(route_logits.T), x, *weights],
            [
                pltpu.VMEM(routes.T.shape, jnp.int32),
                pltpu.VMEM(route_logits.T.shape, f32),
                dma((2,)),
            ],
            size=100000,
            far=range(5),
        )
        x, heads = call(
            gather_line,
            [shape((4 * rows, half), bf16), shape((2 * rows * each, HD), bf16)],
            [
                x,
                *line,
                both,
                share,
                *weights,
            ],
            [pltpu.VMEM((rows * half // HD, HD), f32)],
            size=100000,
            far=(5, 6, 7),
        )
        for order, step in enumerate(steps[2:]):
            ins = [x, swap(x, "wide", wide, step)]
            ins += [heads, swap(heads, "wide", wide, steps[order + 1])]
            outs = [shape((2 * x.shape[0], half), bf16), shape((2 * heads.shape[0], HD), bf16)]
            x, heads = call(grow_both, outs, ins, size=8 * (x.size + heads.size))
        far_heads = swap(heads, "wide", wide, steps[-1])

        product = 2 * count * half * units
        other_x = swap(x, "narrow", 2, 1)
        whole = pltpu.VMEM((units, half), bf16)
        hidden, down_own, down_other = call(
            gate_all,
            [shape((count, units), bf16), whole, whole],
            [
                x,
                other_x,
                near(w_gate),
                near(w_up),
                share,
                distant(w_down),
            ],
            [dma((2, CUTS))],
            flops=4 * product,
            size=6 * piece_bytes,
            far=(5,),
        )
        given = call(
            down,
            shape((count, half), bf16),
            [hidden, near(down_other), far_heads],
            flops=product,
            size=piece_bytes,
            far=(2,),
        )
        taken = swap(given, "narrow", 2, 1)
        terms = call(
            down,
            shape((count, half), f32),
            [hidden, near(down_own), given],
            flops=product,
            size=piece_bytes,
            far=(2,),
        )

        caches = [near(key_cache), near(value_cache), lengths, assignment]
        slots = queries.shape[0]
        early_slots = list(range(slots - 1))
        late_slots = list(range(slots - 1, slots))
        early = None
        after = hidden
        for step in reversed(steps[2:]):
            kept = terms.shape[0] // 2
            terms, sent = call(
                combine,
                [shape((kept, half), f32), shape((kept, half), bf16)],
                [terms, taken, after],
                size=terms.size * 8,
                far=(2,),
            )
            taken = swap(sent, "wide", wide, step)
            if early is None:
                early = call(
                    functools.partial(attend, steps, early_slots),
                    shape((len(early_slots) * heads_local, HD), f32),
                    [heads, far_heads, *caches, sent],
                    flops=2 * key_cache.size * GROUP,
                    size=2 * key_cache.size,
                    smem=(4, 5),
                    far=(6,),
                )
                after = early
        block = shape((rows, half), bf16)
        terms, far_sent, next_sent, last_sent = call(
            part_line,
            [shape((rows, half), f32), block, block, block],
            [terms, taken, after],
            size=terms.size * 8,
            far=(2,),
        )
        got = [
            swap(far_sent, "wide", wide, steps[0]),
            swap(next_sent, "wide", wide, steps[1]),
            swap(last_sent, "wide", wide, steps[0] ^ steps[1]),
        ]
        context = call(
            functools.partial(attend_last, steps, late_slots, heads_local),
            shape(queries.shape, bf16),
            [heads, far_heads, *caches, next_sent, early],
            [
                pltpu.VMEM((len(late_slots) * heads_local, HD), f32),
                pltpu.VMEM((slots * heads_local, HD), f32),
            ],
            flops=2 * key_cache.size * GROUP,
            size=2 * key_cache.size,
            smem=(4, 5),
            far=(6,),
        )
        piece = call(
            finish, block, [terms, *got, tokens, distant(context)], size=terms.size * 8, far=(5,)
        )
        other = swap(piece, "narrow", 2, 1)
        mixed_out = call(join, shape((rows, width), bf16), [piece, other], size=terms.size * 4)
        return (context, mixed_out)

    return local


def solution(mesh):
    placed = (
        P(("groups", "wide"), "narrow"),
        P(("groups", "wide"), "narrow"),
        P(("groups", "wide"), "narrow"),
        P(("groups", "wide"), None, "narrow"),
        P(("groups", "wide"), None, "narrow"),
        P(("groups", "wide")),
        P(("groups", "wide")),
        P(("groups", "wide"), None),
        P(),
        P("groups", None),
        P("groups", None),
        P("narrow", None, "wide"),
        P("narrow", None, "wide"),
        P("narrow", "wide", None),
    )
    return jax.shard_map(
        make_local(mesh.shape["wide"]),
        mesh=mesh,
        in_specs=placed,
        out_specs=(P(("groups", "wide"), "narrow"), P(("groups", "wide"), None)),
        check_vma=False,
    )
```

```python
import functools
import math

import jax
import jax.numpy as jnp
from jax import lax
from jax.experimental import pallas as pl
from jax.experimental.pallas import tpu as pltpu
from jax.sharding import PartitionSpec as P

HQ = 48
KVH = 8
HD = 128
GROUP = HQ // KVH
SCALE = HD ** (-0.5)
TILE = 256
WIDE_TILE = 768
CUTS = 4
MIB = 1024 * 1024


def steps_of(wide):
    bits = int(math.log2(wide))
    return [1 << i for i in range(bits - 2)] + [wide >> 1, wide >> 2]


def swap(block, axis, count, step):
    return lax.ppermute(block, axis, [(i, i ^ step) for i in range(count)])


def owner_of(place, me, steps):
    found = me
    for bit, step in enumerate(steps):
        found = found ^ (((place >> bit) & 1) * step)
    return found


def place_of(owner, me, steps):
    differ = owner ^ me
    found = 0
    for bit, step in enumerate(steps):
        shift = int(math.log2(step))
        found = found | (((differ >> shift) & 1) << bit)
    return found


def call(kernel, outs, ins, scratch=(), flops=0, size=0, limit=4, smem=(), far=()):
    spaces = [pltpu.SMEM if i in smem else pl.ANY if i in far else pltpu.VMEM for i in range(len(ins))]
    return pl.pallas_call(
        kernel,
        name=getattr(kernel, "func", kernel).__name__,
        out_shape=outs,
        in_specs=[pl.BlockSpec(memory_space=space) for space in spaces],
        out_specs=jax.tree.map(lambda _: pl.BlockSpec(memory_space=pltpu.VMEM), outs),
        scratch_shapes=list(scratch),
        compiler_params=pltpu.CompilerParams(vmem_limit_bytes=limit * MIB),
        cost_estimate=pl.CostEstimate(flops=flops, bytes_accessed=size, transcendentals=0),
    )(*ins)


def column_copies(source, target, sems, first):
    columns = target.shape[1] // CUTS
    return [
        pltpu.make_async_copy(
            source.at[0, :, pl.ds(pl.multiple_of(first + i * columns, columns), columns)],
            target.at[:, pl.ds(i * columns, columns)],
            sems.at[i],
        )
        for i in range(CUTS)
    ]


def shape(dims, dtype):
    return jax.ShapeDtypeStruct(dims, dtype)


def near(array):
    return pltpu.with_memory_space_constraint(array, pltpu.VMEM)


def distant(array):
    return pltpu.with_memory_space_constraint(array, pltpu.HBM)


def prepare(far_tokens, far_gain, far_query, far_key, far_value, out_ref, both_ref, *held):
    *near_refs, packed, sems = held
    far_refs = (far_tokens, far_gain, far_query, far_key, far_value)
    copies = [
        pltpu.make_async_copy(far, ref, sems.at[i])
        for i, (far, ref) in enumerate(zip(far_refs, near_refs))
    ]
    for copy in copies:
        copy.start()
    for copy in copies:
        copy.wait()
    tokens_ref, gain_ref, *head_refs = near_refs
    rows, half = out_ref.shape
    core = lax.axis_index("narrow")
    values = tokens_ref[...].astype(jnp.float32)
    scale = lax.rsqrt(jnp.mean(values * values, axis=-1, keepdims=True) + 1e-05)
    normed = values * scale * gain_ref[...]
    normed = jnp.where(core == 0, normed[:, :half], normed[:, half:])
    out_ref[...] = normed.astype(jnp.bfloat16)
    pieces = half // HD
    for piece in range(pieces):
        packed[pl.ds(piece, rows, stride=pieces), :] = normed[:, piece * HD : (piece + 1) * HD]
    at = rows * pieces
    each = (both_ref.shape[0] - at) // rows
    for ref in head_refs:
        block = ref[...].astype(jnp.float32)
        for head in range(ref.shape[1] // HD):
            packed[pl.ds(at, rows, stride=each), :] = block[:, head * HD : (head + 1) * HD]
            at += 1
    both_ref[...] = packed[...].astype(jnp.bfloat16)


def stacked(refs):
    return jnp.concatenate([ref[...].astype(jnp.float32) for ref in refs], axis=0)


def grow_first(own_ref, far_both, own_both, after, out_ref, heads_ref, packed):
    rows, half = own_ref.shape
    pieces = half // HD
    tokens = rows * pieces
    packed[...] = far_both[:tokens, :].astype(jnp.float32)
    far = [packed[pl.ds(piece, rows, stride=pieces), :] for piece in range(pieces)]
    far = jnp.concatenate(far, axis=1)
    own = own_ref[...].astype(jnp.float32)
    out_ref[...] = jnp.concatenate([own, far], axis=0).astype(jnp.bfloat16)
    count = heads_ref.shape[0] // 2
    heads_ref[:count, :] = own_both[tokens:, :]
    heads_ref[count:, :] = far_both[tokens:, :]


def stack(*refs):
    refs[-1][...] = stacked(refs[:-1]).astype(refs[-1].dtype)


def stack_line(own_ref, last_ref, far_ref, next_ref, out_ref):
    stack(own_ref, far_ref, next_ref, last_ref, out_ref)


def stack_after(own_ref, got_ref, after, out_ref):
    stack(own_ref, got_ref, out_ref)


def grow_both(own_ref, got_ref, own_heads, got_heads, *refs):
    refs[-2][...] = stacked([own_ref, got_ref]).astype(jnp.bfloat16)
    refs[-1][...] = stacked([own_heads, got_heads]).astype(jnp.bfloat16)


def shares(steps, rows, far_routes, far_logits, *refs):
    *_, out_ref, routes_ref, logits_ref, sems = refs
    copies = [
        pltpu.make_async_copy(far_routes, routes_ref, sems.at[0]),
        pltpu.make_async_copy(far_logits, logits_ref, sems.at[1]),
    ]
    for copy in copies:
        copy.start()
    for copy in copies:
        copy.wait()
    count = out_ref.shape[0]
    core = lax.axis_index("narrow")
    me = lax.axis_index("wide")
    logits = logits_ref[...]
    first = 1.0 / (1.0 + jnp.exp(logits[1:2] - logits[0:1]))
    second = 1.0 - first
    chosen = (routes_ref[...] == core).astype(jnp.float32)
    weight_row = chosen[0:1] * first + chosen[1:2] * second
    row = lax.broadcasted_iota(jnp.int32, (count, count), 0)
    column = lax.broadcasted_iota(jnp.int32, (count, count), 1)
    shift = int(math.log2(rows))
    token = (owner_of(row >> shift, me, steps) << shift) | (row & (rows - 1))
    weight = jnp.sum(jnp.where(token == column, weight_row, 0.0), axis=1, keepdims=True)
    out_ref[...] = jnp.broadcast_to(weight, out_ref.shape)


def gate_all(
    x_ref,
    other_ref,
    gate_ref,
    up_ref,
    share_ref,
    far_down,
    hidden_out,
    down_own,
    down_other,
    sems,
):
    count, depth = x_ref.shape
    core = lax.axis_index("narrow")
    other_copies = column_copies(far_down, down_other, sems.at[0], (1 - core) * depth)
    own_copies = column_copies(far_down, down_own, sems.at[1], core * depth)
    for copy in other_copies + own_copies:
        copy.start()
    tile = min(TILE, gate_ref.shape[2])
    own = pl.ds(pl.multiple_of(core * depth, depth), depth)
    other = pl.ds(pl.multiple_of((1 - core) * depth, depth), depth)

    weight = share_ref[:, 0:1]

    @pl.loop(0, gate_ref.shape[2] // tile)
    def _(i):
        columns = pl.ds(pl.multiple_of(i * tile, tile), tile)
        x, y = x_ref[...], other_ref[...]
        gate = jnp.dot(x, gate_ref[0, own, columns], preferred_element_type=jnp.float32)
        gate += jnp.dot(y, gate_ref[0, other, columns], preferred_element_type=jnp.float32)
        up = jnp.dot(x, up_ref[0, own, columns], preferred_element_type=jnp.float32)
        up += jnp.dot(y, up_ref[0, other, columns], preferred_element_type=jnp.float32)
        hidden_out[:, columns] = (weight * (gate * jax.nn.sigmoid(gate)) * up).astype(jnp.bfloat16)

    for copy in other_copies + own_copies:
        copy.wait()


def down(hidden_ref, down_ref, after, out_ref):
    @pl.loop(0, out_ref.shape[1] // WIDE_TILE)
    def _(i):
        columns = pl.ds(pl.multiple_of(i * WIDE_TILE, WIDE_TILE), WIDE_TILE)
        out_ref[:, columns] = jnp.dot(
            hidden_ref[...], down_ref[:, columns], preferred_element_type=jnp.float32
        ).astype(out_ref.dtype)


def part_line(terms_ref, taken_ref, kept_ref, far_ref, next_ref, last_ref):
    total = terms_ref[...] + taken_ref[...].astype(jnp.float32)
    rows = kept_ref.shape[0]
    kept_ref[...] = total[:rows]
    for i, ref in enumerate((far_ref, next_ref, last_ref)):
        ref[...] = total[(i + 1) * rows : (i + 2) * rows].astype(jnp.bfloat16)


def combine(*refs):
    terms_ref, *taken, after, kept_ref, sent_ref = refs
    total = terms_ref[...]
    for ref in taken:
        total = total + ref[...].astype(jnp.float32)
    kept = kept_ref.shape[0]
    kept_ref[...] = total[:kept]
    sent_ref[...] = total[kept:].astype(jnp.bfloat16)


def finish(kept_ref, taken_ref, tokens_ref, after, out_ref):
    half = kept_ref.shape[1]
    core = lax.axis_index("narrow")
    own = tokens_ref[...].astype(jnp.float32)
    own = jnp.where(core == 0, own[:, :half], own[:, half:])
    total = kept_ref[...] + taken_ref[...].astype(jnp.float32)
    out_ref[...] = (own + total).astype(jnp.bfloat16)


def join(own_ref, other_ref, out_ref):
    half = own_ref.shape[1]
    core = lax.axis_index("narrow")
    own, other = own_ref[...], other_ref[...]
    out_ref[:, :half] = jnp.where(core == 0, own, other)
    out_ref[:, half:] = jnp.where(core == 0, other, own)


def attend(
    steps, taking, near_ref, far_ref, keys_ref, values_ref, lengths_ref, place_ref, after, out_ref
):
    slots, span, width = keys_ref.shape
    rows = slots
    kv_local = width // HD
    heads = kv_local * GROUP
    each = heads + 2 * kv_local
    me = lax.axis_index("wide")
    shift = int(math.log2(rows))
    half = near_ref.shape[0]
    head_of = lax.broadcasted_iota(jnp.int32, (heads, 1), 0)
    positions = lax.broadcasted_iota(jnp.int32, (heads, span), 1)

    def by_group(pieces):
        result = pieces[0]
        for g in range(1, kv_local):
            result = jnp.where(head_of >= g * GROUP, pieces[g], result)
        return result

    for order, slot in enumerate(taking):
        request = place_ref[slot]
        at = (place_of(request >> shift, me, steps) << shift) | (request & (rows - 1))
        at = at * each
        inside = pl.ds(pl.multiple_of(jnp.where(at < half, at, at - half), each), each)
        block = jnp.where(at < half, near_ref[inside, :], far_ref[inside, :])
        query = block[:heads]
        own = block[heads:].astype(jnp.float32)
        own_key = by_group([own[g : g + 1] for g in range(kv_local)])
        own_value = by_group([own[kv_local + g : kv_local + g + 1] for g in range(kv_local)])
        own_score = jnp.sum(query.astype(jnp.float32) * own_key, axis=1, keepdims=True) * SCALE
        scores = by_group(
            [
                lax.dot_general(
                    query,
                    keys_ref[slot, :, g * HD : (g + 1) * HD],
                    (((1,), (1,)), ((), ())),
                    preferred_element_type=jnp.float32,
                )
                for g in range(kv_local)
            ]
        )
        scores = jnp.where(positions < lengths_ref[slot], scores * SCALE, -jnp.inf)
        row_max = jnp.maximum(jnp.max(scores, axis=1, keepdims=True), own_score)
        weights = jnp.exp(scores - row_max)
        own_weight = jnp.exp(own_score - row_max)
        total = jnp.sum(weights, axis=1, keepdims=True) + own_weight
        probs = (weights / total).astype(jnp.bfloat16)
        own_prob = (own_weight / total).astype(jnp.bfloat16).astype(jnp.float32)
        mixed = by_group(
            [
                jnp.dot(
                    probs,
                    values_ref[slot, :, g * HD : (g + 1) * HD],
                    preferred_element_type=jnp.float32,
                )
                for g in range(kv_local)
            ]
        )
        out_ref[order * heads : (order + 1) * heads, :] = mixed + own_prob * own_value


def lay_out(heads, pieces, out_ref, held):
    at = 0
    for piece in pieces:
        held[at : at + piece.shape[0], :] = piece[...]
        at += piece.shape[0]
    for head in range(heads):
        out_ref[:, head * HD : (head + 1) * HD] = held[
            pl.ds(head, out_ref.shape[0], stride=heads), :
        ].astype(jnp.bfloat16)


def attend_last(steps, taking, heads, *refs):
    *ins, early, out_ref, late, held = refs
    attend(steps, taking, *ins, late)
    lay_out(heads, [early, late], out_ref, held)


def make_local(wide):
    steps = steps_of(wide)

    def local(
        queries,
        new_keys,
        new_values,
        key_cache,
        value_cache,
        lengths,
        assignment,
        tokens,
        norm_gain,
        routes,
        route_logits,
        w_gate,
        w_up,
        w_down,
    ):
        rows, width = tokens.shape
        half = width // 2
        units = w_gate.shape[2]
        count = rows * wide
        each = (queries.shape[1] + 2 * new_keys.shape[1]) // HD
        core = lax.axis_index("narrow")
        bf16, f32 = jnp.bfloat16, jnp.float32
        heads_local = queries.shape[1] // HD
        dma = pltpu.SemaphoreType.DMA
        piece_bytes = 2 * half * units

        firsts = [tokens, norm_gain[None], queries, new_keys, new_values]
        both_rows = rows * (half // HD + each)
        weights = [distant(w_gate), distant(w_up)]
        x, both = call(
            prepare,
            [shape((rows, half), bf16), shape((both_rows, HD), bf16)],
            [distant(a) for a in firsts],
            [pltpu.VMEM(a.shape, a.dtype) for a in firsts]
            + [pltpu.VMEM((both_rows, HD), f32), dma((len(firsts),))],
            size=100000,
            far=range(len(firsts)),
        )
        far_both = swap(both, "wide", wide, steps[0])
        share = call(
            functools.partial(shares, steps, rows),
            shape((count, HD), f32),
            [distant(routes.T), distant(route_logits.T), x, *weights],
            [
                pltpu.VMEM(routes.T.shape, jnp.int32),
                pltpu.VMEM(route_logits.T.shape, f32),
                dma((2,)),
            ],
            size=100000,
            far=range(5),
        )
        x, heads = call(
            grow_first,
            [shape((2 * rows, half), bf16), shape((2 * rows * each, HD), bf16)],
            [x, far_both, both, share],
            [pltpu.VMEM((rows * half // HD, HD), f32)],
            size=100000,
            far=(3,),
        )
        for step in steps[1:-2]:
            ins = [x, swap(x, "wide", wide, step), heads, swap(heads, "wide", wide, step)]
            outs = [shape((2 * x.shape[0], half), bf16), shape((2 * heads.shape[0], HD), bf16)]
            x, heads = call(grow_both, outs, ins, size=8 * (x.size + heads.size))
        line_steps = [steps[-2], steps[-1], steps[-2] ^ steps[-1]]
        last = swap(x, "wide", wide, line_steps[2])
        line = [swap(x, "wide", wide, step) for step in line_steps[:2]]
        got_heads = swap(heads, "wide", wide, steps[-2])
        x = call(
            stack_line, shape((count, half), bf16), [x, last, *line], size=8 * count * half
        )

        product = 2 * count * half * units
        other_x = swap(x, "narrow", 2, 1)
        whole = pltpu.VMEM((units, half), bf16)
        hidden, down_own, down_other = call(
            gate_all,
            [shape((count, units), bf16), whole, whole],
            [
                x,
                other_x,
                near(w_gate),
                near(w_up),
                share,
                distant(w_down),
            ],
            [dma((2, CUTS))],
            flops=4 * product,
            size=6 * piece_bytes,
            far=(5,),
        )
        heads = call(
            stack_after,
            shape((2 * heads.shape[0], HD), bf16),
            [heads, got_heads, hidden],
            size=8 * heads.size,
            far=(2,),
        )
        given = call(
            down,
            shape((count, half), bf16),
            [hidden, near(down_other), heads],
            flops=product,
            size=piece_bytes,
            far=(2,),
        )
        taken = swap(given, "narrow", 2, 1)
        far_heads = swap(heads, "wide", wide, steps[-1])
        terms = call(
            down,
            shape((count, half), f32),
            [hidden, near(down_own), given],
            flops=product,
            size=piece_bytes,
            far=(2,),
        )

        caches = [near(key_cache), near(value_cache), lengths, assignment]
        slots = queries.shape[0]
        early_slots = list(range(slots - 1))
        late_slots = list(range(slots - 1, slots))
        quarter = count // 4
        block = shape((quarter, half), bf16)
        terms, *sent = call(
            part_line,
            [shape((quarter, half), f32), block, block, block],
            [terms, taken],
            size=terms.size * 8,
        )
        taken = [swap(part, "wide", wide, step) for part, step in zip(sent, line_steps)]
        early = call(
            functools.partial(attend, steps, early_slots),
            shape((len(early_slots) * heads_local, HD), f32),
            [heads, far_heads, *caches, sent[0]],
            flops=2 * key_cache.size * GROUP,
            size=2 * key_cache.size,
            smem=(4, 5),
            far=(6,),
        )
        for step in reversed(steps[:-2]):
            kept = terms.shape[0] // 2
            terms, sent = call(
                combine,
                [shape((kept, half), f32), shape((kept, half), bf16)],
                [terms, *taken, early],
                size=terms.size * 8,
                far=(1 + len(taken),),
            )
            taken = [swap(sent, "wide", wide, step)]
        context = call(
            functools.partial(attend_last, steps, late_slots, heads_local),
            shape(queries.shape, bf16),
            [heads, far_heads, *caches, sent, early],
            [
                pltpu.VMEM((len(late_slots) * heads_local, HD), f32),
                pltpu.VMEM((slots * heads_local, HD), f32),
            ],
            flops=2 * key_cache.size * GROUP,
            size=2 * key_cache.size,
            smem=(4, 5),
            far=(6,),
        )
        piece = call(
            finish,
            shape((rows, half), bf16),
            [terms, *taken, tokens, distant(context)],
            size=terms.size * 8,
            far=(3,),
        )
        other = swap(piece, "narrow", 2, 1)
        mixed_out = call(join, shape((rows, width), bf16), [piece, other], size=terms.size * 4)
        return (context, mixed_out)

    return local


def solution(mesh):
    placed = (
        P(("groups", "wide"), "narrow"),
        P(("groups", "wide"), "narrow"),
        P(("groups", "wide"), "narrow"),
        P(("groups", "wide"), None, "narrow"),
        P(("groups", "wide"), None, "narrow"),
        P(("groups", "wide")),
        P(("groups", "wide")),
        P(("groups", "wide"), None),
        P(),
        P("groups", None),
        P("groups", None),
        P("narrow", None, "wide"),
        P("narrow", None, "wide"),
        P("narrow", "wide", None),
    )
    return jax.shard_map(
        make_local(mesh.shape["wide"]),
        mesh=mesh,
        in_specs=placed,
        out_specs=(P(("groups", "wide"), "narrow"), P(("groups", "wide"), None)),
        check_vma=False,
    )
```

```python
import functools
import math

import jax
import jax.numpy as jnp
from jax import lax
from jax.experimental import pallas as pl
from jax.experimental.pallas import tpu as pltpu
from jax.sharding import PartitionSpec as P

HQ = 48
KVH = 8
HD = 128
GROUP = HQ // KVH
SCALE = HD ** (-0.5)
TILE = 256
WIDE_TILE = 768
CUTS = 4
MIB = 1024 * 1024


def steps_of(wide):
    bits = int(math.log2(wide))
    return [1 << i for i in range(bits - 2)], wide >> 1, wide >> 2


def swap(block, axis, count, step):
    return lax.ppermute(block, axis, [(i, i ^ step) for i in range(count)])


def swap_by_core(block, wide, steps):
    pairs = [(2 * i + c, 2 * (i ^ step) + c) for c, step in enumerate(steps) if step for i in range(wide)]
    return lax.ppermute(block, ("wide", "narrow"), pairs)


def owner_of(place, me, steps):
    found = me
    for bit, step in enumerate(steps):
        found = found ^ (((place >> bit) & 1) * step)
    return found


def place_of(owner, me, steps):
    differ = owner ^ me
    found = 0
    for bit, step in enumerate(steps):
        shift = int(math.log2(step))
        found = found | (((differ >> shift) & 1) << bit)
    return found


def call(kernel, outs, ins, scratch=(), flops=0, size=0, limit=4, smem=(), far=()):
    spaces = [pltpu.SMEM if i in smem else pl.ANY if i in far else pltpu.VMEM for i in range(len(ins))]
    return pl.pallas_call(
        kernel,
        name=getattr(kernel, "func", kernel).__name__,
        out_shape=outs,
        in_specs=[pl.BlockSpec(memory_space=space) for space in spaces],
        out_specs=jax.tree.map(lambda _: pl.BlockSpec(memory_space=pltpu.VMEM), outs),
        scratch_shapes=list(scratch),
        compiler_params=pltpu.CompilerParams(vmem_limit_bytes=limit * MIB),
        cost_estimate=pl.CostEstimate(flops=flops, bytes_accessed=size, transcendentals=0),
    )(*ins)


def shape(dims, dtype):
    return jax.ShapeDtypeStruct(dims, dtype)


def near(array):
    return pltpu.with_memory_space_constraint(array, pltpu.VMEM)


def distant(array):
    return pltpu.with_memory_space_constraint(array, pltpu.HBM)


def prepare(far_tokens, far_gain, far_query, far_key, far_value, out_ref, heads_ref, *held):
    *near_refs, packed, sems = held
    far_refs = (far_tokens, far_gain, far_query, far_key, far_value)
    copies = [
        pltpu.make_async_copy(far, ref, sems.at[i])
        for i, (far, ref) in enumerate(zip(far_refs, near_refs))
    ]
    for copy in copies:
        copy.start()
    for copy in copies:
        copy.wait()
    tokens_ref, gain_ref, *head_refs = near_refs
    rows = out_ref.shape[0]
    values = tokens_ref[...].astype(jnp.float32)
    scale = lax.rsqrt(jnp.mean(values * values, axis=-1, keepdims=True) + 1e-05)
    out_ref[...] = (values * scale * gain_ref[...]).astype(jnp.bfloat16)
    at = 0
    each = heads_ref.shape[0] // rows
    for ref in head_refs:
        block = ref[...].astype(jnp.float32)
        for head in range(ref.shape[1] // HD):
            packed[pl.ds(at, rows, stride=each), :] = block[:, head * HD : (head + 1) * HD]
            at += 1
    heads_ref[...] = packed[...].astype(jnp.bfloat16)


def stacked(refs):
    return jnp.concatenate([ref[...].astype(jnp.float32) for ref in refs], axis=0)


def stack(own_ref, got_ref, out_ref):
    out_ref[...] = stacked([own_ref, got_ref]).astype(out_ref.dtype)


def stack_after(own_ref, got_ref, after, out_ref):
    stack(own_ref, got_ref, out_ref)


def stack_line(own_ref, second_ref, first_ref, after, out_ref):
    first = lax.axis_index("narrow") == 0
    own, one, two = (r[...].astype(jnp.float32) for r in (own_ref, first_ref, second_ref))
    both = [jnp.where(first, own, one), jnp.where(first, one, two)]
    out_ref[...] = jnp.concatenate(both, axis=0).astype(jnp.bfloat16)


def shares(steps, rows, far_routes, far_logits, *refs):
    *_, out_ref, routes_ref, logits_ref, sems = refs
    copies = [
        pltpu.make_async_copy(far_routes, routes_ref, sems.at[0]),
        pltpu.make_async_copy(far_logits, logits_ref, sems.at[1]),
    ]
    for copy in copies:
        copy.start()
    for copy in copies:
        copy.wait()
    count = out_ref.shape[0]
    core = lax.axis_index("narrow")
    me = lax.axis_index("wide") ^ (core * steps[-1])
    logits = logits_ref[...]
    first = 1.0 / (1.0 + jnp.exp(logits[1:2] - logits[0:1]))
    second = 1.0 - first
    chosen = (routes_ref[...] == core).astype(jnp.float32)
    weight_row = chosen[0:1] * first + chosen[1:2] * second
    row = lax.broadcasted_iota(jnp.int32, (count, count), 0)
    column = lax.broadcasted_iota(jnp.int32, (count, count), 1)
    shift = int(math.log2(rows))
    token = (owner_of(row >> shift, me, steps) << shift) | (row & (rows - 1))
    weight = jnp.sum(jnp.where(token == column, weight_row, 0.0), axis=1, keepdims=True)
    out_ref[...] = jnp.broadcast_to(weight, out_ref.shape)


def gate_all(
    own_ref,
    other_ref,
    gate_ref,
    up_ref,
    share_ref,
    far_down,
    hidden_out,
    near_down,
    x_ref,
    sems,
):
    span = near_down.shape[0] // CUTS
    copies = [
        pltpu.make_async_copy(
            far_down.at[0, pl.ds(i * span, span), :],
            near_down.at[pl.ds(i * span, span), :],
            sems.at[i],
        )
        for i in range(CUTS)
    ]
    for copy in copies:
        copy.start()
    tile = min(TILE, gate_ref.shape[2])
    held = own_ref.shape[0]
    x_ref[:held, :] = own_ref[...]
    x_ref[held:, :] = other_ref[...]
    weight = share_ref[:, 0:1]

    @pl.loop(0, gate_ref.shape[2] // tile)
    def _(i):
        columns = pl.ds(pl.multiple_of(i * tile, tile), tile)
        x = x_ref[...]
        gate = jnp.dot(x, gate_ref[0, :, columns], preferred_element_type=jnp.float32)
        up = jnp.dot(x, up_ref[0, :, columns], preferred_element_type=jnp.float32)
        hidden_out[:, columns] = (weight * (gate * jax.nn.sigmoid(gate)) * up).astype(jnp.bfloat16)

    for copy in copies:
        copy.wait()


def down(hidden_ref, down_ref, after, kept_ref, given_ref):
    kept = kept_ref.shape[0]

    @pl.loop(0, kept_ref.shape[1] // WIDE_TILE)
    def _(i):
        columns = pl.ds(pl.multiple_of(i * WIDE_TILE, WIDE_TILE), WIDE_TILE)
        terms = jnp.dot(
            hidden_ref[...], down_ref[:, columns], preferred_element_type=jnp.float32
        )
        kept_ref[:, columns] = terms[:kept]
        given_ref[:, columns] = terms[kept:].astype(jnp.bfloat16)


def combine(terms_ref, taken_ref, after, kept_ref, sent_ref):
    total = terms_ref[...] + taken_ref[...].astype(jnp.float32)
    kept = kept_ref.shape[0]
    kept_ref[...] = total[:kept]
    sent_ref[...] = total[kept:].astype(jnp.bfloat16)


def part_line(terms_ref, taken_ref, after, kept_ref, first_ref, second_ref):
    first = lax.axis_index("narrow") == 0
    total = terms_ref[...] + taken_ref[...].astype(jnp.float32)
    rows = kept_ref.shape[0]
    one, two = total[:rows], total[rows:]
    kept_ref[...] = jnp.where(first, one, 0.0)
    first_ref[...] = jnp.where(first, two, one).astype(jnp.bfloat16)
    second_ref[...] = two.astype(jnp.bfloat16)


def merge(kept_ref, second_ref, first_ref, after, out_ref):
    second = second_ref[...].astype(jnp.float32)
    second = jnp.where(lax.axis_index("narrow") == 0, 0.0, second)
    total = kept_ref[...] + first_ref[...].astype(jnp.float32) + second
    out_ref[...] = total.astype(jnp.bfloat16)


def finish(own_ref, other_ref, tokens_ref, out_ref):
    total = own_ref[...].astype(jnp.float32) + other_ref[...].astype(jnp.float32)
    out_ref[...] = (tokens_ref[...].astype(jnp.float32) + total).astype(jnp.bfloat16)


def attend(
    steps, taking, near_ref, far_ref, keys_ref, values_ref, lengths_ref, place_ref, after, out_ref
):
    slots, span, width = keys_ref.shape
    rows = slots
    kv_local = width // HD
    heads = kv_local * GROUP
    each = heads + 2 * kv_local
    me = lax.axis_index("wide")
    shift = int(math.log2(rows))
    half = near_ref.shape[0]
    head_of = lax.broadcasted_iota(jnp.int32, (heads, 1), 0)
    positions = lax.broadcasted_iota(jnp.int32, (heads, span), 1)

    def by_group(pieces):
        result = pieces[0]
        for g in range(1, kv_local):
            result = jnp.where(head_of >= g * GROUP, pieces[g], result)
        return result

    for order, slot in enumerate(taking):
        request = place_ref[slot]
        at = (place_of(request >> shift, me, steps) << shift) | (request & (rows - 1))
        at = at * each
        inside = pl.ds(pl.multiple_of(jnp.where(at < half, at, at - half), each), each)
        block = jnp.where(at < half, near_ref[inside, :], far_ref[inside, :])
        query = block[:heads]
        own = block[heads:].astype(jnp.float32)
        own_key = by_group([own[g : g + 1] for g in range(kv_local)])
        own_value = by_group([own[kv_local + g : kv_local + g + 1] for g in range(kv_local)])
        own_score = jnp.sum(query.astype(jnp.float32) * own_key, axis=1, keepdims=True) * SCALE
        scores = by_group(
            [
                lax.dot_general(
                    query,
                    keys_ref[slot, :, g * HD : (g + 1) * HD],
                    (((1,), (1,)), ((), ())),
                    preferred_element_type=jnp.float32,
                )
                for g in range(kv_local)
            ]
        )
        scores = jnp.where(positions < lengths_ref[slot], scores * SCALE, -jnp.inf)
        row_max = jnp.maximum(jnp.max(scores, axis=1, keepdims=True), own_score)
        weights = jnp.exp(scores - row_max)
        own_weight = jnp.exp(own_score - row_max)
        total = jnp.sum(weights, axis=1, keepdims=True) + own_weight
        probs = (weights / total).astype(jnp.bfloat16)
        own_prob = (own_weight / total).astype(jnp.bfloat16).astype(jnp.float32)
        mixed = by_group(
            [
                jnp.dot(
                    probs,
                    values_ref[slot, :, g * HD : (g + 1) * HD],
                    preferred_element_type=jnp.float32,
                )
                for g in range(kv_local)
            ]
        )
        out_ref[order * heads : (order + 1) * heads, :] = mixed + own_prob * own_value


def lay_out(heads, pieces, out_ref, held):
    at = 0
    for piece in pieces:
        held[at : at + piece.shape[0], :] = piece[...]
        at += piece.shape[0]
    for head in range(heads):
        out_ref[:, head * HD : (head + 1) * HD] = held[
            pl.ds(head, out_ref.shape[0], stride=heads), :
        ].astype(jnp.bfloat16)


def attend_last(steps, taking, heads, *refs):
    *ins, early, out_ref, late, held = refs
    attend(steps, taking, *ins, late)
    lay_out(heads, [early, late], out_ref, held)


def make_local(wide):
    short, far_step, near_step = steps_of(wide)
    steps = [far_step, *short, near_step]
    head_steps = [*short, far_step, near_step]

    def local(
        queries,
        new_keys,
        new_values,
        key_cache,
        value_cache,
        lengths,
        assignment,
        tokens,
        norm_gain,
        routes,
        route_logits,
        w_gate,
        w_up,
        w_down,
    ):
        rows, width = tokens.shape
        half = width // 2
        units = w_gate.shape[2]
        count = rows * wide
        each = (queries.shape[1] + 2 * new_keys.shape[1]) // HD
        bf16, f32 = jnp.bfloat16, jnp.float32
        heads_local = queries.shape[1] // HD
        slots = queries.shape[0]
        dma = pltpu.SemaphoreType.DMA
        piece_bytes = 2 * half * units
        product = 2 * count * half * units

        firsts = [tokens, norm_gain[None], queries, new_keys, new_values]
        x, heads = call(
            prepare,
            [shape((rows, width), bf16), shape((rows * each, HD), bf16)],
            [distant(a) for a in firsts],
            [pltpu.VMEM(a.shape, a.dtype) for a in firsts]
            + [pltpu.VMEM((rows * each, HD), f32), dma((len(firsts),))],
            size=100000,
            far=range(len(firsts)),
        )
        share = call(
            functools.partial(shares, steps, rows),
            shape((count, HD), f32),
            [distant(routes.T), distant(route_logits.T), x, distant(w_gate), distant(w_up)],
            [
                pltpu.VMEM(routes.T.shape, jnp.int32),
                pltpu.VMEM(route_logits.T.shape, f32),
                dma((2,)),
            ],
            size=100000,
            far=range(5),
        )
        second = swap_by_core(x, wide, [0, far_step ^ near_step])
        first = swap_by_core(x, wide, [far_step, near_step])
        x = call(
            stack_line,
            shape((2 * rows, width), bf16),
            [x, second, first, share],
            size=8 * rows * width,
            far=(3,),
        )
        for step in short:
            got_heads = swap(heads, "wide", wide, step)
            heads = call(
                stack, shape((2 * heads.shape[0], HD), bf16), [heads, got_heads], size=4 * heads.size
            )
            x = call(
                stack_after,
                shape((2 * x.shape[0], width), bf16),
                [x, swap(x, "wide", wide, step), heads],
                size=8 * x.size,
                far=(2,),
            )
        got_heads = swap(heads, "wide", wide, far_step)
        other_x = swap(x, "narrow", 2, 1)
        hidden, near_down = call(
            gate_all,
            [shape((count, units), bf16), pltpu.VMEM((units, width), bf16)],
            [x, other_x, near(w_gate), near(w_up), share, distant(w_down)],
            [pltpu.VMEM((count, width), bf16), dma((CUTS,))],
            flops=4 * product,
            size=6 * piece_bytes,
            far=(5,),
        )
        heads = call(
            stack_after,
            shape((2 * heads.shape[0], HD), bf16),
            [heads, got_heads, hidden],
            size=8 * heads.size,
            far=(2,),
        )
        terms, given = call(
            down,
            [shape((count // 2, width), f32), shape((count // 2, width), bf16)],
            [hidden, near(near_down), heads],
            flops=2 * product,
            size=2 * piece_bytes,
            far=(2,),
        )
        taken = swap(given, "narrow", 2, 1)
        far_heads = swap(heads, "wide", wide, near_step)

        caches = [near(key_cache), near(value_cache), lengths, assignment]
        early_slots = list(range(slots - 1))
        late_slots = list(range(slots - 1, slots))
        early = hidden
        for step in reversed(short):
            kept = terms.shape[0] // 2
            terms, sent = call(
                combine,
                [shape((kept, width), f32), shape((kept, width), bf16)],
                [terms, taken, early],
                size=12 * kept * width,
                far=(2,),
            )
            taken = swap(sent, "wide", wide, step)
            if early is hidden:
                early = call(
                    functools.partial(attend, head_steps, early_slots),
                    shape((len(early_slots) * heads_local, HD), f32),
                    [heads, far_heads, *caches, sent],
                    flops=2 * key_cache.size * GROUP,
                    size=2 * key_cache.size,
                    smem=(4, 5),
                    far=(6,),
                )
        block = shape((rows, width), bf16)
        terms, first, second = call(
            part_line,
            [shape((rows, width), f32), block, block],
            [terms, taken, early],
            size=12 * rows * width,
            far=(2,),
        )
        second_taken = swap_by_core(second, wide, [0, far_step ^ near_step])
        first_taken = swap_by_core(first, wide, [far_step, near_step])
        context = call(
            functools.partial(attend_last, head_steps, late_slots, heads_local),
            shape(queries.shape, bf16),
            [heads, far_heads, *caches, first, early],
            [
                pltpu.VMEM((len(late_slots) * heads_local, HD), f32),
                pltpu.VMEM((slots * heads_local, HD), f32),
            ],
            flops=2 * key_cache.size * GROUP,
            size=2 * key_cache.size,
            smem=(4, 5),
            far=(6,),
        )
        part = call(
            merge,
            block,
            [terms, second_taken, first_taken, distant(context)],
            size=12 * rows * width,
            far=(3,),
        )
        other = swap(part, "narrow", 2, 1)
        mixed_out = call(finish, block, [part, other, tokens], size=8 * rows * width)
        return (context, mixed_out)

    return local


def solution(mesh):
    placed = (
        P(("groups", "wide"), "narrow"),
        P(("groups", "wide"), "narrow"),
        P(("groups", "wide"), "narrow"),
        P(("groups", "wide"), None, "narrow"),
        P(("groups", "wide"), None, "narrow"),
        P(("groups", "wide")),
        P(("groups", "wide")),
        P(("groups", "wide"), None),
        P(),
        P("groups", None),
        P("groups", None),
        P("narrow", None, "wide"),
        P("narrow", None, "wide"),
        P("narrow", "wide", None),
    )
    return jax.shard_map(
        make_local(mesh.shape["wide"]),
        mesh=mesh,
        in_specs=placed,
        out_specs=(P(("groups", "wide"), "narrow"), P(("groups", "wide"), None)),
        check_vma=False,
    )
```

```python
import functools
import math

import jax
import jax.numpy as jnp
from jax import lax
from jax.experimental import pallas as pl
from jax.experimental.pallas import tpu as pltpu
from jax.sharding import PartitionSpec as P

HQ = 48
KVH = 8
HD = 128
GROUP = HQ // KVH
SCALE = HD ** (-0.5)
TILE = 256
WIDE_TILE = 768
CUTS = 4
MIB = 1024 * 1024


def steps_of(wide):
    bits = int(math.log2(wide))
    return [1 << i for i in range(bits - 2)], wide >> 1, wide >> 2


def swap(block, axis, count, step):
    return lax.ppermute(block, axis, [(i, i ^ step) for i in range(count)])


def swap_by_core(block, wide, steps):
    pairs = [(2 * i + c, 2 * (i ^ step) + c) for c, step in enumerate(steps) if step for i in range(wide)]
    return lax.ppermute(block, ("wide", "narrow"), pairs)


def owner_of(place, me, steps):
    found = me
    for bit, step in enumerate(steps):
        found = found ^ (((place >> bit) & 1) * step)
    return found


def place_of(owner, me, steps):
    differ = owner ^ me
    found = 0
    for bit, step in enumerate(steps):
        shift = int(math.log2(step))
        found = found | (((differ >> shift) & 1) << bit)
    return found


def call(kernel, outs, ins, scratch=(), flops=0, size=0, limit=4, smem=(), far=()):
    spaces = [pltpu.SMEM if i in smem else pl.ANY if i in far else pltpu.VMEM for i in range(len(ins))]
    return pl.pallas_call(
        kernel,
        name=getattr(kernel, "func", kernel).__name__,
        out_shape=outs,
        in_specs=[pl.BlockSpec(memory_space=space) for space in spaces],
        out_specs=jax.tree.map(lambda _: pl.BlockSpec(memory_space=pltpu.VMEM), outs),
        scratch_shapes=list(scratch),
        compiler_params=pltpu.CompilerParams(vmem_limit_bytes=limit * MIB),
        cost_estimate=pl.CostEstimate(flops=flops, bytes_accessed=size, transcendentals=0),
    )(*ins)


def shape(dims, dtype):
    return jax.ShapeDtypeStruct(dims, dtype)


def near(array):
    return pltpu.with_memory_space_constraint(array, pltpu.VMEM)


def distant(array):
    return pltpu.with_memory_space_constraint(array, pltpu.HBM)


def prepare(far_tokens, far_gain, far_query, far_key, far_value, out_ref, heads_ref, *held):
    *near_refs, packed, sems = held
    far_refs = (far_tokens, far_gain, far_query, far_key, far_value)
    copies = [
        pltpu.make_async_copy(far, ref, sems.at[i])
        for i, (far, ref) in enumerate(zip(far_refs, near_refs))
    ]
    for copy in copies:
        copy.start()
    for copy in copies:
        copy.wait()
    tokens_ref, gain_ref, *head_refs = near_refs
    rows = out_ref.shape[0]
    values = tokens_ref[...].astype(jnp.float32)
    scale = lax.rsqrt(jnp.mean(values * values, axis=-1, keepdims=True) + 1e-05)
    out_ref[...] = (values * scale * gain_ref[...]).astype(jnp.bfloat16)
    at = 0
    each = heads_ref.shape[0] // rows
    for ref in head_refs:
        block = ref[...].astype(jnp.float32)
        for head in range(ref.shape[1] // HD):
            packed[pl.ds(at, rows, stride=each), :] = block[:, head * HD : (head + 1) * HD]
            at += 1
    heads_ref[...] = packed[...].astype(jnp.bfloat16)


def stacked(refs):
    return jnp.concatenate([ref[...].astype(jnp.float32) for ref in refs], axis=0)


def stack(own_ref, got_ref, out_ref):
    out_ref[...] = stacked([own_ref, got_ref]).astype(out_ref.dtype)


def stack_after(own_ref, got_ref, after, out_ref):
    stack(own_ref, got_ref, out_ref)


def stack_line(own_ref, second_ref, first_ref, share, heads, out_ref):
    first = lax.axis_index("narrow") == 0
    own, one, two = (r[...].astype(jnp.float32) for r in (own_ref, first_ref, second_ref))
    both = [jnp.where(first, own, one), jnp.where(first, one, two)]
    out_ref[...] = jnp.concatenate(both, axis=0).astype(jnp.bfloat16)


def shares(steps, rows, far_routes, far_logits, *refs):
    *_, out_ref, routes_ref, logits_ref, sems = refs
    copies = [
        pltpu.make_async_copy(far_routes, routes_ref, sems.at[0]),
        pltpu.make_async_copy(far_logits, logits_ref, sems.at[1]),
    ]
    for copy in copies:
        copy.start()
    for copy in copies:
        copy.wait()
    count = out_ref.shape[0]
    core = lax.axis_index("narrow")
    me = lax.axis_index("wide") ^ (core * steps[-1])
    logits = logits_ref[...]
    first = 1.0 / (1.0 + jnp.exp(logits[1:2] - logits[0:1]))
    second = 1.0 - first
    chosen = (routes_ref[...] == core).astype(jnp.float32)
    weight_row = chosen[0:1] * first + chosen[1:2] * second
    row = lax.broadcasted_iota(jnp.int32, (count, count), 0)
    column = lax.broadcasted_iota(jnp.int32, (count, count), 1)
    shift = int(math.log2(rows))
    token = (owner_of(row >> shift, me, steps) << shift) | (row & (rows - 1))
    weight = jnp.sum(jnp.where(token == column, weight_row, 0.0), axis=1, keepdims=True)
    out_ref[...] = jnp.broadcast_to(weight, out_ref.shape)


def gate_all(
    own_ref,
    other_ref,
    gate_ref,
    up_ref,
    share_ref,
    far_down,
    hidden_out,
    near_down,
    x_ref,
    sems,
):
    span = near_down.shape[0] // CUTS
    copies = [
        pltpu.make_async_copy(
            far_down.at[0, pl.ds(i * span, span), :],
            near_down.at[pl.ds(i * span, span), :],
            sems.at[i],
        )
        for i in range(CUTS)
    ]
    for copy in copies:
        copy.start()
    tile = min(TILE, gate_ref.shape[2])
    held = own_ref.shape[0]
    x_ref[:held, :] = own_ref[...]
    x_ref[held:, :] = other_ref[...]
    weight = share_ref[:, 0:1]

    @pl.loop(0, gate_ref.shape[2] // tile)
    def _(i):
        columns = pl.ds(pl.multiple_of(i * tile, tile), tile)
        x = x_ref[...]
        gate = jnp.dot(x, gate_ref[0, :, columns], preferred_element_type=jnp.float32)
        up = jnp.dot(x, up_ref[0, :, columns], preferred_element_type=jnp.float32)
        hidden_out[:, columns] = (weight * (gate * jax.nn.sigmoid(gate)) * up).astype(jnp.bfloat16)

    for copy in copies:
        copy.wait()


def down_most(hidden_ref, down_ref, kept_ref, given_ref):
    kept = kept_ref.shape[0]

    @pl.loop(0, kept_ref.shape[1] // WIDE_TILE)
    def _(i):
        columns = pl.ds(pl.multiple_of(i * WIDE_TILE, WIDE_TILE), WIDE_TILE)
        terms = jnp.dot(
            hidden_ref[...], down_ref[:, columns], preferred_element_type=jnp.float32
        )
        kept_ref[:, columns] = terms[:kept]
        given_ref[:, columns] = terms[kept:].astype(jnp.bfloat16)


def down_rest(hidden_ref, down_ref, most_kept, most_given, after, kept_ref, given_ref):
    kept, most = most_kept.shape
    terms = jnp.dot(hidden_ref[...], down_ref[:, most:], preferred_element_type=jnp.float32)
    kept_ref[:, :most] = most_kept[...]
    given_ref[:, :most] = most_given[...]
    kept_ref[:, most:] = terms[:kept]
    given_ref[:, most:] = terms[kept:].astype(jnp.bfloat16)


def combine(terms_ref, taken_ref, after, kept_ref, sent_ref):
    total = terms_ref[...] + taken_ref[...].astype(jnp.float32)
    kept = kept_ref.shape[0]
    kept_ref[...] = total[:kept]
    sent_ref[...] = total[kept:].astype(jnp.bfloat16)


def part_line(terms_ref, taken_ref, after, kept_ref, first_ref, second_ref):
    first = lax.axis_index("narrow") == 0
    total = terms_ref[...] + taken_ref[...].astype(jnp.float32)
    rows = kept_ref.shape[0]
    one, two = total[:rows], total[rows:]
    kept_ref[...] = jnp.where(first, one, 0.0)
    first_ref[...] = jnp.where(first, two, one).astype(jnp.bfloat16)
    second_ref[...] = two.astype(jnp.bfloat16)


def merge(kept_ref, second_ref, first_ref, after, out_ref):
    second = second_ref[...].astype(jnp.float32)
    second = jnp.where(lax.axis_index("narrow") == 0, 0.0, second)
    total = kept_ref[...] + first_ref[...].astype(jnp.float32) + second
    out_ref[...] = total.astype(jnp.bfloat16)


def finish(own_ref, other_ref, tokens_ref, out_ref):
    total = own_ref[...].astype(jnp.float32) + other_ref[...].astype(jnp.float32)
    out_ref[...] = (tokens_ref[...].astype(jnp.float32) + total).astype(jnp.bfloat16)


def attend(
    steps, taking, near_ref, far_ref, keys_ref, values_ref, lengths_ref, place_ref, after, out_ref
):
    slots, span, width = keys_ref.shape
    rows = slots
    kv_local = width // HD
    heads = kv_local * GROUP
    each = heads + 2 * kv_local
    me = lax.axis_index("wide")
    shift = int(math.log2(rows))
    half = near_ref.shape[0]
    head_of = lax.broadcasted_iota(jnp.int32, (heads, 1), 0)
    positions = lax.broadcasted_iota(jnp.int32, (heads, span), 1)

    def by_group(pieces):
        result = pieces[0]
        for g in range(1, kv_local):
            result = jnp.where(head_of >= g * GROUP, pieces[g], result)
        return result

    for order, slot in enumerate(taking):
        request = place_ref[slot]
        at = (place_of(request >> shift, me, steps) << shift) | (request & (rows - 1))
        at = at * each
        inside = pl.ds(pl.multiple_of(jnp.where(at < half, at, at - half), each), each)
        block = jnp.where(at < half, near_ref[inside, :], far_ref[inside, :])
        query = block[:heads]
        own = block[heads:].astype(jnp.float32)
        own_key = by_group([own[g : g + 1] for g in range(kv_local)])
        own_value = by_group([own[kv_local + g : kv_local + g + 1] for g in range(kv_local)])
        own_score = jnp.sum(query.astype(jnp.float32) * own_key, axis=1, keepdims=True) * SCALE
        scores = by_group(
            [
                lax.dot_general(
                    query,
                    keys_ref[slot, :, g * HD : (g + 1) * HD],
                    (((1,), (1,)), ((), ())),
                    preferred_element_type=jnp.float32,
                )
                for g in range(kv_local)
            ]
        )
        scores = jnp.where(positions < lengths_ref[slot], scores * SCALE, -jnp.inf)
        row_max = jnp.maximum(jnp.max(scores, axis=1, keepdims=True), own_score)
        weights = jnp.exp(scores - row_max)
        own_weight = jnp.exp(own_score - row_max)
        total = jnp.sum(weights, axis=1, keepdims=True) + own_weight
        probs = (weights / total).astype(jnp.bfloat16)
        own_prob = (own_weight / total).astype(jnp.bfloat16).astype(jnp.float32)
        mixed = by_group(
            [
                jnp.dot(
                    probs,
                    values_ref[slot, :, g * HD : (g + 1) * HD],
                    preferred_element_type=jnp.float32,
                )
                for g in range(kv_local)
            ]
        )
        out_ref[order * heads : (order + 1) * heads, :] = mixed + own_prob * own_value


def lay_out(heads, pieces, out_ref, held):
    at = 0
    for piece in pieces:
        held[at : at + piece.shape[0], :] = piece[...]
        at += piece.shape[0]
    for head in range(heads):
        out_ref[:, head * HD : (head + 1) * HD] = held[
            pl.ds(head, out_ref.shape[0], stride=heads), :
        ].astype(jnp.bfloat16)


def attend_last(steps, taking, heads, *refs):
    *ins, early, out_ref, late, held = refs
    attend(steps, taking, *ins, late)
    lay_out(heads, [early, late], out_ref, held)


def make_local(wide):
    short, far_step, near_step = steps_of(wide)
    cross_step = far_step ^ near_step
    steps = [cross_step, *short, near_step]
    head_steps = [*short, near_step, far_step]

    def local(
        queries,
        new_keys,
        new_values,
        key_cache,
        value_cache,
        lengths,
        assignment,
        tokens,
        norm_gain,
        routes,
        route_logits,
        w_gate,
        w_up,
        w_down,
    ):
        rows, width = tokens.shape
        half = width // 2
        units = w_gate.shape[2]
        count = rows * wide
        each = (queries.shape[1] + 2 * new_keys.shape[1]) // HD
        bf16, f32 = jnp.bfloat16, jnp.float32
        heads_local = queries.shape[1] // HD
        slots = queries.shape[0]
        dma = pltpu.SemaphoreType.DMA
        piece_bytes = 2 * half * units
        product = 2 * count * half * units

        firsts = [tokens, norm_gain[None], queries, new_keys, new_values]
        x, heads = call(
            prepare,
            [shape((rows, width), bf16), shape((rows * each, HD), bf16)],
            [distant(a) for a in firsts],
            [pltpu.VMEM(a.shape, a.dtype) for a in firsts]
            + [pltpu.VMEM((rows * each, HD), f32), dma((len(firsts),))],
            size=100000,
            far=range(len(firsts)),
        )
        share = call(
            functools.partial(shares, steps, rows),
            shape((count, HD), f32),
            [distant(routes.T), distant(route_logits.T), x, distant(w_gate), distant(w_up)],
            [
                pltpu.VMEM(routes.T.shape, jnp.int32),
                pltpu.VMEM(route_logits.T.shape, f32),
                dma((2,)),
            ],
            size=100000,
            far=range(5),
        )
        first = swap_by_core(x, wide, [cross_step, near_step])
        second = swap_by_core(x, wide, [0, far_step])

        def grown(heads, step):
            got = swap(heads, "wide", wide, step)
            return call(
                stack, shape((2 * heads.shape[0], HD), bf16), [heads, got], size=4 * heads.size
            )

        heads = grown(heads, head_steps[0])
        x = call(
            stack_line,
            shape((2 * rows, width), bf16),
            [x, second, first, share, heads],
            size=8 * rows * width,
            far=(3, 4),
        )
        for order, step in enumerate(short):
            heads = grown(heads, head_steps[order + 1])
            x = call(
                stack_after,
                shape((2 * x.shape[0], width), bf16),
                [x, swap(x, "wide", wide, step), heads],
                size=8 * x.size,
                far=(2,),
            )
        far_heads = swap(heads, "wide", wide, far_step)
        other_x = swap(x, "narrow", 2, 1)
        hidden, near_down = call(
            gate_all,
            [shape((count, units), bf16), pltpu.VMEM((units, width), bf16)],
            [x, other_x, near(w_gate), near(w_up), share, distant(w_down)],
            [pltpu.VMEM((count, width), bf16), dma((CUTS,))],
            flops=4 * product,
            size=6 * piece_bytes,
            far=(5,),
        )
        most = width - WIDE_TILE
        parts = call(
            down_most,
            [shape((count // 2, most), f32), shape((count // 2, most), bf16)],
            [hidden, near(near_down)],
        )
        terms, given = call(
            down_rest,
            [shape((count // 2, width), f32), shape((count // 2, width), bf16)],
            [hidden, near(near_down), *parts, far_heads],
            flops=2 * product,
            size=2 * piece_bytes,
            far=(4,),
        )
        taken = swap(given, "narrow", 2, 1)

        caches = [near(key_cache), near(value_cache), lengths, assignment]
        early_slots = list(range(slots - 1))
        late_slots = list(range(slots - 1, slots))
        early = hidden
        for step in reversed(short):
            kept = terms.shape[0] // 2
            terms, sent = call(
                combine,
                [shape((kept, width), f32), shape((kept, width), bf16)],
                [terms, taken, early],
                size=12 * kept * width,
                far=(2,),
            )
            taken = swap(sent, "wide", wide, step)
            if early is hidden:
                early = call(
                    functools.partial(attend, head_steps, early_slots),
                    shape((len(early_slots) * heads_local, HD), f32),
                    [heads, far_heads, *caches, sent],
                    flops=2 * key_cache.size * GROUP,
                    size=2 * key_cache.size,
                    smem=(4, 5),
                    far=(6,),
                )
        block = shape((rows, width), bf16)
        terms, first, second = call(
            part_line,
            [shape((rows, width), f32), block, block],
            [terms, taken, early],
            size=12 * rows * width,
            far=(2,),
        )
        first_taken = swap_by_core(first, wide, [cross_step, near_step])
        second_taken = swap_by_core(second, wide, [0, far_step])
        context = call(
            functools.partial(attend_last, head_steps, late_slots, heads_local),
            shape(queries.shape, bf16),
            [heads, far_heads, *caches, second, early],
            [
                pltpu.VMEM((len(late_slots) * heads_local, HD), f32),
                pltpu.VMEM((slots * heads_local, HD), f32),
            ],
            flops=2 * key_cache.size * GROUP,
            size=2 * key_cache.size,
            smem=(4, 5),
            far=(6,),
        )
        part = call(
            merge,
            block,
            [terms, second_taken, first_taken, distant(context)],
            size=12 * rows * width,
            far=(3,),
        )
        other = swap(part, "narrow", 2, 1)
        mixed_out = call(finish, block, [part, other, tokens], size=8 * rows * width)
        return (context, mixed_out)

    return local


def solution(mesh):
    placed = (
        P(("groups", "wide"), "narrow"),
        P(("groups", "wide"), "narrow"),
        P(("groups", "wide"), "narrow"),
        P(("groups", "wide"), None, "narrow"),
        P(("groups", "wide"), None, "narrow"),
        P(("groups", "wide")),
        P(("groups", "wide")),
        P(("groups", "wide"), None),
        P(),
        P("groups", None),
        P("groups", None),
        P("narrow", None, "wide"),
        P("narrow", None, "wide"),
        P("narrow", "wide", None),
    )
    return jax.shard_map(
        make_local(mesh.shape["wide"]),
        mesh=mesh,
        in_specs=placed,
        out_specs=(P(("groups", "wide"), "narrow"), P(("groups", "wide"), None)),
        check_vma=False,
    )
```

```python
import functools
import math

import jax
import jax.numpy as jnp
from jax import lax
from jax.experimental import pallas as pl
from jax.experimental.pallas import tpu as pltpu
from jax.sharding import PartitionSpec as P

HQ = 48
KVH = 8
HD = 128
GROUP = HQ // KVH
SCALE = HD ** (-0.5)
TILE = 256
WIDE_TILE = 768
CUTS = 4
MIB = 1024 * 1024


def steps_of(wide):
    bits = int(math.log2(wide))
    return [1 << i for i in range(bits - 2)], wide >> 1, wide >> 2


def swap(block, axis, count, step):
    return lax.ppermute(block, axis, [(i, i ^ step) for i in range(count)])


def swap_by_core(block, wide, steps):
    pairs = [(2 * i + c, 2 * (i ^ step) + c) for c, step in enumerate(steps) for i in range(wide)]
    return lax.ppermute(block, ("wide", "narrow"), pairs)


def owner_of(place, me, steps):
    found = me
    for bit, step in enumerate(steps):
        found = found ^ (((place >> bit) & 1) * step)
    return found


def place_of(owner, me, steps):
    differ = owner ^ me
    found = 0
    for bit, step in enumerate(steps):
        shift = int(math.log2(step))
        found = found | (((differ >> shift) & 1) << bit)
    return found


def call(kernel, outs, ins, scratch=(), flops=0, size=0, limit=4, smem=(), far=()):
    spaces = [pltpu.SMEM if i in smem else pl.ANY if i in far else pltpu.VMEM for i in range(len(ins))]
    return pl.pallas_call(
        kernel,
        name=getattr(kernel, "func", kernel).__name__,
        out_shape=outs,
        in_specs=[pl.BlockSpec(memory_space=space) for space in spaces],
        out_specs=jax.tree.map(lambda _: pl.BlockSpec(memory_space=pltpu.VMEM), outs),
        scratch_shapes=list(scratch),
        compiler_params=pltpu.CompilerParams(vmem_limit_bytes=limit * MIB),
        cost_estimate=pl.CostEstimate(flops=flops, bytes_accessed=size, transcendentals=0),
    )(*ins)


def shape(dims, dtype):
    return jax.ShapeDtypeStruct(dims, dtype)


def near(array):
    return pltpu.with_memory_space_constraint(array, pltpu.VMEM)


def distant(array):
    return pltpu.with_memory_space_constraint(array, pltpu.HBM)


def prepare(far_tokens, far_gain, far_query, far_key, far_value, out_ref, heads_ref, *held):
    *near_refs, packed, sems = held
    far_refs = (far_tokens, far_gain, far_query, far_key, far_value)
    copies = [
        pltpu.make_async_copy(far, ref, sems.at[i])
        for i, (far, ref) in enumerate(zip(far_refs, near_refs))
    ]
    for copy in copies:
        copy.start()
    for copy in copies:
        copy.wait()
    tokens_ref, gain_ref, *head_refs = near_refs
    rows = out_ref.shape[0]
    values = tokens_ref[...].astype(jnp.float32)
    scale = lax.rsqrt(jnp.mean(values * values, axis=-1, keepdims=True) + 1e-05)
    out_ref[...] = (values * scale * gain_ref[...]).astype(jnp.bfloat16)
    at = 0
    each = heads_ref.shape[0] // rows
    for ref in head_refs:
        block = ref[...].astype(jnp.float32)
        for head in range(ref.shape[1] // HD):
            packed[pl.ds(at, rows, stride=each), :] = block[:, head * HD : (head + 1) * HD]
            at += 1
    heads_ref[...] = packed[...].astype(jnp.bfloat16)


def stacked(refs):
    return jnp.concatenate([ref[...].astype(jnp.float32) for ref in refs], axis=0)


def stack(own_ref, got_ref, out_ref):
    out_ref[...] = stacked([own_ref, got_ref]).astype(out_ref.dtype)


def stack_after(own_ref, got_ref, after, out_ref):
    stack(own_ref, got_ref, out_ref)


def stack_line(own_ref, second_ref, first_ref, share, heads, out_ref):
    first = lax.axis_index("narrow") == 0
    own, one, two = (r[...].astype(jnp.float32) for r in (own_ref, first_ref, second_ref))
    both = [jnp.where(first, own, one), jnp.where(first, one, two)]
    out_ref[...] = jnp.concatenate(both, axis=0).astype(jnp.bfloat16)


def shares(steps, rows, far_routes, far_logits, *refs):
    *_, out_ref, routes_ref, logits_ref, sems = refs
    copies = [
        pltpu.make_async_copy(far_routes, routes_ref, sems.at[0]),
        pltpu.make_async_copy(far_logits, logits_ref, sems.at[1]),
    ]
    for copy in copies:
        copy.start()
    for copy in copies:
        copy.wait()
    count = out_ref.shape[0]
    core = lax.axis_index("narrow")
    me = lax.axis_index("wide") ^ (core * steps[-1])
    logits = logits_ref[...]
    first = 1.0 / (1.0 + jnp.exp(logits[1:2] - logits[0:1]))
    second = 1.0 - first
    chosen = (routes_ref[...] == core).astype(jnp.float32)
    weight_row = chosen[0:1] * first + chosen[1:2] * second
    row = lax.broadcasted_iota(jnp.int32, (count, count), 0)
    column = lax.broadcasted_iota(jnp.int32, (count, count), 1)
    shift = int(math.log2(rows))
    token = (owner_of(row >> shift, me, steps) << shift) | (row & (rows - 1))
    weight = jnp.sum(jnp.where(token == column, weight_row, 0.0), axis=1, keepdims=True)
    out_ref[...] = jnp.broadcast_to(weight, out_ref.shape)


def gate_all(
    own_ref,
    other_ref,
    gate_ref,
    up_ref,
    share_ref,
    far_down,
    hidden_out,
    near_down,
    x_ref,
    sems,
):
    span = near_down.shape[0] // CUTS
    copies = [
        pltpu.make_async_copy(
            far_down.at[0, pl.ds(i * span, span), :],
            near_down.at[pl.ds(i * span, span), :],
            sems.at[i],
        )
        for i in range(CUTS)
    ]
    for copy in copies:
        copy.start()
    tile = min(TILE, gate_ref.shape[2])
    held = own_ref.shape[0]
    x_ref[:held, :] = own_ref[...]
    x_ref[held:, :] = other_ref[...]
    weight = share_ref[:, 0:1]

    @pl.loop(0, gate_ref.shape[2] // tile)
    def _(i):
        columns = pl.ds(pl.multiple_of(i * tile, tile), tile)
        x = x_ref[...]
        gate = jnp.dot(x, gate_ref[0, :, columns], preferred_element_type=jnp.float32)
        up = jnp.dot(x, up_ref[0, :, columns], preferred_element_type=jnp.float32)
        hidden_out[:, columns] = (weight * (gate * jax.nn.sigmoid(gate)) * up).astype(jnp.bfloat16)

    for copy in copies:
        copy.wait()


def down_most(hidden_ref, down_ref, kept_ref, given_ref):
    kept = kept_ref.shape[0]

    @pl.loop(0, kept_ref.shape[1] // WIDE_TILE)
    def _(i):
        columns = pl.ds(pl.multiple_of(i * WIDE_TILE, WIDE_TILE), WIDE_TILE)
        terms = jnp.dot(
            hidden_ref[...], down_ref[:, columns], preferred_element_type=jnp.float32
        )
        kept_ref[:, columns] = terms[:kept]
        given_ref[:, columns] = terms[kept:].astype(jnp.bfloat16)


def down_rest(hidden_ref, down_ref, most_kept, most_given, after, kept_ref, given_ref):
    kept, most = most_kept.shape
    terms = jnp.dot(hidden_ref[...], down_ref[:, most:], preferred_element_type=jnp.float32)
    kept_ref[:, :most] = most_kept[...]
    given_ref[:, :most] = most_given[...]
    kept_ref[:, most:] = terms[:kept]
    given_ref[:, most:] = terms[kept:].astype(jnp.bfloat16)


def combine(terms_ref, taken_ref, after, kept_ref, sent_ref):
    total = terms_ref[...] + taken_ref[...].astype(jnp.float32)
    kept = kept_ref.shape[0]
    kept_ref[...] = total[:kept]
    sent_ref[...] = total[kept:].astype(jnp.bfloat16)


def part_line(terms_ref, taken_ref, after, kept_ref, first_ref, second_ref):
    first = lax.axis_index("narrow") == 0
    total = terms_ref[...] + taken_ref[...].astype(jnp.float32)
    rows = kept_ref.shape[0]
    one, two = total[:rows], total[rows:]
    kept_ref[...] = jnp.where(first, one, 0.0)
    first_ref[...] = jnp.where(first, two, one).astype(jnp.bfloat16)
    second_ref[...] = two.astype(jnp.bfloat16)


def merge(kept_ref, second_ref, first_ref, after, out_ref):
    second = second_ref[...].astype(jnp.float32)
    second = jnp.where(lax.axis_index("narrow") == 0, 0.0, second)
    total = kept_ref[...] + first_ref[...].astype(jnp.float32) + second
    out_ref[...] = total.astype(jnp.bfloat16)


def finish(own_ref, other_ref, tokens_ref, out_ref):
    total = own_ref[...].astype(jnp.float32) + other_ref[...].astype(jnp.float32)
    out_ref[...] = (tokens_ref[...].astype(jnp.float32) + total).astype(jnp.bfloat16)


def attend(
    steps, taking, near_ref, far_ref, keys_ref, values_ref, lengths_ref, place_ref, after, out_ref
):
    slots, span, width = keys_ref.shape
    rows = slots
    kv_local = width // HD
    heads = kv_local * GROUP
    each = heads + 2 * kv_local
    me = lax.axis_index("wide")
    shift = int(math.log2(rows))
    half = near_ref.shape[0]
    head_of = lax.broadcasted_iota(jnp.int32, (heads, 1), 0)
    positions = lax.broadcasted_iota(jnp.int32, (heads, span), 1)

    def by_group(pieces):
        result = pieces[0]
        for g in range(1, kv_local):
            result = jnp.where(head_of >= g * GROUP, pieces[g], result)
        return result

    for order, slot in enumerate(taking):
        request = place_ref[slot]
        at = (place_of(request >> shift, me, steps) << shift) | (request & (rows - 1))
        at = at * each
        inside = pl.ds(pl.multiple_of(jnp.where(at < half, at, at - half), each), each)
        block = jnp.where(at < half, near_ref[inside, :], far_ref[inside, :])
        query = block[:heads]
        own = block[heads:].astype(jnp.float32)
        own_key = by_group([own[g : g + 1] for g in range(kv_local)])
        own_value = by_group([own[kv_local + g : kv_local + g + 1] for g in range(kv_local)])
        own_score = jnp.sum(query.astype(jnp.float32) * own_key, axis=1, keepdims=True) * SCALE
        scores = by_group(
            [
                lax.dot_general(
                    query,
                    keys_ref[slot, :, g * HD : (g + 1) * HD],
                    (((1,), (1,)), ((), ())),
                    preferred_element_type=jnp.float32,
                )
                for g in range(kv_local)
            ]
        )
        scores = jnp.where(positions < lengths_ref[slot], scores * SCALE, -jnp.inf)
        row_max = jnp.maximum(jnp.max(scores, axis=1, keepdims=True), own_score)
        weights = jnp.exp(scores - row_max)
        own_weight = jnp.exp(own_score - row_max)
        total = jnp.sum(weights, axis=1, keepdims=True) + own_weight
        probs = (weights / total).astype(jnp.bfloat16)
        own_prob = (own_weight / total).astype(jnp.bfloat16).astype(jnp.float32)
        mixed = by_group(
            [
                jnp.dot(
                    probs,
                    values_ref[slot, :, g * HD : (g + 1) * HD],
                    preferred_element_type=jnp.float32,
                )
                for g in range(kv_local)
            ]
        )
        out_ref[order * heads : (order + 1) * heads, :] = mixed + own_prob * own_value


def lay_out(heads, pieces, out_ref, held):
    at = 0
    for piece in pieces:
        held[at : at + piece.shape[0], :] = piece[...]
        at += piece.shape[0]
    for head in range(heads):
        out_ref[:, head * HD : (head + 1) * HD] = held[
            pl.ds(head, out_ref.shape[0], stride=heads), :
        ].astype(jnp.bfloat16)


def attend_last(steps, taking, heads, *refs):
    *ins, early, out_ref, late, held = refs
    attend(steps, taking, *ins, late)
    lay_out(heads, [early, late], out_ref, held)


def make_local(wide):
    short, far_step, near_step = steps_of(wide)
    cross_step = far_step ^ near_step
    steps = [cross_step, *short, near_step]
    head_steps = [*short, near_step, far_step]

    def local(
        queries,
        new_keys,
        new_values,
        key_cache,
        value_cache,
        lengths,
        assignment,
        tokens,
        norm_gain,
        routes,
        route_logits,
        w_gate,
        w_up,
        w_down,
    ):
        rows, width = tokens.shape
        half = width // 2
        units = w_gate.shape[2]
        count = rows * wide
        each = (queries.shape[1] + 2 * new_keys.shape[1]) // HD
        bf16, f32 = jnp.bfloat16, jnp.float32
        heads_local = queries.shape[1] // HD
        slots = queries.shape[0]
        dma = pltpu.SemaphoreType.DMA
        piece_bytes = 2 * half * units
        product = 2 * count * half * units

        firsts = [tokens, norm_gain[None], queries, new_keys, new_values]
        x, heads = call(
            prepare,
            [shape((rows, width), bf16), shape((rows * each, HD), bf16)],
            [distant(a) for a in firsts],
            [pltpu.VMEM(a.shape, a.dtype) for a in firsts]
            + [pltpu.VMEM((rows * each, HD), f32), dma((len(firsts),))],
            size=100000,
            far=range(len(firsts)),
        )
        share = call(
            functools.partial(shares, steps, rows),
            shape((count, HD), f32),
            [distant(routes.T), distant(route_logits.T), x, distant(w_gate), distant(w_up)],
            [
                pltpu.VMEM(routes.T.shape, jnp.int32),
                pltpu.VMEM(route_logits.T.shape, f32),
                dma((2,)),
            ],
            size=100000,
            far=range(5),
        )
        first = swap_by_core(x, wide, [cross_step, near_step])
        second = swap_by_core(x, wide, [0, far_step])

        def grown(heads, step):
            got = swap(heads, "wide", wide, step)
            return call(
                stack, shape((2 * heads.shape[0], HD), bf16), [heads, got], size=4 * heads.size
            )

        heads = grown(heads, head_steps[0])
        x = call(
            stack_line,
            shape((2 * rows, width), bf16),
            [x, second, first, share, heads],
            size=8 * rows * width,
            far=(3, 4),
        )
        for order, step in enumerate(short):
            heads = grown(heads, head_steps[order + 1])
            x = call(
                stack_after,
                shape((2 * x.shape[0], width), bf16),
                [x, swap(x, "wide", wide, step), heads],
                size=8 * x.size,
                far=(2,),
            )
        far_heads = swap(heads, "wide", wide, far_step)
        other_x = swap(x, "narrow", 2, 1)
        hidden, near_down = call(
            gate_all,
            [shape((count, units), bf16), pltpu.VMEM((units, width), bf16)],
            [x, other_x, near(w_gate), near(w_up), share, distant(w_down)],
            [pltpu.VMEM((count, width), bf16), dma((CUTS,))],
            flops=4 * product,
            size=6 * piece_bytes,
            far=(5,),
        )
        most = width - WIDE_TILE
        parts = call(
            down_most,
            [shape((count // 2, most), f32), shape((count // 2, most), bf16)],
            [hidden, near(near_down)],
        )
        terms, given = call(
            down_rest,
            [shape((count // 2, width), f32), shape((count // 2, width), bf16)],
            [hidden, near(near_down), *parts, far_heads],
            flops=2 * product,
            size=2 * piece_bytes,
            far=(4,),
        )
        taken = swap(given, "narrow", 2, 1)

        caches = [near(key_cache), near(value_cache), lengths, assignment]
        early_slots = list(range(slots - 1))
        late_slots = list(range(slots - 1, slots))
        early = hidden
        for step in reversed(short):
            kept = terms.shape[0] // 2
            terms, sent = call(
                combine,
                [shape((kept, width), f32), shape((kept, width), bf16)],
                [terms, taken, early],
                size=12 * kept * width,
                far=(2,),
            )
            taken = swap(sent, "wide", wide, step)
            if early is hidden:
                early = call(
                    functools.partial(attend, head_steps, early_slots),
                    shape((len(early_slots) * heads_local, HD), f32),
                    [heads, far_heads, *caches, sent],
                    flops=2 * key_cache.size * GROUP,
                    size=2 * key_cache.size,
                    smem=(4, 5),
                    far=(6,),
                )
        block = shape((rows, width), bf16)
        terms, first, second = call(
            part_line,
            [shape((rows, width), f32), block, block],
            [terms, taken, early],
            size=12 * rows * width,
            far=(2,),
        )
        first_taken = swap_by_core(first, wide, [cross_step, near_step])
        second_taken = swap_by_core(second, wide, [0, far_step])
        context = call(
            functools.partial(attend_last, head_steps, late_slots, heads_local),
            shape(queries.shape, bf16),
            [heads, far_heads, *caches, second, early],
            [
                pltpu.VMEM((len(late_slots) * heads_local, HD), f32),
                pltpu.VMEM((slots * heads_local, HD), f32),
            ],
            flops=2 * key_cache.size * GROUP,
            size=2 * key_cache.size,
            smem=(4, 5),
            far=(6,),
        )
        part = call(
            merge,
            block,
            [terms, second_taken, first_taken, distant(context)],
            size=12 * rows * width,
            far=(3,),
        )
        other = swap(part, "narrow", 2, 1)
        mixed_out = call(finish, block, [part, other, tokens], size=8 * rows * width)
        return (context, mixed_out)

    return local


def solution(mesh):
    placed = (
        P(("groups", "wide"), "narrow"),
        P(("groups", "wide"), "narrow"),
        P(("groups", "wide"), "narrow"),
        P(("groups", "wide"), None, "narrow"),
        P(("groups", "wide"), None, "narrow"),
        P(("groups", "wide")),
        P(("groups", "wide")),
        P(("groups", "wide"), None),
        P(),
        P("groups", None),
        P("groups", None),
        P("narrow", None, "wide"),
        P("narrow", None, "wide"),
        P("narrow", "wide", None),
    )
    return jax.shard_map(
        make_local(mesh.shape["wide"]),
        mesh=mesh,
        in_specs=placed,
        out_specs=(P(("groups", "wide"), "narrow"), P(("groups", "wide"), None)),
        check_vma=False,
    )
```

```python
import functools
import math

import jax
import jax.numpy as jnp
from jax import lax
from jax.experimental import pallas as pl
from jax.experimental.pallas import tpu as pltpu
from jax.sharding import PartitionSpec as P

HQ = 48
KVH = 8
HD = 128
GROUP = HQ // KVH
SCALE = HD ** (-0.5)
TILE = 512
WIDE_TILE = 1536
CUTS = 4
MIB = 1024 * 1024


def steps_of(wide):
    bits = int(math.log2(wide))
    return [1 << i for i in range(bits - 2)] + [wide >> 1, wide >> 2]


def swap(block, axis, count, step):
    return lax.ppermute(block, axis, [(i, i ^ step) for i in range(count)])


def owner_of(place, me, steps):
    found = me
    for bit, step in enumerate(steps):
        found = found ^ (((place >> bit) & 1) * step)
    return found


def place_of(owner, me, steps):
    differ = owner ^ me
    found = 0
    for bit, step in enumerate(steps):
        shift = int(math.log2(step))
        found = found | (((differ >> shift) & 1) << bit)
    return found


def call(kernel, outs, ins, scratch=(), flops=0, size=0, limit=4, smem=(), far=()):
    spaces = [pltpu.SMEM if i in smem else pl.ANY if i in far else pltpu.VMEM for i in range(len(ins))]
    return pl.pallas_call(
        kernel,
        name=getattr(kernel, "func", kernel).__name__,
        out_shape=outs,
        in_specs=[pl.BlockSpec(memory_space=space) for space in spaces],
        out_specs=jax.tree.map(lambda _: pl.BlockSpec(memory_space=pltpu.VMEM), outs),
        scratch_shapes=list(scratch),
        compiler_params=pltpu.CompilerParams(vmem_limit_bytes=limit * MIB),
        cost_estimate=pl.CostEstimate(flops=flops, bytes_accessed=size, transcendentals=0),
    )(*ins)


def column_copies(source, target, sems, first):
    columns = target.shape[1] // CUTS
    return [
        pltpu.make_async_copy(
            source.at[0, :, pl.ds(pl.multiple_of(first + i * columns, columns), columns)],
            target.at[:, pl.ds(i * columns, columns)],
            sems.at[i],
        )
        for i in range(CUTS)
    ]


def shape(dims, dtype):
    return jax.ShapeDtypeStruct(dims, dtype)


def near(array):
    return pltpu.with_memory_space_constraint(array, pltpu.VMEM)


def distant(array):
    return pltpu.with_memory_space_constraint(array, pltpu.HBM)


def pack(far_query, far_key, far_value, far_tokens, far_gain, heads_ref, *held):
    tokens_ref, gain_ref, *near_refs, packed, sems = held
    far_refs = (far_query, far_key, far_value, far_tokens, far_gain)
    copies = [
        pltpu.make_async_copy(far, ref, sems.at[i])
        for i, (far, ref) in enumerate(zip(far_refs, (*near_refs, tokens_ref, gain_ref)))
    ]
    for copy in copies:
        copy.start()
    for copy in copies:
        copy.wait()
    rows = near_refs[0].shape[0]
    at = 0
    each = heads_ref.shape[0] // rows
    for ref in near_refs:
        block = ref[...].astype(jnp.float32)
        for head in range(ref.shape[1] // HD):
            packed[pl.ds(at, rows, stride=each), :] = block[:, head * HD : (head + 1) * HD]
            at += 1
    heads_ref[...] = packed[...].astype(jnp.bfloat16)


def norm_both(own_ref, got_ref, gain_ref, share, heads, out_ref):
    half = out_ref.shape[1]
    core = lax.axis_index("narrow")
    values = stacked([own_ref, got_ref])
    scale = lax.rsqrt(jnp.mean(values * values, axis=-1, keepdims=True) + 1e-05)
    normed = values * scale * gain_ref[...]
    out_ref[...] = jnp.where(core == 0, normed[:, :half], normed[:, half:]).astype(jnp.bfloat16)


def stacked(refs):
    return jnp.concatenate([ref[...].astype(jnp.float32) for ref in refs], axis=0)


def stack(*refs):
    refs[-1][...] = stacked(refs[:-1]).astype(refs[-1].dtype)


def stack_line(own_ref, last_ref, far_ref, next_ref, heads, out_ref):
    stack(own_ref, far_ref, next_ref, last_ref, out_ref)


def stack_after(own_ref, got_ref, after, out_ref):
    stack(own_ref, got_ref, out_ref)


def grow_both(own_ref, got_ref, own_heads, got_heads, *refs):
    refs[-2][...] = stacked([own_ref, got_ref]).astype(jnp.bfloat16)
    refs[-1][...] = stacked([own_heads, got_heads]).astype(jnp.bfloat16)


def shares(steps, rows, far_routes, far_logits, *refs):
    *_, out_ref, routes_ref, logits_ref, sems = refs
    copies = [
        pltpu.make_async_copy(far_routes, routes_ref, sems.at[0]),
        pltpu.make_async_copy(far_logits, logits_ref, sems.at[1]),
    ]
    for copy in copies:
        copy.start()
    for copy in copies:
        copy.wait()
    count = out_ref.shape[0]
    core = lax.axis_index("narrow")
    me = lax.axis_index("wide")
    logits = logits_ref[...]
    first = 1.0 / (1.0 + jnp.exp(logits[1:2] - logits[0:1]))
    second = 1.0 - first
    chosen = (routes_ref[...] == core).astype(jnp.float32)
    weight_row = chosen[0:1] * first + chosen[1:2] * second
    row = lax.broadcasted_iota(jnp.int32, (count, count), 0)
    column = lax.broadcasted_iota(jnp.int32, (count, count), 1)
    shift = int(math.log2(rows))
    token = (owner_of(row >> shift, me, steps) << shift) | (row & (rows - 1))
    weight = jnp.sum(jnp.where(token == column, weight_row, 0.0), axis=1, keepdims=True)
    out_ref[...] = jnp.broadcast_to(weight, out_ref.shape)


def gate_all(
    x_ref,
    other_ref,
    gate_ref,
    up_ref,
    share_ref,
    far_down,
    hidden_out,
    down_own,
    down_other,
    sems,
):
    count, depth = x_ref.shape
    core = lax.axis_index("narrow")
    other_copies = column_copies(far_down, down_other, sems.at[0], (1 - core) * depth)
    own_copies = column_copies(far_down, down_own, sems.at[1], core * depth)
    for copy in other_copies + own_copies:
        copy.start()
    tile = min(TILE, gate_ref.shape[2])
    own = pl.ds(pl.multiple_of(core * depth, depth), depth)
    other = pl.ds(pl.multiple_of((1 - core) * depth, depth), depth)

    weight = share_ref[:, 0:1]

    @pl.loop(0, gate_ref.shape[2] // tile)
    def _(i):
        columns = pl.ds(pl.multiple_of(i * tile, tile), tile)
        x, y = x_ref[...], other_ref[...]
        gate = jnp.dot(x, gate_ref[0, own, columns], preferred_element_type=jnp.float32)
        gate += jnp.dot(y, gate_ref[0, other, columns], preferred_element_type=jnp.float32)
        up = jnp.dot(x, up_ref[0, own, columns], preferred_element_type=jnp.float32)
        up += jnp.dot(y, up_ref[0, other, columns], preferred_element_type=jnp.float32)
        hidden_out[:, columns] = (weight * (gate * jax.nn.sigmoid(gate)) * up).astype(jnp.bfloat16)

    for copy in other_copies + own_copies:
        copy.wait()


def down(hidden_ref, down_ref, after, out_ref):
    @pl.loop(0, out_ref.shape[1] // WIDE_TILE)
    def _(i):
        columns = pl.ds(pl.multiple_of(i * WIDE_TILE, WIDE_TILE), WIDE_TILE)
        out_ref[:, columns] = jnp.dot(
            hidden_ref[...], down_ref[:, columns], preferred_element_type=jnp.float32
        ).astype(out_ref.dtype)


def part_line(terms_ref, taken_ref, kept_ref, far_ref, next_ref, last_ref):
    total = terms_ref[...] + taken_ref[...].astype(jnp.float32)
    rows = kept_ref.shape[0]
    kept_ref[...] = total[:rows]
    for i, ref in enumerate((far_ref, next_ref, last_ref)):
        ref[...] = total[(i + 1) * rows : (i + 2) * rows].astype(jnp.bfloat16)


def combine(*refs):
    terms_ref, *taken, after, kept_ref, sent_ref = refs
    total = terms_ref[...]
    for ref in taken:
        total = total + ref[...].astype(jnp.float32)
    kept = kept_ref.shape[0]
    kept_ref[...] = total[:kept]
    sent_ref[...] = total[kept:].astype(jnp.bfloat16)


def finish(kept_ref, taken_ref, tokens_ref, after, out_ref):
    half = kept_ref.shape[1]
    core = lax.axis_index("narrow")
    own = tokens_ref[...].astype(jnp.float32)
    own = jnp.where(core == 0, own[:, :half], own[:, half:])
    total = kept_ref[...] + taken_ref[...].astype(jnp.float32)
    out_ref[...] = (own + total).astype(jnp.bfloat16)


def join(own_ref, other_ref, out_ref):
    half = own_ref.shape[1]
    core = lax.axis_index("narrow")
    own, other = own_ref[...], other_ref[...]
    out_ref[:, :half] = jnp.where(core == 0, own, other)
    out_ref[:, half:] = jnp.where(core == 0, other, own)


def attend(
    steps, taking, near_ref, far_ref, keys_ref, values_ref, lengths_ref, place_ref, after, out_ref
):
    slots, span, width = keys_ref.shape
    rows = slots
    kv_local = width // HD
    heads = kv_local * GROUP
    each = heads + 2 * kv_local
    me = lax.axis_index("wide")
    shift = int(math.log2(rows))
    half = near_ref.shape[0]
    head_of = lax.broadcasted_iota(jnp.int32, (heads, 1), 0)
    positions = lax.broadcasted_iota(jnp.int32, (heads, span), 1)

    def by_group(pieces):
        result = pieces[0]
        for g in range(1, kv_local):
            result = jnp.where(head_of >= g * GROUP, pieces[g], result)
        return result

    for order, slot in enumerate(taking):
        request = place_ref[slot]
        at = (place_of(request >> shift, me, steps) << shift) | (request & (rows - 1))
        at = at * each
        inside = pl.ds(pl.multiple_of(jnp.where(at < half, at, at - half), each), each)
        block = jnp.where(at < half, near_ref[inside, :], far_ref[inside, :])
        query = block[:heads]
        own = block[heads:].astype(jnp.float32)
        own_key = by_group([own[g : g + 1] for g in range(kv_local)])
        own_value = by_group([own[kv_local + g : kv_local + g + 1] for g in range(kv_local)])
        own_score = jnp.sum(query.astype(jnp.float32) * own_key, axis=1, keepdims=True) * SCALE
        scores = by_group(
            [
                lax.dot_general(
                    query,
                    keys_ref[slot, :, g * HD : (g + 1) * HD],
                    (((1,), (1,)), ((), ())),
                    preferred_element_type=jnp.float32,
                )
                for g in range(kv_local)
            ]
        )
        scores = jnp.where(positions < lengths_ref[slot], scores * SCALE, -jnp.inf)
        row_max = jnp.maximum(jnp.max(scores, axis=1, keepdims=True), own_score)
        weights = jnp.exp(scores - row_max)
        own_weight = jnp.exp(own_score - row_max)
        total = jnp.sum(weights, axis=1, keepdims=True) + own_weight
        probs = (weights / total).astype(jnp.bfloat16)
        own_prob = (own_weight / total).astype(jnp.bfloat16).astype(jnp.float32)
        mixed = by_group(
            [
                jnp.dot(
                    probs,
                    values_ref[slot, :, g * HD : (g + 1) * HD],
                    preferred_element_type=jnp.float32,
                )
                for g in range(kv_local)
            ]
        )
        out_ref[order * heads : (order + 1) * heads, :] = mixed + own_prob * own_value


def lay_out(heads, pieces, out_ref, held):
    at = 0
    for piece in pieces:
        held[at : at + piece.shape[0], :] = piece[...]
        at += piece.shape[0]
    for head in range(heads):
        out_ref[:, head * HD : (head + 1) * HD] = held[
            pl.ds(head, out_ref.shape[0], stride=heads), :
        ].astype(jnp.bfloat16)


def attend_last(steps, taking, heads, *refs):
    *ins, early, out_ref, late, held = refs
    attend(steps, taking, *ins, late)
    lay_out(heads, [early, late], out_ref, held)


def make_local(wide):
    steps = steps_of(wide)

    def local(
        queries,
        new_keys,
        new_values,
        key_cache,
        value_cache,
        lengths,
        assignment,
        tokens,
        norm_gain,
        routes,
        route_logits,
        w_gate,
        w_up,
        w_down,
    ):
        rows, width = tokens.shape
        half = width // 2
        units = w_gate.shape[2]
        count = rows * wide
        each = (queries.shape[1] + 2 * new_keys.shape[1]) // HD
        core = lax.axis_index("narrow")
        bf16, f32 = jnp.bfloat16, jnp.float32
        heads_local = queries.shape[1] // HD
        dma = pltpu.SemaphoreType.DMA
        piece_bytes = 2 * half * units

        got = swap(tokens, "wide", wide, steps[0])
        heads_in = [queries, new_keys, new_values]
        row_in = [tokens, norm_gain[None]]
        heads, *row_near = call(
            pack,
            [shape((rows * each, HD), bf16)] + [pltpu.VMEM(a.shape, a.dtype) for a in row_in],
            [distant(a) for a in heads_in + row_in],
            [pltpu.VMEM(a.shape, a.dtype) for a in heads_in]
            + [pltpu.VMEM((rows * each, HD), f32), dma((5,))],
            size=100000,
            far=range(5),
        )
        share = call(
            functools.partial(shares, steps, rows),
            shape((count, HD), f32),
            [distant(routes.T), distant(route_logits.T), heads, distant(w_gate), distant(w_up)],
            [
                pltpu.VMEM(routes.T.shape, jnp.int32),
                pltpu.VMEM(route_logits.T.shape, f32),
                dma((2,)),
            ],
            size=100000,
            far=range(5),
        )
        x = call(
            norm_both,
            shape((2 * rows, half), bf16),
            [near(row_near[0]), got, near(row_near[1]), share, heads],
            size=100000,
            far=(3, 4),
        )

        def grown(heads, step):
            got = swap(heads, "wide", wide, step)
            return call(
                stack, shape((2 * heads.shape[0], HD), bf16), [heads, got], size=4 * heads.size
            )

        for step in steps[1:-2]:
            heads = grown(heads, step)
            x = call(
                stack_after,
                shape((2 * x.shape[0], half), bf16),
                [x, swap(x, "wide", wide, step), heads],
                size=8 * x.size,
                far=(2,),
            )
        heads = grown(heads, steps[0])
        line_steps = [steps[-2], steps[-1], steps[-2] ^ steps[-1]]
        last = swap(x, "wide", wide, line_steps[2])
        line = [swap(x, "wide", wide, step) for step in line_steps[:2]]
        got_heads = swap(heads, "wide", wide, steps[-2])
        x = call(
            stack_line,
            shape((count, half), bf16),
            [x, last, *line, heads],
            size=8 * count * half,
            far=(4,),
        )

        product = 2 * count * half * units
        other_x = swap(x, "narrow", 2, 1)
        whole = pltpu.VMEM((units, half), bf16)
        hidden, down_own, down_other = call(
            gate_all,
            [shape((count, units), bf16), whole, whole],
            [
                x,
                other_x,
                near(w_gate),
                near(w_up),
                share,
                distant(w_down),
            ],
            [dma((2, CUTS))],
            flops=4 * product,
            size=6 * piece_bytes,
            far=(5,),
        )
        heads = call(
            stack_after,
            shape((2 * heads.shape[0], HD), bf16),
            [heads, got_heads, hidden],
            size=8 * heads.size,
            far=(2,),
        )
        given = call(
            down,
            shape((count, half), bf16),
            [hidden, near(down_other), heads],
            flops=product,
            size=piece_bytes,
            far=(2,),
        )
        taken = swap(given, "narrow", 2, 1)
        far_heads = swap(heads, "wide", wide, steps[-1])
        terms = call(
            down,
            shape((count, half), f32),
            [hidden, near(down_own), given],
            flops=product,
            size=piece_bytes,
            far=(2,),
        )

        caches = [near(key_cache), near(value_cache), lengths, assignment]
        slots = queries.shape[0]
        early_slots = list(range(slots - 1))
        late_slots = list(range(slots - 1, slots))
        quarter = count // 4
        block = shape((quarter, half), bf16)
        terms, *sent = call(
            part_line,
            [shape((quarter, half), f32), block, block, block],
            [terms, taken],
            size=terms.size * 8,
        )
        taken = [swap(part, "wide", wide, step) for part, step in zip(sent, line_steps)]
        early = call(
            functools.partial(attend, steps, early_slots),
            shape((len(early_slots) * heads_local, HD), f32),
            [heads, far_heads, *caches, sent[0]],
            flops=2 * key_cache.size * GROUP,
            size=2 * key_cache.size,
            smem=(4, 5),
            far=(6,),
        )
        for step in reversed(steps[:-2]):
            kept = terms.shape[0] // 2
            terms, sent = call(
                combine,
                [shape((kept, half), f32), shape((kept, half), bf16)],
                [terms, *taken, early],
                size=terms.size * 8,
                far=(1 + len(taken),),
            )
            taken = [swap(sent, "wide", wide, step)]
        context = call(
            functools.partial(attend_last, steps, late_slots, heads_local),
            shape(queries.shape, bf16),
            [heads, far_heads, *caches, sent, early],
            [
                pltpu.VMEM((len(late_slots) * heads_local, HD), f32),
                pltpu.VMEM((slots * heads_local, HD), f32),
            ],
            flops=2 * key_cache.size * GROUP,
            size=2 * key_cache.size,
            smem=(4, 5),
            far=(6,),
        )
        piece = call(
            finish,
            shape((rows, half), bf16),
            [terms, *taken, tokens, distant(context)],
            size=terms.size * 8,
            far=(3,),
        )
        other = swap(piece, "narrow", 2, 1)
        mixed_out = call(join, shape((rows, width), bf16), [piece, other], size=terms.size * 4)
        return (context, mixed_out)

    return local


def solution(mesh):
    placed = (
        P(("groups", "wide"), "narrow"),
        P(("groups", "wide"), "narrow"),
        P(("groups", "wide"), "narrow"),
        P(("groups", "wide"), None, "narrow"),
        P(("groups", "wide"), None, "narrow"),
        P(("groups", "wide")),
        P(("groups", "wide")),
        P(("groups", "wide"), None),
        P(),
        P("groups", None),
        P("groups", None),
        P("narrow", None, "wide"),
        P("narrow", None, "wide"),
        P("narrow", "wide", None),
    )
    return jax.shard_map(
        make_local(mesh.shape["wide"]),
        mesh=mesh,
        in_specs=placed,
        out_specs=(P(("groups", "wide"), "narrow"), P(("groups", "wide"), None)),
        check_vma=False,
    )
```

```python
import functools
import math

import jax
import jax.numpy as jnp
from jax import lax
from jax.experimental import pallas as pl
from jax.experimental.pallas import tpu as pltpu
from jax.sharding import PartitionSpec as P

HQ = 48
KVH = 8
HD = 128
GROUP = HQ // KVH
SCALE = HD ** (-0.5)
TILE = 512
WIDE_TILE = 1536
CUTS = 4
MIB = 1024 * 1024


def steps_of(wide):
    bits = int(math.log2(wide))
    return [1 << i for i in range(bits - 2)] + [wide >> 1, wide >> 2]


def swap(block, axis, count, step):
    return lax.ppermute(block, axis, [(i, i ^ step) for i in range(count)])


def owner_of(place, me, steps):
    found = me
    for bit, step in enumerate(steps):
        found = found ^ (((place >> bit) & 1) * step)
    return found


def place_of(owner, me, steps):
    differ = owner ^ me
    found = 0
    for bit, step in enumerate(steps):
        shift = int(math.log2(step))
        found = found | (((differ >> shift) & 1) << bit)
    return found


def call(kernel, outs, ins, scratch=(), flops=0, size=0, limit=4, smem=(), far=()):
    spaces = [pltpu.SMEM if i in smem else pl.ANY if i in far else pltpu.VMEM for i in range(len(ins))]
    return pl.pallas_call(
        kernel,
        name=getattr(kernel, "func", kernel).__name__,
        out_shape=outs,
        in_specs=[pl.BlockSpec(memory_space=space) for space in spaces],
        out_specs=jax.tree.map(lambda _: pl.BlockSpec(memory_space=pltpu.VMEM), outs),
        scratch_shapes=list(scratch),
        compiler_params=pltpu.CompilerParams(vmem_limit_bytes=limit * MIB),
        cost_estimate=pl.CostEstimate(flops=flops, bytes_accessed=size, transcendentals=0),
    )(*ins)


def column_copies(source, target, sems, first):
    columns = target.shape[1] // CUTS
    return [
        pltpu.make_async_copy(
            source.at[0, :, pl.ds(pl.multiple_of(first + i * columns, columns), columns)],
            target.at[:, pl.ds(i * columns, columns)],
            sems.at[i],
        )
        for i in range(CUTS)
    ]


def shape(dims, dtype):
    return jax.ShapeDtypeStruct(dims, dtype)


def near(array):
    return pltpu.with_memory_space_constraint(array, pltpu.VMEM)


def distant(array):
    return pltpu.with_memory_space_constraint(array, pltpu.HBM)


def pack(far_query, far_key, far_value, far_tokens, far_gain, heads_ref, *held):
    tokens_ref, gain_ref, *near_refs, packed, sems = held
    far_refs = (far_query, far_key, far_value, far_tokens, far_gain)
    copies = [
        pltpu.make_async_copy(far, ref, sems.at[i])
        for i, (far, ref) in enumerate(zip(far_refs, (*near_refs, tokens_ref, gain_ref)))
    ]
    for copy in copies:
        copy.start()
    for copy in copies:
        copy.wait()
    rows = near_refs[0].shape[0]
    at = 0
    each = heads_ref.shape[0] // rows
    for ref in near_refs:
        block = ref[...].astype(jnp.float32)
        for head in range(ref.shape[1] // HD):
            packed[pl.ds(at, rows, stride=each), :] = block[:, head * HD : (head + 1) * HD]
            at += 1
    heads_ref[...] = packed[...].astype(jnp.bfloat16)


def norm_both(own_ref, got_ref, gain_ref, share, heads, out_ref):
    half = out_ref.shape[1]
    core = lax.axis_index("narrow")
    values = stacked([own_ref, got_ref])
    scale = lax.rsqrt(jnp.mean(values * values, axis=-1, keepdims=True) + 1e-05)
    normed = values * scale * gain_ref[...]
    out_ref[...] = jnp.where(core == 0, normed[:, :half], normed[:, half:]).astype(jnp.bfloat16)


def stacked(refs):
    return jnp.concatenate([ref[...].astype(jnp.float32) for ref in refs], axis=0)


def stack(*refs):
    refs[-1][...] = stacked(refs[:-1]).astype(refs[-1].dtype)


def stack_line(own_ref, last_ref, far_ref, got_heads, next_ref, own_heads, out_ref, heads_ref):
    count = own_heads.shape[0]
    heads_ref[:count, :] = own_heads[...]
    heads_ref[count:, :] = got_heads[:count, :]
    rows = [own_ref, far_ref, next_ref, last_ref]
    out_ref[...] = stacked(rows).astype(jnp.bfloat16)


def widen(own_ref, out_ref):
    count = own_ref.shape[0]
    out_ref[:count, :] = own_ref[...]
    out_ref[count:, :] = jnp.zeros((out_ref.shape[0] - count, HD), out_ref.dtype)


def stack_after(own_ref, got_ref, after, out_ref):
    stack(own_ref, got_ref, out_ref)


def grow_both(own_ref, got_ref, own_heads, got_heads, *refs):
    refs[-2][...] = stacked([own_ref, got_ref]).astype(jnp.bfloat16)
    refs[-1][...] = stacked([own_heads, got_heads]).astype(jnp.bfloat16)


def shares(steps, rows, far_routes, far_logits, *refs):
    *_, out_ref, routes_ref, logits_ref, sems = refs
    copies = [
        pltpu.make_async_copy(far_routes, routes_ref, sems.at[0]),
        pltpu.make_async_copy(far_logits, logits_ref, sems.at[1]),
    ]
    for copy in copies:
        copy.start()
    for copy in copies:
        copy.wait()
    count = out_ref.shape[0]
    core = lax.axis_index("narrow")
    me = lax.axis_index("wide")
    logits = logits_ref[...]
    first = 1.0 / (1.0 + jnp.exp(logits[1:2] - logits[0:1]))
    second = 1.0 - first
    chosen = (routes_ref[...] == core).astype(jnp.float32)
    weight_row = chosen[0:1] * first + chosen[1:2] * second
    row = lax.broadcasted_iota(jnp.int32, (count, count), 0)
    column = lax.broadcasted_iota(jnp.int32, (count, count), 1)
    shift = int(math.log2(rows))
    token = (owner_of(row >> shift, me, steps) << shift) | (row & (rows - 1))
    weight = jnp.sum(jnp.where(token == column, weight_row, 0.0), axis=1, keepdims=True)
    out_ref[...] = jnp.broadcast_to(weight, out_ref.shape)


def gate_all(
    x_ref,
    other_ref,
    gate_ref,
    up_ref,
    share_ref,
    far_down,
    hidden_out,
    down_own,
    down_other,
    sems,
):
    count, depth = x_ref.shape
    core = lax.axis_index("narrow")
    other_copies = column_copies(far_down, down_other, sems.at[0], (1 - core) * depth)
    own_copies = column_copies(far_down, down_own, sems.at[1], core * depth)
    for copy in other_copies + own_copies:
        copy.start()
    tile = min(TILE, gate_ref.shape[2])
    own = pl.ds(pl.multiple_of(core * depth, depth), depth)
    other = pl.ds(pl.multiple_of((1 - core) * depth, depth), depth)

    weight = share_ref[:, 0:1]

    @pl.loop(0, gate_ref.shape[2] // tile)
    def _(i):
        columns = pl.ds(pl.multiple_of(i * tile, tile), tile)
        x, y = x_ref[...], other_ref[...]
        gate = jnp.dot(x, gate_ref[0, own, columns], preferred_element_type=jnp.float32)
        gate += jnp.dot(y, gate_ref[0, other, columns], preferred_element_type=jnp.float32)
        up = jnp.dot(x, up_ref[0, own, columns], preferred_element_type=jnp.float32)
        up += jnp.dot(y, up_ref[0, other, columns], preferred_element_type=jnp.float32)
        hidden_out[:, columns] = (weight * (gate * jax.nn.sigmoid(gate)) * up).astype(jnp.bfloat16)

    for copy in other_copies + own_copies:
        copy.wait()


def down(hidden_ref, down_ref, after, out_ref):
    @pl.loop(0, out_ref.shape[1] // WIDE_TILE)
    def _(i):
        columns = pl.ds(pl.multiple_of(i * WIDE_TILE, WIDE_TILE), WIDE_TILE)
        out_ref[:, columns] = jnp.dot(
            hidden_ref[...], down_ref[:, columns], preferred_element_type=jnp.float32
        ).astype(out_ref.dtype)


def part_line(terms_ref, taken_ref, kept_ref, far_ref, next_ref, last_ref):
    total = terms_ref[...] + taken_ref[...].astype(jnp.float32)
    rows = kept_ref.shape[0]
    kept_ref[...] = total[:rows]
    for i, ref in enumerate((far_ref, next_ref, last_ref)):
        ref[...] = total[(i + 1) * rows : (i + 2) * rows].astype(jnp.bfloat16)


def combine(*refs):
    terms_ref, *taken, after, kept_ref, sent_ref = refs
    total = terms_ref[...]
    for ref in taken:
        total = total + ref[...].astype(jnp.float32)
    kept = kept_ref.shape[0]
    kept_ref[...] = total[:kept]
    sent_ref[...] = total[kept:].astype(jnp.bfloat16)


def finish(kept_ref, taken_ref, tokens_ref, after, out_ref):
    half = kept_ref.shape[1]
    core = lax.axis_index("narrow")
    own = tokens_ref[...].astype(jnp.float32)
    own = jnp.where(core == 0, own[:, :half], own[:, half:])
    total = kept_ref[...] + taken_ref[...].astype(jnp.float32)
    out_ref[...] = (own + total).astype(jnp.bfloat16)


def join(own_ref, other_ref, out_ref):
    half = own_ref.shape[1]
    core = lax.axis_index("narrow")
    own, other = own_ref[...], other_ref[...]
    out_ref[:, :half] = jnp.where(core == 0, own, other)
    out_ref[:, half:] = jnp.where(core == 0, other, own)


def attend(
    steps, taking, near_ref, far_ref, keys_ref, values_ref, lengths_ref, place_ref, after, out_ref
):
    slots, span, width = keys_ref.shape
    rows = slots
    kv_local = width // HD
    heads = kv_local * GROUP
    each = heads + 2 * kv_local
    me = lax.axis_index("wide")
    shift = int(math.log2(rows))
    half = near_ref.shape[0]
    head_of = lax.broadcasted_iota(jnp.int32, (heads, 1), 0)
    positions = lax.broadcasted_iota(jnp.int32, (heads, span), 1)

    def by_group(pieces):
        result = pieces[0]
        for g in range(1, kv_local):
            result = jnp.where(head_of >= g * GROUP, pieces[g], result)
        return result

    for order, slot in enumerate(taking):
        request = place_ref[slot]
        at = (place_of(request >> shift, me, steps) << shift) | (request & (rows - 1))
        at = at * each
        inside = pl.ds(pl.multiple_of(jnp.where(at < half, at, at - half), each), each)
        block = jnp.where(at < half, near_ref[inside, :], far_ref[inside, :])
        query = block[:heads]
        own = block[heads:].astype(jnp.float32)
        own_key = by_group([own[g : g + 1] for g in range(kv_local)])
        own_value = by_group([own[kv_local + g : kv_local + g + 1] for g in range(kv_local)])
        own_score = jnp.sum(query.astype(jnp.float32) * own_key, axis=1, keepdims=True) * SCALE
        scores = by_group(
            [
                lax.dot_general(
                    query,
                    keys_ref[slot, :, g * HD : (g + 1) * HD],
                    (((1,), (1,)), ((), ())),
                    preferred_element_type=jnp.float32,
                )
                for g in range(kv_local)
            ]
        )
        scores = jnp.where(positions < lengths_ref[slot], scores * SCALE, -jnp.inf)
        row_max = jnp.maximum(jnp.max(scores, axis=1, keepdims=True), own_score)
        weights = jnp.exp(scores - row_max)
        own_weight = jnp.exp(own_score - row_max)
        total = jnp.sum(weights, axis=1, keepdims=True) + own_weight
        probs = (weights / total).astype(jnp.bfloat16)
        own_prob = (own_weight / total).astype(jnp.bfloat16).astype(jnp.float32)
        mixed = by_group(
            [
                jnp.dot(
                    probs,
                    values_ref[slot, :, g * HD : (g + 1) * HD],
                    preferred_element_type=jnp.float32,
                )
                for g in range(kv_local)
            ]
        )
        out_ref[order * heads : (order + 1) * heads, :] = mixed + own_prob * own_value


def lay_out(heads, pieces, out_ref, held):
    at = 0
    for piece in pieces:
        held[at : at + piece.shape[0], :] = piece[...]
        at += piece.shape[0]
    for head in range(heads):
        out_ref[:, head * HD : (head + 1) * HD] = held[
            pl.ds(head, out_ref.shape[0], stride=heads), :
        ].astype(jnp.bfloat16)


def attend_last(steps, taking, heads, *refs):
    *ins, early, out_ref, late, held = refs
    attend(steps, taking, *ins, late)
    lay_out(heads, [early, late], out_ref, held)


def make_local(wide):
    steps = steps_of(wide)
    head_steps = [*steps[1:-2], *steps[:1], *steps[-2:]]

    def local(
        queries,
        new_keys,
        new_values,
        key_cache,
        value_cache,
        lengths,
        assignment,
        tokens,
        norm_gain,
        routes,
        route_logits,
        w_gate,
        w_up,
        w_down,
    ):
        rows, width = tokens.shape
        half = width // 2
        units = w_gate.shape[2]
        count = rows * wide
        each = (queries.shape[1] + 2 * new_keys.shape[1]) // HD
        core = lax.axis_index("narrow")
        bf16, f32 = jnp.bfloat16, jnp.float32
        heads_local = queries.shape[1] // HD
        dma = pltpu.SemaphoreType.DMA
        piece_bytes = 2 * half * units

        got = swap(tokens, "wide", wide, steps[0])
        heads_in = [queries, new_keys, new_values]
        row_in = [tokens, norm_gain[None]]
        heads, *row_near = call(
            pack,
            [shape((rows * each, HD), bf16)] + [pltpu.VMEM(a.shape, a.dtype) for a in row_in],
            [distant(a) for a in heads_in + row_in],
            [pltpu.VMEM(a.shape, a.dtype) for a in heads_in]
            + [pltpu.VMEM((rows * each, HD), f32), dma((5,))],
            size=100000,
            far=range(5),
        )
        share = call(
            functools.partial(shares, steps, rows),
            shape((count, HD), f32),
            [distant(routes.T), distant(route_logits.T), heads, distant(w_gate), distant(w_up)],
            [
                pltpu.VMEM(routes.T.shape, jnp.int32),
                pltpu.VMEM(route_logits.T.shape, f32),
                dma((2,)),
            ],
            size=100000,
            far=range(5),
        )
        x = call(
            norm_both,
            shape((2 * rows, half), bf16),
            [near(row_near[0]), got, near(row_near[1]), share, heads],
            size=100000,
            far=(3, 4),
        )

        def grown(heads, step):
            got = swap(heads, "wide", wide, step)
            return call(
                stack, shape((2 * heads.shape[0], HD), bf16), [heads, got], size=4 * heads.size
            )

        for step in steps[1:-2]:
            heads = grown(heads, step)
            x = call(
                stack_after,
                shape((2 * x.shape[0], half), bf16),
                [x, swap(x, "wide", wide, step), heads],
                size=8 * x.size,
                far=(2,),
            )
        line_steps = [steps[-2], steps[-1], steps[-2] ^ steps[-1]]
        last = swap(x, "wide", wide, line_steps[2])
        line = [swap(x, "wide", wide, step) for step in line_steps[:2]]
        wider = max(x.shape[0] * half // HD, heads.shape[0])
        sent_heads = call(widen, shape((wider, HD), bf16), [heads], size=4 * wider * HD)
        far_rows = swap(sent_heads, "wide", wide, steps[0])
        x, heads = call(
            stack_line,
            [shape((count, half), bf16), shape((2 * heads.shape[0], HD), bf16)],
            [x, last, line[0], far_rows, line[1], heads],
            size=8 * count * half,
        )
        got_heads = swap(heads, "wide", wide, steps[-2])

        product = 2 * count * half * units
        other_x = swap(x, "narrow", 2, 1)
        whole = pltpu.VMEM((units, half), bf16)
        hidden, down_own, down_other = call(
            gate_all,
            [shape((count, units), bf16), whole, whole],
            [
                x,
                other_x,
                near(w_gate),
                near(w_up),
                share,
                distant(w_down),
            ],
            [dma((2, CUTS))],
            flops=4 * product,
            size=6 * piece_bytes,
            far=(5,),
        )
        heads = call(
            stack_after,
            shape((2 * heads.shape[0], HD), bf16),
            [heads, got_heads, hidden],
            size=8 * heads.size,
            far=(2,),
        )
        given = call(
            down,
            shape((count, half), bf16),
            [hidden, near(down_other), heads],
            flops=product,
            size=piece_bytes,
            far=(2,),
        )
        taken = swap(given, "narrow", 2, 1)
        far_heads = swap(heads, "wide", wide, steps[-1])
        terms = call(
            down,
            shape((count, half), f32),
            [hidden, near(down_own), given],
            flops=product,
            size=piece_bytes,
            far=(2,),
        )

        caches = [near(key_cache), near(value_cache), lengths, assignment]
        slots = queries.shape[0]
        early_slots = list(range(slots - 1))
        late_slots = list(range(slots - 1, slots))
        quarter = count // 4
        block = shape((quarter, half), bf16)
        terms, *sent = call(
            part_line,
            [shape((quarter, half), f32), block, block, block],
            [terms, taken],
            size=terms.size * 8,
        )
        taken = [swap(part, "wide", wide, step) for part, step in zip(sent, line_steps)]
        taken = [taken[i] for i in (1, 2, 0)]
        early = call(
            functools.partial(attend, head_steps, early_slots),
            shape((len(early_slots) * heads_local, HD), f32),
            [heads, far_heads, *caches, sent[0]],
            flops=2 * key_cache.size * GROUP,
            size=2 * key_cache.size,
            smem=(4, 5),
            far=(6,),
        )
        for step in reversed(steps[:-2]):
            kept = terms.shape[0] // 2
            terms, sent = call(
                combine,
                [shape((kept, half), f32), shape((kept, half), bf16)],
                [terms, *taken, early],
                size=terms.size * 8,
                far=(1 + len(taken),),
            )
            taken = [swap(sent, "wide", wide, step)]
        context = call(
            functools.partial(attend_last, head_steps, late_slots, heads_local),
            shape(queries.shape, bf16),
            [heads, far_heads, *caches, sent, early],
            [
                pltpu.VMEM((len(late_slots) * heads_local, HD), f32),
                pltpu.VMEM((slots * heads_local, HD), f32),
            ],
            flops=2 * key_cache.size * GROUP,
            size=2 * key_cache.size,
            smem=(4, 5),
            far=(6,),
        )
        piece = call(
            finish,
            shape((rows, half), bf16),
            [terms, *taken, tokens, distant(context)],
            size=terms.size * 8,
            far=(3,),
        )
        other = swap(piece, "narrow", 2, 1)
        mixed_out = call(join, shape((rows, width), bf16), [piece, other], size=terms.size * 4)
        return (context, mixed_out)

    return local


def solution(mesh):
    placed = (
        P(("groups", "wide"), "narrow"),
        P(("groups", "wide"), "narrow"),
        P(("groups", "wide"), "narrow"),
        P(("groups", "wide"), None, "narrow"),
        P(("groups", "wide"), None, "narrow"),
        P(("groups", "wide")),
        P(("groups", "wide")),
        P(("groups", "wide"), None),
        P(),
        P("groups", None),
        P("groups", None),
        P("narrow", None, "wide"),
        P("narrow", None, "wide"),
        P("narrow", "wide", None),
    )
    return jax.shard_map(
        make_local(mesh.shape["wide"]),
        mesh=mesh,
        in_specs=placed,
        out_specs=(P(("groups", "wide"), "narrow"), P(("groups", "wide"), None)),
        check_vma=False,
    )
```

```python
import functools
import math

import jax
import jax.numpy as jnp
from jax import lax
from jax.experimental import pallas as pl
from jax.experimental.pallas import tpu as pltpu
from jax.sharding import PartitionSpec as P

HQ = 48
KVH = 8
HD = 128
GROUP = HQ // KVH
SCALE = HD ** (-0.5)
TILE = 512
WIDE_TILE = 1536
CUTS = 4
MIB = 1024 * 1024


def steps_of(wide):
    bits = int(math.log2(wide))
    return [1 << i for i in range(bits - 2)] + [wide >> 1, wide >> 2]


def swap(block, axis, count, step):
    return lax.ppermute(block, axis, [(i, i ^ step) for i in range(count)])


def owner_of(place, me, steps):
    found = me
    for bit, step in enumerate(steps):
        found = found ^ (((place >> bit) & 1) * step)
    return found


def place_of(owner, me, steps):
    differ = owner ^ me
    found = 0
    for bit, step in enumerate(steps):
        shift = int(math.log2(step))
        found = found | (((differ >> shift) & 1) << bit)
    return found


def call(kernel, outs, ins, scratch=(), flops=0, size=0, limit=4, smem=(), far=()):
    spaces = [pltpu.SMEM if i in smem else pl.ANY if i in far else pltpu.VMEM for i in range(len(ins))]
    return pl.pallas_call(
        kernel,
        name=getattr(kernel, "func", kernel).__name__,
        out_shape=outs,
        in_specs=[pl.BlockSpec(memory_space=space) for space in spaces],
        out_specs=jax.tree.map(lambda _: pl.BlockSpec(memory_space=pltpu.VMEM), outs),
        scratch_shapes=list(scratch),
        compiler_params=pltpu.CompilerParams(vmem_limit_bytes=limit * MIB),
        cost_estimate=pl.CostEstimate(flops=flops, bytes_accessed=size, transcendentals=0),
    )(*ins)


def column_copies(source, target, sems, first):
    columns = target.shape[1] // CUTS
    return [
        pltpu.make_async_copy(
            source.at[0, :, pl.ds(pl.multiple_of(first + i * columns, columns), columns)],
            target.at[:, pl.ds(i * columns, columns)],
            sems.at[i],
        )
        for i in range(CUTS)
    ]


def shape(dims, dtype):
    return jax.ShapeDtypeStruct(dims, dtype)


def near(array):
    return pltpu.with_memory_space_constraint(array, pltpu.VMEM)


def distant(array):
    return pltpu.with_memory_space_constraint(array, pltpu.HBM)


def pack(far_query, far_key, far_value, far_tokens, far_gain, heads_ref, *held):
    tokens_ref, gain_ref, *near_refs, packed, sems = held
    far_refs = (far_query, far_key, far_value, far_tokens, far_gain)
    copies = [
        pltpu.make_async_copy(far, ref, sems.at[i])
        for i, (far, ref) in enumerate(zip(far_refs, (*near_refs, tokens_ref, gain_ref)))
    ]
    for copy in copies:
        copy.start()
    for copy in copies:
        copy.wait()
    rows = near_refs[0].shape[0]
    at = 0
    each = heads_ref.shape[0] // rows
    for ref in near_refs:
        block = ref[...].astype(jnp.float32)
        for head in range(ref.shape[1] // HD):
            packed[pl.ds(at, rows, stride=each), :] = block[:, head * HD : (head + 1) * HD]
            at += 1
    heads_ref[...] = packed[...].astype(jnp.bfloat16)


def norm_both(own_ref, got_ref, gain_ref, share, heads, out_ref):
    half = out_ref.shape[1]
    core = lax.axis_index("narrow")
    values = stacked([own_ref, got_ref])
    scale = lax.rsqrt(jnp.mean(values * values, axis=-1, keepdims=True) + 1e-05)
    normed = values * scale * gain_ref[...]
    out_ref[...] = jnp.where(core == 0, normed[:, :half], normed[:, half:]).astype(jnp.bfloat16)


def stacked(refs):
    return jnp.concatenate([ref[...].astype(jnp.float32) for ref in refs], axis=0)


def stack(*refs):
    refs[-1][...] = stacked(refs[:-1]).astype(refs[-1].dtype)


def stack_line(own_ref, last_ref, far_ref, got_heads, next_ref, own_heads, out_ref, heads_ref):
    count = own_heads.shape[0]
    heads_ref[:count, :] = own_heads[...]
    heads_ref[count:, :] = got_heads[:count, :]
    rows = [own_ref, far_ref, next_ref, last_ref]
    out_ref[...] = stacked(rows).astype(jnp.bfloat16)


def widen(own_ref, out_ref):
    count = own_ref.shape[0]
    out_ref[:count, :] = own_ref[...]
    out_ref[count:, :] = jnp.zeros((out_ref.shape[0] - count, HD), out_ref.dtype)


def stack_after(own_ref, got_ref, after, out_ref):
    stack(own_ref, got_ref, out_ref)


def grow_both(own_ref, got_ref, own_heads, got_heads, *refs):
    refs[-2][...] = stacked([own_ref, got_ref]).astype(jnp.bfloat16)
    refs[-1][...] = stacked([own_heads, got_heads]).astype(jnp.bfloat16)


def shares(steps, rows, far_routes, far_logits, *refs):
    *_, out_ref, routes_ref, logits_ref, sems = refs
    copies = [
        pltpu.make_async_copy(far_routes, routes_ref, sems.at[0]),
        pltpu.make_async_copy(far_logits, logits_ref, sems.at[1]),
    ]
    for copy in copies:
        copy.start()
    for copy in copies:
        copy.wait()
    count = out_ref.shape[0]
    core = lax.axis_index("narrow")
    me = lax.axis_index("wide")
    logits = logits_ref[...]
    first = 1.0 / (1.0 + jnp.exp(logits[1:2] - logits[0:1]))
    second = 1.0 - first
    chosen = (routes_ref[...] == core).astype(jnp.float32)
    weight_row = chosen[0:1] * first + chosen[1:2] * second
    row = lax.broadcasted_iota(jnp.int32, (count, count), 0)
    column = lax.broadcasted_iota(jnp.int32, (count, count), 1)
    shift = int(math.log2(rows))
    token = (owner_of(row >> shift, me, steps) << shift) | (row & (rows - 1))
    weight = jnp.sum(jnp.where(token == column, weight_row, 0.0), axis=1, keepdims=True)
    out_ref[...] = jnp.broadcast_to(weight, out_ref.shape)


def gate_all(
    x_ref,
    other_ref,
    gate_ref,
    up_ref,
    share_ref,
    far_down,
    hidden_out,
    down_own,
    down_other,
    sems,
):
    count, depth = x_ref.shape
    core = lax.axis_index("narrow")
    other_copies = column_copies(far_down, down_other, sems.at[0], (1 - core) * depth)
    own_copies = column_copies(far_down, down_own, sems.at[1], core * depth)
    for copy in other_copies + own_copies:
        copy.start()
    tile = min(TILE, gate_ref.shape[2])
    own = pl.ds(pl.multiple_of(core * depth, depth), depth)
    other = pl.ds(pl.multiple_of((1 - core) * depth, depth), depth)

    weight = share_ref[:, 0:1]

    @pl.loop(0, gate_ref.shape[2] // tile)
    def _(i):
        columns = pl.ds(pl.multiple_of(i * tile, tile), tile)
        x, y = x_ref[...], other_ref[...]
        gate = jnp.dot(x, gate_ref[0, own, columns], preferred_element_type=jnp.float32)
        gate += jnp.dot(y, gate_ref[0, other, columns], preferred_element_type=jnp.float32)
        up = jnp.dot(x, up_ref[0, own, columns], preferred_element_type=jnp.float32)
        up += jnp.dot(y, up_ref[0, other, columns], preferred_element_type=jnp.float32)
        hidden_out[:, columns] = (weight * (gate * jax.nn.sigmoid(gate)) * up).astype(jnp.bfloat16)

    for copy in other_copies + own_copies:
        copy.wait()


def down(hidden_ref, down_ref, after, out_ref):
    @pl.loop(0, out_ref.shape[1] // WIDE_TILE)
    def _(i):
        columns = pl.ds(pl.multiple_of(i * WIDE_TILE, WIDE_TILE), WIDE_TILE)
        out_ref[:, columns] = jnp.dot(
            hidden_ref[...], down_ref[:, columns], preferred_element_type=jnp.float32
        ).astype(out_ref.dtype)


def part_line(terms_ref, taken_ref, kept_ref, far_ref, next_ref, last_ref):
    total = terms_ref[...] + taken_ref[...].astype(jnp.float32)
    rows = kept_ref.shape[0]
    kept_ref[...] = total[:rows]
    for i, ref in enumerate((far_ref, next_ref, last_ref)):
        ref[...] = total[(i + 1) * rows : (i + 2) * rows].astype(jnp.bfloat16)


def combine(*refs):
    terms_ref, *taken, after, kept_ref, sent_ref = refs
    total = terms_ref[...]
    for ref in taken:
        total = total + ref[...].astype(jnp.float32)
    kept = kept_ref.shape[0]
    kept_ref[...] = total[:kept].astype(kept_ref.dtype)
    sent_ref[...] = total[kept:].astype(jnp.bfloat16)


def finish(kept_ref, other_kept, other_taken, taken_ref, tokens_ref, after, out_ref):
    half = kept_ref.shape[1]
    first = lax.axis_index("narrow") == 0
    own = kept_ref[...].astype(jnp.float32) + taken_ref[...].astype(jnp.float32)
    other = other_kept[...].astype(jnp.float32) + other_taken[...].astype(jnp.float32)
    tokens = tokens_ref[...].astype(jnp.float32)
    left = tokens[:, :half] + jnp.where(first, own, other)
    right = tokens[:, half:] + jnp.where(first, other, own)
    out_ref[:, :half] = left.astype(jnp.bfloat16)
    out_ref[:, half:] = right.astype(jnp.bfloat16)


def attend(
    steps, taking, near_ref, far_ref, keys_ref, values_ref, lengths_ref, place_ref, after, out_ref
):
    slots, span, width = keys_ref.shape
    rows = slots
    kv_local = width // HD
    heads = kv_local * GROUP
    each = heads + 2 * kv_local
    me = lax.axis_index("wide")
    shift = int(math.log2(rows))
    half = near_ref.shape[0]
    head_of = lax.broadcasted_iota(jnp.int32, (heads, 1), 0)
    positions = lax.broadcasted_iota(jnp.int32, (heads, span), 1)

    def by_group(pieces):
        result = pieces[0]
        for g in range(1, kv_local):
            result = jnp.where(head_of >= g * GROUP, pieces[g], result)
        return result

    for order, slot in enumerate(taking):
        request = place_ref[slot]
        at = (place_of(request >> shift, me, steps) << shift) | (request & (rows - 1))
        at = at * each
        inside = pl.ds(pl.multiple_of(jnp.where(at < half, at, at - half), each), each)
        block = jnp.where(at < half, near_ref[inside, :], far_ref[inside, :])
        query = block[:heads]
        own = block[heads:].astype(jnp.float32)
        own_key = by_group([own[g : g + 1] for g in range(kv_local)])
        own_value = by_group([own[kv_local + g : kv_local + g + 1] for g in range(kv_local)])
        own_score = jnp.sum(query.astype(jnp.float32) * own_key, axis=1, keepdims=True) * SCALE
        scores = by_group(
            [
                lax.dot_general(
                    query,
                    keys_ref[slot, :, g * HD : (g + 1) * HD],
                    (((1,), (1,)), ((), ())),
                    preferred_element_type=jnp.float32,
                )
                for g in range(kv_local)
            ]
        )
        scores = jnp.where(positions < lengths_ref[slot], scores * SCALE, -jnp.inf)
        row_max = jnp.maximum(jnp.max(scores, axis=1, keepdims=True), own_score)
        weights = jnp.exp(scores - row_max)
        own_weight = jnp.exp(own_score - row_max)
        total = jnp.sum(weights, axis=1, keepdims=True) + own_weight
        probs = (weights / total).astype(jnp.bfloat16)
        own_prob = (own_weight / total).astype(jnp.bfloat16).astype(jnp.float32)
        mixed = by_group(
            [
                jnp.dot(
                    probs,
                    values_ref[slot, :, g * HD : (g + 1) * HD],
                    preferred_element_type=jnp.float32,
                )
                for g in range(kv_local)
            ]
        )
        out_ref[order * heads : (order + 1) * heads, :] = mixed + own_prob * own_value


def lay_out(heads, pieces, out_ref, held):
    at = 0
    for piece in pieces:
        held[at : at + piece.shape[0], :] = piece[...]
        at += piece.shape[0]
    for head in range(heads):
        out_ref[:, head * HD : (head + 1) * HD] = held[
            pl.ds(head, out_ref.shape[0], stride=heads), :
        ].astype(jnp.bfloat16)


def attend_last(steps, taking, heads, *refs):
    *ins, early, out_ref, late, held = refs
    attend(steps, taking, *ins, late)
    lay_out(heads, [early, late], out_ref, held)


def make_local(wide):
    steps = steps_of(wide)
    head_steps = [*steps[1:-2], *steps[:1], *steps[-2:]]

    def local(
        queries,
        new_keys,
        new_values,
        key_cache,
        value_cache,
        lengths,
        assignment,
        tokens,
        norm_gain,
        routes,
        route_logits,
        w_gate,
        w_up,
        w_down,
    ):
        rows, width = tokens.shape
        half = width // 2
        units = w_gate.shape[2]
        count = rows * wide
        each = (queries.shape[1] + 2 * new_keys.shape[1]) // HD
        core = lax.axis_index("narrow")
        bf16, f32 = jnp.bfloat16, jnp.float32
        heads_local = queries.shape[1] // HD
        dma = pltpu.SemaphoreType.DMA
        piece_bytes = 2 * half * units

        got = swap(tokens, "wide", wide, steps[0])
        heads_in = [queries, new_keys, new_values]
        row_in = [tokens, norm_gain[None]]
        heads, *row_near = call(
            pack,
            [shape((rows * each, HD), bf16)] + [pltpu.VMEM(a.shape, a.dtype) for a in row_in],
            [distant(a) for a in heads_in + row_in],
            [pltpu.VMEM(a.shape, a.dtype) for a in heads_in]
            + [pltpu.VMEM((rows * each, HD), f32), dma((5,))],
            size=100000,
            far=range(5),
        )
        share = call(
            functools.partial(shares, steps, rows),
            shape((count, HD), f32),
            [distant(routes.T), distant(route_logits.T), heads, distant(w_gate), distant(w_up)],
            [
                pltpu.VMEM(routes.T.shape, jnp.int32),
                pltpu.VMEM(route_logits.T.shape, f32),
                dma((2,)),
            ],
            size=100000,
            far=range(5),
        )
        x = call(
            norm_both,
            shape((2 * rows, half), bf16),
            [near(row_near[0]), got, near(row_near[1]), share, heads],
            size=100000,
            far=(3, 4),
        )

        def grown(heads, step):
            got = swap(heads, "wide", wide, step)
            return call(
                stack, shape((2 * heads.shape[0], HD), bf16), [heads, got], size=4 * heads.size
            )

        for step in steps[1:-2]:
            heads = grown(heads, step)
            x = call(
                stack_after,
                shape((2 * x.shape[0], half), bf16),
                [x, swap(x, "wide", wide, step), heads],
                size=8 * x.size,
                far=(2,),
            )
        line_steps = [steps[-2], steps[-1], steps[-2] ^ steps[-1]]
        last = swap(x, "wide", wide, line_steps[2])
        line = [swap(x, "wide", wide, step) for step in line_steps[:2]]
        wider = max(x.shape[0] * half // HD, heads.shape[0])
        sent_heads = call(widen, shape((wider, HD), bf16), [heads], size=4 * wider * HD)
        far_rows = swap(sent_heads, "wide", wide, steps[0])
        x, heads = call(
            stack_line,
            [shape((count, half), bf16), shape((2 * heads.shape[0], HD), bf16)],
            [x, last, line[0], far_rows, line[1], heads],
            size=8 * count * half,
        )
        got_heads = swap(heads, "wide", wide, steps[-2])

        product = 2 * count * half * units
        other_x = swap(x, "narrow", 2, 1)
        whole = pltpu.VMEM((units, half), bf16)
        hidden, down_own, down_other = call(
            gate_all,
            [shape((count, units), bf16), whole, whole],
            [
                x,
                other_x,
                near(w_gate),
                near(w_up),
                share,
                distant(w_down),
            ],
            [dma((2, CUTS))],
            flops=4 * product,
            size=6 * piece_bytes,
            far=(5,),
        )
        heads = call(
            stack_after,
            shape((2 * heads.shape[0], HD), bf16),
            [heads, got_heads, hidden],
            size=8 * heads.size,
            far=(2,),
        )
        given = call(
            down,
            shape((count, half), bf16),
            [hidden, near(down_other), heads],
            flops=product,
            size=piece_bytes,
            far=(2,),
        )
        taken = swap(given, "narrow", 2, 1)
        far_heads = swap(heads, "wide", wide, steps[-1])
        terms = call(
            down,
            shape((count, half), f32),
            [hidden, near(down_own), given],
            flops=product,
            size=piece_bytes,
            far=(2,),
        )

        caches = [near(key_cache), near(value_cache), lengths, assignment]
        slots = queries.shape[0]
        early_slots = list(range(slots - 1))
        late_slots = list(range(slots - 1, slots))
        quarter = count // 4
        block = shape((quarter, half), bf16)
        terms, *sent = call(
            part_line,
            [shape((quarter, half), f32), block, block, block],
            [terms, taken],
            size=terms.size * 8,
        )
        taken = [swap(part, "wide", wide, step) for part, step in zip(sent, line_steps)]
        taken = [taken[i] for i in (1, 2, 0)]
        early = call(
            functools.partial(attend, head_steps, early_slots),
            shape((len(early_slots) * heads_local, HD), f32),
            [heads, far_heads, *caches, sent[0]],
            flops=2 * key_cache.size * GROUP,
            size=2 * key_cache.size,
            smem=(4, 5),
            far=(6,),
        )
        for step in reversed(steps[:-2]):
            kept = terms.shape[0] // 2
            terms, sent = call(
                combine,
                [shape((kept, half), bf16 if kept == rows else f32), shape((kept, half), bf16)],
                [terms, *taken, early],
                size=terms.size * 8,
                far=(1 + len(taken),),
            )
            taken = [swap(sent, "wide", wide, step)]
        context = call(
            functools.partial(attend_last, head_steps, late_slots, heads_local),
            shape(queries.shape, bf16),
            [heads, far_heads, *caches, sent, early],
            [
                pltpu.VMEM((len(late_slots) * heads_local, HD), f32),
                pltpu.VMEM((slots * heads_local, HD), f32),
            ],
            flops=2 * key_cache.size * GROUP,
            size=2 * key_cache.size,
            smem=(4, 5),
            far=(6,),
        )
        other_kept = swap(terms, "narrow", 2, 1)
        crossed = [(i, (((i >> 1) ^ steps[0]) << 1) | (1 - (i & 1))) for i in range(2 * wide)]
        other_taken = lax.ppermute(sent, ("wide", "narrow"), crossed)
        mixed_out = call(
            finish,
            shape((rows, width), bf16),
            [terms, other_kept, other_taken, *taken, tokens, distant(context)],
            size=terms.size * 8,
            far=(5,),
        )
        return (context, mixed_out)

    return local


def solution(mesh):
    placed = (
        P(("groups", "wide"), "narrow"),
        P(("groups", "wide"), "narrow"),
        P(("groups", "wide"), "narrow"),
        P(("groups", "wide"), None, "narrow"),
        P(("groups", "wide"), None, "narrow"),
        P(("groups", "wide")),
        P(("groups", "wide")),
        P(("groups", "wide"), None),
        P(),
        P("groups", None),
        P("groups", None),
        P("narrow", None, "wide"),
        P("narrow", None, "wide"),
        P("narrow", "wide", None),
    )
    return jax.shard_map(
        make_local(mesh.shape["wide"]),
        mesh=mesh,
        in_specs=placed,
        out_specs=(P(("groups", "wide"), "narrow"), P(("groups", "wide"), None)),
        check_vma=False,
    )
```

```python
import functools
import math

import jax
import jax.numpy as jnp
from jax import lax
from jax.experimental import pallas as pl
from jax.experimental.pallas import tpu as pltpu
from jax.sharding import PartitionSpec as P

HQ = 48
KVH = 8
HD = 128
GROUP = HQ // KVH
SCALE = HD ** (-0.5)
TILE = 512
WIDE_TILE = 1536
CUTS = 4
MIB = 1024 * 1024


def steps_of(wide):
    bits = int(math.log2(wide))
    return [1 << i for i in range(bits - 2)] + [wide >> 1, wide >> 2]


def swap(block, axis, count, step):
    return lax.ppermute(block, axis, [(i, i ^ step) for i in range(count)])


def owner_of(place, me, steps):
    found = me
    for bit, step in enumerate(steps):
        found = found ^ (((place >> bit) & 1) * step)
    return found


def place_of(owner, me, steps):
    differ = owner ^ me
    found = 0
    for bit, step in enumerate(steps):
        shift = int(math.log2(step))
        found = found | (((differ >> shift) & 1) << bit)
    return found


def call(kernel, outs, ins, scratch=(), flops=0, size=0, limit=4, smem=(), far=()):
    spaces = [pltpu.SMEM if i in smem else pl.ANY if i in far else pltpu.VMEM for i in range(len(ins))]
    return pl.pallas_call(
        kernel,
        name=getattr(kernel, "func", kernel).__name__,
        out_shape=outs,
        in_specs=[pl.BlockSpec(memory_space=space) for space in spaces],
        out_specs=jax.tree.map(lambda _: pl.BlockSpec(memory_space=pltpu.VMEM), outs),
        scratch_shapes=list(scratch),
        compiler_params=pltpu.CompilerParams(vmem_limit_bytes=limit * MIB),
        cost_estimate=pl.CostEstimate(flops=flops, bytes_accessed=size, transcendentals=0),
    )(*ins)


def column_copies(source, target, sems, first):
    columns = target.shape[1] // CUTS
    return [
        pltpu.make_async_copy(
            source.at[0, :, pl.ds(pl.multiple_of(first + i * columns, columns), columns)],
            target.at[:, pl.ds(i * columns, columns)],
            sems.at[i],
        )
        for i in range(CUTS)
    ]


def shape(dims, dtype):
    return jax.ShapeDtypeStruct(dims, dtype)


def near(array):
    return pltpu.with_memory_space_constraint(array, pltpu.VMEM)


def distant(array):
    return pltpu.with_memory_space_constraint(array, pltpu.HBM)


def pack(far_query, far_key, far_value, far_tokens, far_gain, heads_ref, *held):
    tokens_ref, gain_ref, *near_refs, packed, sems = held
    far_refs = (far_query, far_key, far_value, far_tokens, far_gain)
    copies = [
        pltpu.make_async_copy(far, ref, sems.at[i])
        for i, (far, ref) in enumerate(zip(far_refs, (*near_refs, tokens_ref, gain_ref)))
    ]
    for copy in copies:
        copy.start()
    for copy in copies:
        copy.wait()
    rows = near_refs[0].shape[0]
    at = 0
    each = heads_ref.shape[0] // rows
    for ref in near_refs:
        block = ref[...].astype(jnp.float32)
        for head in range(ref.shape[1] // HD):
            packed[pl.ds(at, rows, stride=each), :] = block[:, head * HD : (head + 1) * HD]
            at += 1
    heads_ref[...] = packed[...].astype(jnp.bfloat16)


def norm_both(own_ref, got_ref, gain_ref, share, heads, out_ref):
    half = out_ref.shape[1]
    core = lax.axis_index("narrow")
    values = stacked([own_ref, got_ref])
    scale = lax.rsqrt(jnp.mean(values * values, axis=-1, keepdims=True) + 1e-05)
    normed = values * scale * gain_ref[...]
    out_ref[...] = jnp.where(core == 0, normed[:, :half], normed[:, half:]).astype(jnp.bfloat16)


def stacked(refs):
    return jnp.concatenate([ref[...].astype(jnp.float32) for ref in refs], axis=0)


def stack(*refs):
    refs[-1][...] = stacked(refs[:-1]).astype(refs[-1].dtype)


def stack_line(own_ref, last_ref, far_ref, got_heads, next_ref, own_heads, out_ref, heads_ref):
    count = own_heads.shape[0]
    heads_ref[:count, :] = own_heads[...]
    heads_ref[count:, :] = got_heads[:count, :]
    rows = [own_ref, far_ref, next_ref, last_ref]
    out_ref[...] = stacked(rows).astype(jnp.bfloat16)


def widen(own_ref, out_ref):
    count = own_ref.shape[0]
    out_ref[:count, :] = own_ref[...]
    out_ref[count:, :] = jnp.zeros((out_ref.shape[0] - count, HD), out_ref.dtype)


def stack_after(own_ref, got_ref, after, out_ref):
    stack(own_ref, got_ref, out_ref)


def grow_both(own_ref, got_ref, own_heads, got_heads, *refs):
    refs[-2][...] = stacked([own_ref, got_ref]).astype(jnp.bfloat16)
    refs[-1][...] = stacked([own_heads, got_heads]).astype(jnp.bfloat16)


def shares(steps, rows, far_routes, far_logits, *refs):
    *_, out_ref, routes_ref, logits_ref, sems = refs
    copies = [
        pltpu.make_async_copy(far_routes, routes_ref, sems.at[0]),
        pltpu.make_async_copy(far_logits, logits_ref, sems.at[1]),
    ]
    for copy in copies:
        copy.start()
    for copy in copies:
        copy.wait()
    count = out_ref.shape[0]
    core = lax.axis_index("narrow")
    me = lax.axis_index("wide")
    logits = logits_ref[...]
    first = 1.0 / (1.0 + jnp.exp(logits[1:2] - logits[0:1]))
    second = 1.0 - first
    chosen = (routes_ref[...] == core).astype(jnp.float32)
    weight_row = chosen[0:1] * first + chosen[1:2] * second
    row = lax.broadcasted_iota(jnp.int32, (count, count), 0)
    column = lax.broadcasted_iota(jnp.int32, (count, count), 1)
    shift = int(math.log2(rows))
    token = (owner_of(row >> shift, me, steps) << shift) | (row & (rows - 1))
    weight = jnp.sum(jnp.where(token == column, weight_row, 0.0), axis=1, keepdims=True)
    out_ref[...] = jnp.broadcast_to(weight, out_ref.shape)


def gate_all(
    x_ref,
    other_ref,
    gate_ref,
    up_ref,
    share_ref,
    far_down,
    hidden_out,
    down_own,
    down_other,
    sems,
):
    count, depth = x_ref.shape
    core = lax.axis_index("narrow")
    other_copies = column_copies(far_down, down_other, sems.at[0], (1 - core) * depth)
    own_copies = column_copies(far_down, down_own, sems.at[1], core * depth)
    for copy in other_copies + own_copies:
        copy.start()
    tile = min(TILE, gate_ref.shape[2])
    own = pl.ds(pl.multiple_of(core * depth, depth), depth)
    other = pl.ds(pl.multiple_of((1 - core) * depth, depth), depth)

    weight = share_ref[:, 0:1]

    @pl.loop(0, gate_ref.shape[2] // tile)
    def _(i):
        columns = pl.ds(pl.multiple_of(i * tile, tile), tile)
        x, y = x_ref[...], other_ref[...]
        gate = jnp.dot(x, gate_ref[0, own, columns], preferred_element_type=jnp.float32)
        gate += jnp.dot(y, gate_ref[0, other, columns], preferred_element_type=jnp.float32)
        up = jnp.dot(x, up_ref[0, own, columns], preferred_element_type=jnp.float32)
        up += jnp.dot(y, up_ref[0, other, columns], preferred_element_type=jnp.float32)
        hidden_out[:, columns] = (weight * (gate * jax.nn.sigmoid(gate)) * up).astype(jnp.bfloat16)

    for copy in other_copies + own_copies:
        copy.wait()


def down(hidden_ref, down_ref, after, out_ref):
    @pl.loop(0, out_ref.shape[1] // WIDE_TILE)
    def _(i):
        columns = pl.ds(pl.multiple_of(i * WIDE_TILE, WIDE_TILE), WIDE_TILE)
        out_ref[:, columns] = jnp.dot(
            hidden_ref[...], down_ref[:, columns], preferred_element_type=jnp.float32
        ).astype(out_ref.dtype)


def part_line(terms_ref, taken_ref, kept_ref, far_ref, next_ref, last_ref):
    total = terms_ref[...] + taken_ref[...].astype(jnp.float32)
    rows = kept_ref.shape[0]
    kept_ref[...] = total[:rows]
    for i, ref in enumerate((far_ref, next_ref, last_ref)):
        ref[...] = total[(i + 1) * rows : (i + 2) * rows].astype(jnp.bfloat16)


def combine(*refs):
    terms_ref, *taken, after, kept_ref, sent_ref = refs
    total = terms_ref[...]
    for ref in taken:
        total = total + ref[...].astype(jnp.float32)
    kept = kept_ref.shape[0]
    kept_ref[...] = total[:kept].astype(kept_ref.dtype)
    sent_ref[...] = total[kept:].astype(jnp.bfloat16)


def finish(kept_ref, taken_ref, other_kept, other_taken, tokens_ref, after, out_ref):
    half = kept_ref.shape[1]
    first = lax.axis_index("narrow") == 0
    own = kept_ref[...].astype(jnp.float32) + taken_ref[...].astype(jnp.float32)
    other = other_kept[...].astype(jnp.float32) + other_taken[...].astype(jnp.float32)
    tokens = tokens_ref[...].astype(jnp.float32)
    left = tokens[:, :half] + jnp.where(first, own, other)
    right = tokens[:, half:] + jnp.where(first, other, own)
    out_ref[:, :half] = left.astype(jnp.bfloat16)
    out_ref[:, half:] = right.astype(jnp.bfloat16)


def attend(
    steps, taking, near_ref, far_ref, keys_ref, values_ref, lengths_ref, place_ref, after, out_ref
):
    slots, span, width = keys_ref.shape
    rows = slots
    kv_local = width // HD
    heads = kv_local * GROUP
    each = heads + 2 * kv_local
    me = lax.axis_index("wide")
    shift = int(math.log2(rows))
    half = near_ref.shape[0]
    head_of = lax.broadcasted_iota(jnp.int32, (heads, 1), 0)
    positions = lax.broadcasted_iota(jnp.int32, (heads, span), 1)

    def by_group(pieces):
        result = pieces[0]
        for g in range(1, kv_local):
            result = jnp.where(head_of >= g * GROUP, pieces[g], result)
        return result

    for order, slot in enumerate(taking):
        request = place_ref[slot]
        at = (place_of(request >> shift, me, steps) << shift) | (request & (rows - 1))
        at = at * each
        inside = pl.ds(pl.multiple_of(jnp.where(at < half, at, at - half), each), each)
        block = jnp.where(at < half, near_ref[inside, :], far_ref[inside, :])
        query = block[:heads]
        own = block[heads:].astype(jnp.float32)
        own_key = by_group([own[g : g + 1] for g in range(kv_local)])
        own_value = by_group([own[kv_local + g : kv_local + g + 1] for g in range(kv_local)])
        own_score = jnp.sum(query.astype(jnp.float32) * own_key, axis=1, keepdims=True) * SCALE
        scores = by_group(
            [
                lax.dot_general(
                    query,
                    keys_ref[slot, :, g * HD : (g + 1) * HD],
                    (((1,), (1,)), ((), ())),
                    preferred_element_type=jnp.float32,
                )
                for g in range(kv_local)
            ]
        )
        scores = jnp.where(positions < lengths_ref[slot], scores * SCALE, -jnp.inf)
        row_max = jnp.maximum(jnp.max(scores, axis=1, keepdims=True), own_score)
        weights = jnp.exp(scores - row_max)
        own_weight = jnp.exp(own_score - row_max)
        total = jnp.sum(weights, axis=1, keepdims=True) + own_weight
        probs = (weights / total).astype(jnp.bfloat16)
        own_prob = (own_weight / total).astype(jnp.bfloat16).astype(jnp.float32)
        mixed = by_group(
            [
                jnp.dot(
                    probs,
                    values_ref[slot, :, g * HD : (g + 1) * HD],
                    preferred_element_type=jnp.float32,
                )
                for g in range(kv_local)
            ]
        )
        out_ref[order * heads : (order + 1) * heads, :] = mixed + own_prob * own_value


def lay_out(heads, pieces, out_ref, held):
    at = 0
    for piece in pieces:
        held[at : at + piece.shape[0], :] = piece[...]
        at += piece.shape[0]
    for head in range(heads):
        out_ref[:, head * HD : (head + 1) * HD] = held[
            pl.ds(head, out_ref.shape[0], stride=heads), :
        ].astype(jnp.bfloat16)


def attend_last(steps, taking, heads, *refs):
    *ins, early, out_ref, late, held = refs
    attend(steps, taking, *ins, late)
    lay_out(heads, [early, late], out_ref, held)


def make_local(wide):
    steps = steps_of(wide)
    head_steps = [*steps[1:-2], *steps[:1], *steps[-2:]]

    def local(
        queries,
        new_keys,
        new_values,
        key_cache,
        value_cache,
        lengths,
        assignment,
        tokens,
        norm_gain,
        routes,
        route_logits,
        w_gate,
        w_up,
        w_down,
    ):
        rows, width = tokens.shape
        half = width // 2
        units = w_gate.shape[2]
        count = rows * wide
        each = (queries.shape[1] + 2 * new_keys.shape[1]) // HD
        core = lax.axis_index("narrow")
        bf16, f32 = jnp.bfloat16, jnp.float32
        heads_local = queries.shape[1] // HD
        dma = pltpu.SemaphoreType.DMA
        piece_bytes = 2 * half * units

        got = swap(tokens, "wide", wide, steps[0])
        heads_in = [queries, new_keys, new_values]
        row_in = [tokens, norm_gain[None]]
        heads, *row_near = call(
            pack,
            [shape((rows * each, HD), bf16)] + [pltpu.VMEM(a.shape, a.dtype) for a in row_in],
            [distant(a) for a in heads_in + row_in],
            [pltpu.VMEM(a.shape, a.dtype) for a in heads_in]
            + [pltpu.VMEM((rows * each, HD), f32), dma((5,))],
            size=100000,
            far=range(5),
        )
        share = call(
            functools.partial(shares, steps, rows),
            shape((count, HD), f32),
            [distant(routes.T), distant(route_logits.T), heads, distant(w_gate), distant(w_up)],
            [
                pltpu.VMEM(routes.T.shape, jnp.int32),
                pltpu.VMEM(route_logits.T.shape, f32),
                dma((2,)),
            ],
            size=100000,
            far=range(5),
        )
        x = call(
            norm_both,
            shape((2 * rows, half), bf16),
            [near(row_near[0]), got, near(row_near[1]), share, heads],
            size=100000,
            far=(3, 4),
        )

        def grown(heads, step):
            got = swap(heads, "wide", wide, step)
            return call(
                stack, shape((2 * heads.shape[0], HD), bf16), [heads, got], size=4 * heads.size
            )

        for step in steps[1:-2]:
            heads = grown(heads, step)
            x = call(
                stack_after,
                shape((2 * x.shape[0], half), bf16),
                [x, swap(x, "wide", wide, step), heads],
                size=8 * x.size,
                far=(2,),
            )
        line_steps = [steps[-2], steps[-1], steps[-2] ^ steps[-1]]
        last = swap(x, "wide", wide, line_steps[2])
        line = [swap(x, "wide", wide, step) for step in line_steps[:2]]
        wider = max(x.shape[0] * half // HD, heads.shape[0])
        sent_heads = call(widen, shape((wider, HD), bf16), [heads], size=4 * wider * HD)
        far_rows = swap(sent_heads, "wide", wide, steps[0])
        x, heads = call(
            stack_line,
            [shape((count, half), bf16), shape((2 * heads.shape[0], HD), bf16)],
            [x, last, line[0], far_rows, line[1], heads],
            size=8 * count * half,
        )
        got_heads = swap(heads, "wide", wide, steps[-2])

        product = 2 * count * half * units
        other_x = swap(x, "narrow", 2, 1)
        whole = pltpu.VMEM((units, half), bf16)
        hidden, down_own, down_other = call(
            gate_all,
            [shape((count, units), bf16), whole, whole],
            [
                x,
                other_x,
                near(w_gate),
                near(w_up),
                share,
                distant(w_down),
            ],
            [dma((2, CUTS))],
            flops=4 * product,
            size=6 * piece_bytes,
            far=(5,),
        )
        heads = call(
            stack_after,
            shape((2 * heads.shape[0], HD), bf16),
            [heads, got_heads, hidden],
            size=8 * heads.size,
            far=(2,),
        )
        given = call(
            down,
            shape((count, half), bf16),
            [hidden, near(down_other), heads],
            flops=product,
            size=piece_bytes,
            far=(2,),
        )
        taken = swap(given, "narrow", 2, 1)
        far_heads = swap(heads, "wide", wide, steps[-1])
        terms = call(
            down,
            shape((count, half), f32),
            [hidden, near(down_own), given],
            flops=product,
            size=piece_bytes,
            far=(2,),
        )

        caches = [near(key_cache), near(value_cache), lengths, assignment]
        slots = queries.shape[0]
        early_slots = list(range(slots - 1))
        late_slots = list(range(slots - 1, slots))
        quarter = count // 4
        block = shape((quarter, half), bf16)
        terms, *sent = call(
            part_line,
            [shape((quarter, half), f32), block, block, block],
            [terms, taken],
            size=terms.size * 8,
        )
        taken = [swap(part, "wide", wide, step) for part, step in zip(sent, line_steps)]
        taken = [taken[i] for i in (1, 2, 0)]
        early = call(
            functools.partial(attend, head_steps, early_slots),
            shape((len(early_slots) * heads_local, HD), f32),
            [heads, far_heads, *caches, sent[0]],
            flops=2 * key_cache.size * GROUP,
            size=2 * key_cache.size,
            smem=(4, 5),
            far=(6,),
        )
        for step in reversed(steps[:-2]):
            kept = terms.shape[0] // 2
            terms, sent = call(
                combine,
                [shape((kept, half), bf16 if kept == rows else f32), shape((kept, half), bf16)],
                [terms, *taken, early],
                size=terms.size * 8,
                far=(1 + len(taken),),
            )
            taken = [swap(sent, "wide", wide, step)]
        context = call(
            functools.partial(attend_last, head_steps, late_slots, heads_local),
            shape(queries.shape, bf16),
            [heads, far_heads, *caches, sent, early],
            [
                pltpu.VMEM((len(late_slots) * heads_local, HD), f32),
                pltpu.VMEM((slots * heads_local, HD), f32),
            ],
            flops=2 * key_cache.size * GROUP,
            size=2 * key_cache.size,
            smem=(4, 5),
            far=(6,),
        )
        other_kept = swap(terms, "narrow", 2, 1)
        crossed = [(i, (((i >> 1) ^ steps[0]) << 1) | (1 - (i & 1))) for i in range(2 * wide)]
        other_taken = lax.ppermute(sent, ("wide", "narrow"), crossed)
        mixed_out = call(
            finish,
            shape((rows, width), bf16),
            [terms, *taken, other_kept, other_taken, tokens, distant(context)],
            size=terms.size * 8,
            far=(5,),
        )
        return (context, mixed_out)

    return local


def solution(mesh):
    placed = (
        P(("groups", "wide"), "narrow"),
        P(("groups", "wide"), "narrow"),
        P(("groups", "wide"), "narrow"),
        P(("groups", "wide"), None, "narrow"),
        P(("groups", "wide"), None, "narrow"),
        P(("groups", "wide")),
        P(("groups", "wide")),
        P(("groups", "wide"), None),
        P(),
        P("groups", None),
        P("groups", None),
        P("narrow", None, "wide"),
        P("narrow", None, "wide"),
        P("narrow", "wide", None),
    )
    return jax.shard_map(
        make_local(mesh.shape["wide"]),
        mesh=mesh,
        in_specs=placed,
        out_specs=(P(("groups", "wide"), "narrow"), P(("groups", "wide"), None)),
        check_vma=False,
    )
```

```python
import functools
import math

import jax
import jax.numpy as jnp
from jax import lax
from jax.experimental import pallas as pl
from jax.experimental.pallas import tpu as pltpu
from jax.sharding import PartitionSpec as P

HQ = 48
KVH = 8
HD = 128
GROUP = HQ // KVH
SCALE = HD ** (-0.5)
TILE = 512
WIDE_TILE = 1536
CUTS = 4
MIB = 1024 * 1024


def steps_of(wide):
    bits = int(math.log2(wide))
    return [1 << i for i in range(bits - 2)] + [wide >> 1, wide >> 2]


def swap(block, axis, count, step):
    return lax.ppermute(block, axis, [(i, i ^ step) for i in range(count)])


def cross(block, wide, step):
    pairs = [(2 * i + c, 2 * (i ^ step) + 1 - c) for i in range(wide) for c in range(2)]
    return lax.ppermute(block, ("wide", "narrow"), pairs)


def side_of(flip):
    bit = (lax.axis_index("wide") // flip) % 2
    return lax.axis_index("narrow") ^ bit


def owner_of(place, me, steps):
    found = me
    for bit, step in enumerate(steps):
        found = found ^ (((place >> bit) & 1) * step)
    return found


def place_of(owner, me, steps):
    differ = owner ^ me
    found = 0
    for bit, step in enumerate(steps):
        shift = int(math.log2(step))
        found = found | (((differ >> shift) & 1) << bit)
    return found


def call(kernel, outs, ins, scratch=(), flops=0, size=0, limit=4, smem=(), far=()):
    spaces = [pltpu.SMEM if i in smem else pl.ANY if i in far else pltpu.VMEM for i in range(len(ins))]
    return pl.pallas_call(
        kernel,
        name=getattr(kernel, "func", kernel).__name__,
        out_shape=outs,
        in_specs=[pl.BlockSpec(memory_space=space) for space in spaces],
        out_specs=jax.tree.map(lambda _: pl.BlockSpec(memory_space=pltpu.VMEM), outs),
        scratch_shapes=list(scratch),
        compiler_params=pltpu.CompilerParams(vmem_limit_bytes=limit * MIB),
        cost_estimate=pl.CostEstimate(flops=flops, bytes_accessed=size, transcendentals=0),
    )(*ins)


def column_copies(source, target, sems, first):
    columns = target.shape[1] // CUTS
    return [
        pltpu.make_async_copy(
            source.at[0, :, pl.ds(pl.multiple_of(first + i * columns, columns), columns)],
            target.at[:, pl.ds(i * columns, columns)],
            sems.at[i],
        )
        for i in range(CUTS)
    ]


def shape(dims, dtype):
    return jax.ShapeDtypeStruct(dims, dtype)


def near(array):
    return pltpu.with_memory_space_constraint(array, pltpu.VMEM)


def distant(array):
    return pltpu.with_memory_space_constraint(array, pltpu.HBM)


def pack(far_query, far_key, far_value, far_tokens, far_gain, heads_ref, *held):
    tokens_ref, gain_ref, *near_refs, packed, sems = held
    far_refs = (far_query, far_key, far_value, far_tokens, far_gain)
    copies = [
        pltpu.make_async_copy(far, ref, sems.at[i])
        for i, (far, ref) in enumerate(zip(far_refs, (*near_refs, tokens_ref, gain_ref)))
    ]
    for copy in copies:
        copy.start()
    for copy in copies:
        copy.wait()
    rows = near_refs[0].shape[0]
    at = 0
    each = heads_ref.shape[0] // rows
    for ref in near_refs:
        block = ref[...].astype(jnp.float32)
        for head in range(ref.shape[1] // HD):
            packed[pl.ds(at, rows, stride=each), :] = block[:, head * HD : (head + 1) * HD]
            at += 1
    heads_ref[...] = packed[...].astype(jnp.bfloat16)


def norm_both(flip, own_ref, got_ref, gain_ref, share, heads, out_ref):
    half = out_ref.shape[1]
    values = stacked([own_ref, got_ref])
    scale = lax.rsqrt(jnp.mean(values * values, axis=-1, keepdims=True) + 1e-05)
    normed = values * scale * gain_ref[...]
    out_ref[...] = jnp.where(side_of(flip) == 0, normed[:, :half], normed[:, half:]).astype(jnp.bfloat16)


def stacked(refs):
    return jnp.concatenate([ref[...].astype(jnp.float32) for ref in refs], axis=0)


def stack(*refs):
    refs[-1][...] = stacked(refs[:-1]).astype(refs[-1].dtype)


def stack_line(own_ref, last_ref, far_ref, got_heads, next_ref, own_heads, out_ref, heads_ref):
    count = own_heads.shape[0]
    heads_ref[:count, :] = own_heads[...]
    heads_ref[count:, :] = got_heads[:count, :]
    rows = [own_ref, far_ref, next_ref, last_ref]
    out_ref[...] = stacked(rows).astype(jnp.bfloat16)


def widen(own_ref, out_ref):
    count = own_ref.shape[0]
    out_ref[:count, :] = own_ref[...]
    out_ref[count:, :] = jnp.zeros((out_ref.shape[0] - count, HD), out_ref.dtype)


def stack_after(own_ref, got_ref, after, out_ref):
    stack(own_ref, got_ref, out_ref)


def grow_both(own_ref, got_ref, own_heads, got_heads, *refs):
    refs[-2][...] = stacked([own_ref, got_ref]).astype(jnp.bfloat16)
    refs[-1][...] = stacked([own_heads, got_heads]).astype(jnp.bfloat16)


def shares(steps, rows, far_routes, far_logits, *refs):
    *_, out_ref, routes_ref, logits_ref, sems = refs
    copies = [
        pltpu.make_async_copy(far_routes, routes_ref, sems.at[0]),
        pltpu.make_async_copy(far_logits, logits_ref, sems.at[1]),
    ]
    for copy in copies:
        copy.start()
    for copy in copies:
        copy.wait()
    count = out_ref.shape[0]
    core = lax.axis_index("narrow")
    me = lax.axis_index("wide")
    logits = logits_ref[...]
    first = 1.0 / (1.0 + jnp.exp(logits[1:2] - logits[0:1]))
    second = 1.0 - first
    chosen = (routes_ref[...] == core).astype(jnp.float32)
    weight_row = chosen[0:1] * first + chosen[1:2] * second
    row = lax.broadcasted_iota(jnp.int32, (count, count), 0)
    column = lax.broadcasted_iota(jnp.int32, (count, count), 1)
    shift = int(math.log2(rows))
    token = (owner_of(row >> shift, me, steps) << shift) | (row & (rows - 1))
    weight = jnp.sum(jnp.where(token == column, weight_row, 0.0), axis=1, keepdims=True)
    out_ref[...] = jnp.broadcast_to(weight, out_ref.shape)


def gate_all(
    flip,
    x_ref,
    other_ref,
    gate_ref,
    up_ref,
    share_ref,
    far_down,
    hidden_out,
    down_own,
    down_other,
    sems,
):
    count, depth = x_ref.shape
    side = side_of(flip)
    other_copies = column_copies(far_down, down_other, sems.at[0], (1 - side) * depth)
    own_copies = column_copies(far_down, down_own, sems.at[1], side * depth)
    for copy in other_copies + own_copies:
        copy.start()
    tile = min(TILE, gate_ref.shape[2])
    own = pl.ds(pl.multiple_of(side * depth, depth), depth)
    other = pl.ds(pl.multiple_of((1 - side) * depth, depth), depth)

    weight = share_ref[:, 0:1]

    @pl.loop(0, gate_ref.shape[2] // tile)
    def _(i):
        columns = pl.ds(pl.multiple_of(i * tile, tile), tile)
        x, y = x_ref[...], other_ref[...]
        gate = jnp.dot(x, gate_ref[0, own, columns], preferred_element_type=jnp.float32)
        gate += jnp.dot(y, gate_ref[0, other, columns], preferred_element_type=jnp.float32)
        up = jnp.dot(x, up_ref[0, own, columns], preferred_element_type=jnp.float32)
        up += jnp.dot(y, up_ref[0, other, columns], preferred_element_type=jnp.float32)
        hidden_out[:, columns] = (weight * (gate * jax.nn.sigmoid(gate)) * up).astype(jnp.bfloat16)

    for copy in other_copies + own_copies:
        copy.wait()


def down(hidden_ref, down_ref, after, out_ref):
    @pl.loop(0, out_ref.shape[1] // WIDE_TILE)
    def _(i):
        columns = pl.ds(pl.multiple_of(i * WIDE_TILE, WIDE_TILE), WIDE_TILE)
        out_ref[:, columns] = jnp.dot(
            hidden_ref[...], down_ref[:, columns], preferred_element_type=jnp.float32
        ).astype(out_ref.dtype)


def part_line(terms_ref, taken_ref, kept_ref, far_ref, next_ref, last_ref):
    total = terms_ref[...] + taken_ref[...].astype(jnp.float32)
    rows = kept_ref.shape[0]
    kept_ref[...] = total[:rows]
    for i, ref in enumerate((far_ref, next_ref, last_ref)):
        ref[...] = total[(i + 1) * rows : (i + 2) * rows].astype(jnp.bfloat16)


def combine(*refs):
    terms_ref, *taken, after, kept_ref, sent_ref = refs
    total = terms_ref[...]
    for ref in taken:
        total = total + ref[...].astype(jnp.float32)
    kept = kept_ref.shape[0]
    kept_ref[...] = total[:kept].astype(kept_ref.dtype)
    sent_ref[...] = total[kept:].astype(jnp.bfloat16)


def finish(flip, kept_ref, taken_ref, other_kept, other_taken, tokens_ref, after, out_ref):
    half = kept_ref.shape[1]
    first = side_of(flip) == 0
    own = kept_ref[...].astype(jnp.float32) + taken_ref[...].astype(jnp.float32)
    other = other_kept[...].astype(jnp.float32) + other_taken[...].astype(jnp.float32)
    tokens = tokens_ref[...].astype(jnp.float32)
    left = tokens[:, :half] + jnp.where(first, own, other)
    right = tokens[:, half:] + jnp.where(first, other, own)
    out_ref[:, :half] = left.astype(jnp.bfloat16)
    out_ref[:, half:] = right.astype(jnp.bfloat16)


def attend(
    steps, taking, near_ref, far_ref, keys_ref, values_ref, lengths_ref, place_ref, after, out_ref
):
    slots, span, width = keys_ref.shape
    rows = slots
    kv_local = width // HD
    heads = kv_local * GROUP
    each = heads + 2 * kv_local
    me = lax.axis_index("wide")
    shift = int(math.log2(rows))
    half = near_ref.shape[0]
    head_of = lax.broadcasted_iota(jnp.int32, (heads, 1), 0)
    positions = lax.broadcasted_iota(jnp.int32, (heads, span), 1)

    def by_group(pieces):
        result = pieces[0]
        for g in range(1, kv_local):
            result = jnp.where(head_of >= g * GROUP, pieces[g], result)
        return result

    for order, slot in enumerate(taking):
        request = place_ref[slot]
        at = (place_of(request >> shift, me, steps) << shift) | (request & (rows - 1))
        at = at * each
        inside = pl.ds(pl.multiple_of(jnp.where(at < half, at, at - half), each), each)
        block = jnp.where(at < half, near_ref[inside, :], far_ref[inside, :])
        query = block[:heads]
        own = block[heads:].astype(jnp.float32)
        own_key = by_group([own[g : g + 1] for g in range(kv_local)])
        own_value = by_group([own[kv_local + g : kv_local + g + 1] for g in range(kv_local)])
        own_score = jnp.sum(query.astype(jnp.float32) * own_key, axis=1, keepdims=True) * SCALE
        scores = by_group(
            [
                lax.dot_general(
                    query,
                    keys_ref[slot, :, g * HD : (g + 1) * HD],
                    (((1,), (1,)), ((), ())),
                    preferred_element_type=jnp.float32,
                )
                for g in range(kv_local)
            ]
        )
        scores = jnp.where(positions < lengths_ref[slot], scores * SCALE, -jnp.inf)
        row_max = jnp.maximum(jnp.max(scores, axis=1, keepdims=True), own_score)
        weights = jnp.exp(scores - row_max)
        own_weight = jnp.exp(own_score - row_max)
        total = jnp.sum(weights, axis=1, keepdims=True) + own_weight
        probs = (weights / total).astype(jnp.bfloat16)
        own_prob = (own_weight / total).astype(jnp.bfloat16).astype(jnp.float32)
        mixed = by_group(
            [
                jnp.dot(
                    probs,
                    values_ref[slot, :, g * HD : (g + 1) * HD],
                    preferred_element_type=jnp.float32,
                )
                for g in range(kv_local)
            ]
        )
        out_ref[order * heads : (order + 1) * heads, :] = mixed + own_prob * own_value


def lay_out(heads, pieces, out_ref, held):
    at = 0
    for piece in pieces:
        held[at : at + piece.shape[0], :] = piece[...]
        at += piece.shape[0]
    for head in range(heads):
        out_ref[:, head * HD : (head + 1) * HD] = held[
            pl.ds(head, out_ref.shape[0], stride=heads), :
        ].astype(jnp.bfloat16)


def attend_last(steps, taking, heads, *refs):
    *ins, early, out_ref, late, held = refs
    attend(steps, taking, *ins, late)
    lay_out(heads, [early, late], out_ref, held)


def make_local(wide):
    steps = steps_of(wide)
    head_steps = [*steps[1:-2], *steps[:1], *steps[-2:]]

    def local(
        queries,
        new_keys,
        new_values,
        key_cache,
        value_cache,
        lengths,
        assignment,
        tokens,
        norm_gain,
        routes,
        route_logits,
        w_gate,
        w_up,
        w_down,
    ):
        rows, width = tokens.shape
        half = width // 2
        units = w_gate.shape[2]
        count = rows * wide
        each = (queries.shape[1] + 2 * new_keys.shape[1]) // HD
        core = lax.axis_index("narrow")
        bf16, f32 = jnp.bfloat16, jnp.float32
        heads_local = queries.shape[1] // HD
        dma = pltpu.SemaphoreType.DMA
        piece_bytes = 2 * half * units

        got = cross(tokens, wide, steps[0])
        heads_in = [queries, new_keys, new_values]
        row_in = [tokens, norm_gain[None]]
        heads, *row_near = call(
            pack,
            [shape((rows * each, HD), bf16)] + [pltpu.VMEM(a.shape, a.dtype) for a in row_in],
            [distant(a) for a in heads_in + row_in],
            [pltpu.VMEM(a.shape, a.dtype) for a in heads_in]
            + [pltpu.VMEM((rows * each, HD), f32), dma((5,))],
            size=100000,
            far=range(5),
        )
        share = call(
            functools.partial(shares, steps, rows),
            shape((count, HD), f32),
            [distant(routes.T), distant(route_logits.T), heads, distant(w_gate), distant(w_up)],
            [
                pltpu.VMEM(routes.T.shape, jnp.int32),
                pltpu.VMEM(route_logits.T.shape, f32),
                dma((2,)),
            ],
            size=100000,
            far=range(5),
        )
        x = call(
            functools.partial(norm_both, steps[-2]),
            shape((2 * rows, half), bf16),
            [near(row_near[0]), got, near(row_near[1]), share, heads],
            size=100000,
            far=(3, 4),
        )

        def grown(heads, step):
            got = swap(heads, "wide", wide, step)
            return call(
                stack, shape((2 * heads.shape[0], HD), bf16), [heads, got], size=4 * heads.size
            )

        for step in steps[1:-2]:
            heads = grown(heads, step)
            x = call(
                stack_after,
                shape((2 * x.shape[0], half), bf16),
                [x, swap(x, "wide", wide, step), heads],
                size=8 * x.size,
                far=(2,),
            )
        line_steps = [steps[-2], steps[-1], steps[-2] ^ steps[-1]]
        last = cross(x, wide, line_steps[2])
        line = [cross(x, wide, line_steps[0]), swap(x, "wide", wide, line_steps[1])]
        wider = max(x.shape[0] * half // HD, heads.shape[0])
        sent_heads = call(widen, shape((wider, HD), bf16), [heads], size=4 * wider * HD)
        far_rows = swap(sent_heads, "wide", wide, steps[0])
        x, heads = call(
            stack_line,
            [shape((count, half), bf16), shape((2 * heads.shape[0], HD), bf16)],
            [x, last, line[0], far_rows, line[1], heads],
            size=8 * count * half,
        )
        got_heads = swap(heads, "wide", wide, steps[-2])

        product = 2 * count * half * units
        other_x = swap(x, "narrow", 2, 1)
        whole = pltpu.VMEM((units, half), bf16)
        hidden, down_own, down_other = call(
            functools.partial(gate_all, steps[-2]),
            [shape((count, units), bf16), whole, whole],
            [
                x,
                other_x,
                near(w_gate),
                near(w_up),
                share,
                distant(w_down),
            ],
            [dma((2, CUTS))],
            flops=4 * product,
            size=6 * piece_bytes,
            far=(5,),
        )
        heads = call(
            stack_after,
            shape((2 * heads.shape[0], HD), bf16),
            [heads, got_heads, hidden],
            size=8 * heads.size,
            far=(2,),
        )
        given = call(
            down,
            shape((count, half), bf16),
            [hidden, near(down_other), heads],
            flops=product,
            size=piece_bytes,
            far=(2,),
        )
        taken = swap(given, "narrow", 2, 1)
        far_heads = swap(heads, "wide", wide, steps[-1])
        terms = call(
            down,
            shape((count, half), f32),
            [hidden, near(down_own), given],
            flops=product,
            size=piece_bytes,
            far=(2,),
        )

        caches = [near(key_cache), near(value_cache), lengths, assignment]
        slots = queries.shape[0]
        early_slots = list(range(slots - 1))
        late_slots = list(range(slots - 1, slots))
        quarter = count // 4
        block = shape((quarter, half), bf16)
        terms, *sent = call(
            part_line,
            [shape((quarter, half), f32), block, block, block],
            [terms, taken],
            size=terms.size * 8,
        )
        taken = [
            swap(sent[1], "wide", wide, line_steps[1]),
            cross(sent[2], wide, line_steps[2]),
            cross(sent[0], wide, line_steps[0]),
        ]
        early = call(
            functools.partial(attend, head_steps, early_slots),
            shape((len(early_slots) * heads_local, HD), f32),
            [heads, far_heads, *caches, sent[0]],
            flops=2 * key_cache.size * GROUP,
            size=2 * key_cache.size,
            smem=(4, 5),
            far=(6,),
        )
        for step in reversed(steps[:-2]):
            kept = terms.shape[0] // 2
            terms, sent = call(
                combine,
                [shape((kept, half), bf16 if kept == rows else f32), shape((kept, half), bf16)],
                [terms, *taken, early],
                size=terms.size * 8,
                far=(1 + len(taken),),
            )
            taken = [swap(sent, "wide", wide, step)]
        context = call(
            functools.partial(attend_last, head_steps, late_slots, heads_local),
            shape(queries.shape, bf16),
            [heads, far_heads, *caches, sent, early],
            [
                pltpu.VMEM((len(late_slots) * heads_local, HD), f32),
                pltpu.VMEM((slots * heads_local, HD), f32),
            ],
            flops=2 * key_cache.size * GROUP,
            size=2 * key_cache.size,
            smem=(4, 5),
            far=(6,),
        )
        other_kept = swap(terms, "narrow", 2, 1)
        other_taken = cross(sent, wide, steps[0])
        mixed_out = call(
            functools.partial(finish, steps[-2]),
            shape((rows, width), bf16),
            [terms, *taken, other_kept, other_taken, tokens, distant(context)],
            size=terms.size * 8,
            far=(5,),
        )
        return (context, mixed_out)

    return local


def solution(mesh):
    placed = (
        P(("groups", "wide"), "narrow"),
        P(("groups", "wide"), "narrow"),
        P(("groups", "wide"), "narrow"),
        P(("groups", "wide"), None, "narrow"),
        P(("groups", "wide"), None, "narrow"),
        P(("groups", "wide")),
        P(("groups", "wide")),
        P(("groups", "wide"), None),
        P(),
        P("groups", None),
        P("groups", None),
        P("narrow", None, "wide"),
        P("narrow", None, "wide"),
        P("narrow", "wide", None),
    )
    return jax.shard_map(
        make_local(mesh.shape["wide"]),
        mesh=mesh,
        in_specs=placed,
        out_specs=(P(("groups", "wide"), "narrow"), P(("groups", "wide"), None)),
        check_vma=False,
    )
```

```python
import functools
import math

import jax
import jax.numpy as jnp
from jax import lax
from jax.experimental import pallas as pl
from jax.experimental.pallas import tpu as pltpu
from jax.sharding import PartitionSpec as P

HQ = 48
KVH = 8
HD = 128
GROUP = HQ // KVH
SCALE = HD ** (-0.5)
TILE = 512
WIDE_TILE = 1536
CUTS = 4
MIB = 1024 * 1024


def steps_of(wide):
    bits = int(math.log2(wide))
    return [1 << i for i in range(bits - 2)] + [wide >> 1, wide >> 2]


def swap(block, axis, count, step):
    return lax.ppermute(block, axis, [(i, i ^ step) for i in range(count)])


def cross(block, wide, step):
    pairs = [(2 * i + c, 2 * (i ^ step) + 1 - c) for i in range(wide) for c in range(2)]
    return lax.ppermute(block, ("wide", "narrow"), pairs)


def side_of(flips):
    side = lax.axis_index("narrow")
    for flip in flips:
        side = side ^ ((lax.axis_index("wide") // flip) % 2)
    return side


def owner_of(place, me, steps):
    found = me
    for bit, step in enumerate(steps):
        found = found ^ (((place >> bit) & 1) * step)
    return found


def place_of(owner, me, steps):
    differ = owner ^ me
    found = 0
    for bit, step in enumerate(steps):
        shift = int(math.log2(step))
        found = found | (((differ >> shift) & 1) << bit)
    return found


def call(kernel, outs, ins, scratch=(), flops=0, size=0, limit=4, smem=(), far=()):
    spaces = [pltpu.SMEM if i in smem else pl.ANY if i in far else pltpu.VMEM for i in range(len(ins))]
    return pl.pallas_call(
        kernel,
        name=getattr(kernel, "func", kernel).__name__,
        out_shape=outs,
        in_specs=[pl.BlockSpec(memory_space=space) for space in spaces],
        out_specs=jax.tree.map(lambda _: pl.BlockSpec(memory_space=pltpu.VMEM), outs),
        scratch_shapes=list(scratch),
        compiler_params=pltpu.CompilerParams(vmem_limit_bytes=limit * MIB),
        cost_estimate=pl.CostEstimate(flops=flops, bytes_accessed=size, transcendentals=0),
    )(*ins)


def column_copies(source, target, sems, first):
    columns = target.shape[1] // CUTS
    return [
        pltpu.make_async_copy(
            source.at[0, :, pl.ds(pl.multiple_of(first + i * columns, columns), columns)],
            target.at[:, pl.ds(i * columns, columns)],
            sems.at[i],
        )
        for i in range(CUTS)
    ]


def shape(dims, dtype):
    return jax.ShapeDtypeStruct(dims, dtype)


def near(array):
    return pltpu.with_memory_space_constraint(array, pltpu.VMEM)


def distant(array):
    return pltpu.with_memory_space_constraint(array, pltpu.HBM)


def pack(far_query, far_key, far_value, far_tokens, far_gain, heads_ref, *held):
    tokens_ref, gain_ref, *near_refs, packed, sems = held
    far_refs = (far_query, far_key, far_value, far_tokens, far_gain)
    copies = [
        pltpu.make_async_copy(far, ref, sems.at[i])
        for i, (far, ref) in enumerate(zip(far_refs, (*near_refs, tokens_ref, gain_ref)))
    ]
    for copy in copies:
        copy.start()
    for copy in copies:
        copy.wait()
    rows = near_refs[0].shape[0]
    at = 0
    each = heads_ref.shape[0] // rows
    for ref in near_refs:
        block = ref[...].astype(jnp.float32)
        for head in range(ref.shape[1] // HD):
            packed[pl.ds(at, rows, stride=each), :] = block[:, head * HD : (head + 1) * HD]
            at += 1
    heads_ref[...] = packed[...].astype(jnp.bfloat16)


def norm_both(flips, own_ref, got_ref, gain_ref, share, heads, out_ref):
    half = out_ref.shape[1]
    values = stacked([own_ref, got_ref])
    scale = lax.rsqrt(jnp.mean(values * values, axis=-1, keepdims=True) + 1e-05)
    normed = values * scale * gain_ref[...]
    out_ref[...] = jnp.where(side_of(flips) == 0, normed[:, :half], normed[:, half:]).astype(jnp.bfloat16)


def stacked(refs):
    return jnp.concatenate([ref[...].astype(jnp.float32) for ref in refs], axis=0)


def stack(*refs):
    refs[-1][...] = stacked(refs[:-1]).astype(refs[-1].dtype)


def stack_line(rows, own_ref, last_ref, far_ref, got_heads, next_ref, own_heads, out_ref, heads_ref):
    count = own_heads.shape[0]
    heads_ref[:count, :] = own_heads[...]
    heads_ref[count:, :] = got_heads[:count, :]
    line = [ref[...].astype(jnp.float32) for ref in (own_ref, far_ref, next_ref, last_ref)]
    blocks = range(0, own_ref.shape[0], rows)
    parts = [values[at : at + rows] for at in blocks for values in line]
    out_ref[...] = jnp.concatenate(parts, axis=0).astype(jnp.bfloat16)


def widen(own_ref, out_ref):
    count = own_ref.shape[0]
    out_ref[:count, :] = own_ref[...]
    out_ref[count:, :] = jnp.zeros((out_ref.shape[0] - count, HD), out_ref.dtype)


def stack_after(own_ref, got_ref, after, out_ref):
    stack(own_ref, got_ref, out_ref)


def grow_both(own_ref, got_ref, own_heads, got_heads, *refs):
    refs[-2][...] = stacked([own_ref, got_ref]).astype(jnp.bfloat16)
    refs[-1][...] = stacked([own_heads, got_heads]).astype(jnp.bfloat16)


def shares(steps, rows, far_routes, far_logits, *refs):
    *_, out_ref, routes_ref, logits_ref, sems = refs
    copies = [
        pltpu.make_async_copy(far_routes, routes_ref, sems.at[0]),
        pltpu.make_async_copy(far_logits, logits_ref, sems.at[1]),
    ]
    for copy in copies:
        copy.start()
    for copy in copies:
        copy.wait()
    count = out_ref.shape[0]
    core = lax.axis_index("narrow")
    me = lax.axis_index("wide")
    logits = logits_ref[...]
    first = 1.0 / (1.0 + jnp.exp(logits[1:2] - logits[0:1]))
    second = 1.0 - first
    chosen = (routes_ref[...] == core).astype(jnp.float32)
    weight_row = chosen[0:1] * first + chosen[1:2] * second
    row = lax.broadcasted_iota(jnp.int32, (count, count), 0)
    column = lax.broadcasted_iota(jnp.int32, (count, count), 1)
    shift = int(math.log2(rows))
    token = (owner_of(row >> shift, me, steps) << shift) | (row & (rows - 1))
    weight = jnp.sum(jnp.where(token == column, weight_row, 0.0), axis=1, keepdims=True)
    out_ref[...] = jnp.broadcast_to(weight, out_ref.shape)


def gate_all(
    flips,
    x_ref,
    other_ref,
    gate_ref,
    up_ref,
    share_ref,
    far_down,
    hidden_out,
    down_own,
    down_other,
    sems,
):
    count, depth = x_ref.shape
    side = side_of(flips)
    other_copies = column_copies(far_down, down_other, sems.at[0], (1 - side) * depth)
    own_copies = column_copies(far_down, down_own, sems.at[1], side * depth)
    for copy in other_copies + own_copies:
        copy.start()
    tile = min(TILE, gate_ref.shape[2])
    own = pl.ds(pl.multiple_of(side * depth, depth), depth)
    other = pl.ds(pl.multiple_of((1 - side) * depth, depth), depth)

    weight = share_ref[:, 0:1]

    @pl.loop(0, gate_ref.shape[2] // tile)
    def _(i):
        columns = pl.ds(pl.multiple_of(i * tile, tile), tile)
        x, y = x_ref[...], other_ref[...]
        gate = jnp.dot(x, gate_ref[0, own, columns], preferred_element_type=jnp.float32)
        gate += jnp.dot(y, gate_ref[0, other, columns], preferred_element_type=jnp.float32)
        up = jnp.dot(x, up_ref[0, own, columns], preferred_element_type=jnp.float32)
        up += jnp.dot(y, up_ref[0, other, columns], preferred_element_type=jnp.float32)
        hidden_out[:, columns] = (weight * (gate * jax.nn.sigmoid(gate)) * up).astype(jnp.bfloat16)

    for copy in other_copies + own_copies:
        copy.wait()


def down(hidden_ref, down_ref, after, out_ref):
    @pl.loop(0, out_ref.shape[1] // WIDE_TILE)
    def _(i):
        columns = pl.ds(pl.multiple_of(i * WIDE_TILE, WIDE_TILE), WIDE_TILE)
        out_ref[:, columns] = jnp.dot(
            hidden_ref[...], down_ref[:, columns], preferred_element_type=jnp.float32
        ).astype(out_ref.dtype)


def combine(terms_ref, taken_ref, after, kept_ref, sent_ref):
    total = terms_ref[...] + taken_ref[...].astype(jnp.float32)
    kept = kept_ref.shape[0]
    kept_ref[...] = total[:kept]
    sent_ref[...] = total[kept:].astype(jnp.bfloat16)


def part_line(terms_ref, taken_ref, after, kept_ref, far_ref, next_ref, last_ref):
    total = terms_ref[...] + taken_ref[...].astype(jnp.float32)
    rows = kept_ref.shape[0]
    kept_ref[...] = total[:rows]
    for i, ref in enumerate((far_ref, next_ref, last_ref)):
        ref[...] = total[(i + 1) * rows : (i + 2) * rows].astype(jnp.bfloat16)


def finish(flips, kept_ref, *refs):
    *taken, tokens_ref, after, out_ref = refs
    half = kept_ref.shape[1]
    total = kept_ref[...]
    for ref in taken:
        total = total + ref[...].astype(jnp.float32)
    tokens = tokens_ref[...].astype(jnp.float32)
    tokens = jnp.where(side_of(flips) == 0, tokens[:, :half], tokens[:, half:])
    out_ref[...] = (tokens + total).astype(jnp.bfloat16)


def join(flips, own_ref, other_ref, out_ref):
    half = own_ref.shape[1]
    first = side_of(flips) == 0
    own, other = own_ref[...], other_ref[...]
    out_ref[:, :half] = jnp.where(first, own, other)
    out_ref[:, half:] = jnp.where(first, other, own)


def attend(
    steps, taking, near_ref, far_ref, keys_ref, values_ref, lengths_ref, place_ref, after, out_ref
):
    slots, span, width = keys_ref.shape
    rows = slots
    kv_local = width // HD
    heads = kv_local * GROUP
    each = heads + 2 * kv_local
    me = lax.axis_index("wide")
    shift = int(math.log2(rows))
    half = near_ref.shape[0]
    head_of = lax.broadcasted_iota(jnp.int32, (heads, 1), 0)
    positions = lax.broadcasted_iota(jnp.int32, (heads, span), 1)

    def by_group(pieces):
        result = pieces[0]
        for g in range(1, kv_local):
            result = jnp.where(head_of >= g * GROUP, pieces[g], result)
        return result

    for order, slot in enumerate(taking):
        request = place_ref[slot]
        at = (place_of(request >> shift, me, steps) << shift) | (request & (rows - 1))
        at = at * each
        inside = pl.ds(pl.multiple_of(jnp.where(at < half, at, at - half), each), each)
        block = jnp.where(at < half, near_ref[inside, :], far_ref[inside, :])
        query = block[:heads]
        own = block[heads:].astype(jnp.float32)
        own_key = by_group([own[g : g + 1] for g in range(kv_local)])
        own_value = by_group([own[kv_local + g : kv_local + g + 1] for g in range(kv_local)])
        own_score = jnp.sum(query.astype(jnp.float32) * own_key, axis=1, keepdims=True) * SCALE
        scores = by_group(
            [
                lax.dot_general(
                    query,
                    keys_ref[slot, :, g * HD : (g + 1) * HD],
                    (((1,), (1,)), ((), ())),
                    preferred_element_type=jnp.float32,
                )
                for g in range(kv_local)
            ]
        )
        scores = jnp.where(positions < lengths_ref[slot], scores * SCALE, -jnp.inf)
        row_max = jnp.maximum(jnp.max(scores, axis=1, keepdims=True), own_score)
        weights = jnp.exp(scores - row_max)
        own_weight = jnp.exp(own_score - row_max)
        total = jnp.sum(weights, axis=1, keepdims=True) + own_weight
        probs = (weights / total).astype(jnp.bfloat16)
        own_prob = (own_weight / total).astype(jnp.bfloat16).astype(jnp.float32)
        mixed = by_group(
            [
                jnp.dot(
                    probs,
                    values_ref[slot, :, g * HD : (g + 1) * HD],
                    preferred_element_type=jnp.float32,
                )
                for g in range(kv_local)
            ]
        )
        out_ref[order * heads : (order + 1) * heads, :] = mixed + own_prob * own_value


def lay_out(heads, pieces, out_ref, held):
    at = 0
    for piece in pieces:
        held[at : at + piece.shape[0], :] = piece[...]
        at += piece.shape[0]
    for head in range(heads):
        out_ref[:, head * HD : (head + 1) * HD] = held[
            pl.ds(head, out_ref.shape[0], stride=heads), :
        ].astype(jnp.bfloat16)


def attend_last(steps, taking, heads, *refs):
    *ins, early, out_ref, late, held = refs
    attend(steps, taking, *ins, late)
    lay_out(heads, [early, late], out_ref, held)


def make_local(wide):
    steps = steps_of(wide)
    head_steps = [*steps[1:-2], *steps[:1], *steps[-2:]]
    row_steps = [*steps[-2:], *steps[:-2]]
    flips = [steps[-2], steps[0]]

    def local(
        queries,
        new_keys,
        new_values,
        key_cache,
        value_cache,
        lengths,
        assignment,
        tokens,
        norm_gain,
        routes,
        route_logits,
        w_gate,
        w_up,
        w_down,
    ):
        rows, width = tokens.shape
        half = width // 2
        units = w_gate.shape[2]
        count = rows * wide
        each = (queries.shape[1] + 2 * new_keys.shape[1]) // HD
        core = lax.axis_index("narrow")
        bf16, f32 = jnp.bfloat16, jnp.float32
        heads_local = queries.shape[1] // HD
        dma = pltpu.SemaphoreType.DMA
        piece_bytes = 2 * half * units

        got = cross(tokens, wide, steps[0])
        heads_in = [queries, new_keys, new_values]
        row_in = [tokens, norm_gain[None]]
        heads, *row_near = call(
            pack,
            [shape((rows * each, HD), bf16)] + [pltpu.VMEM(a.shape, a.dtype) for a in row_in],
            [distant(a) for a in heads_in + row_in],
            [pltpu.VMEM(a.shape, a.dtype) for a in heads_in]
            + [pltpu.VMEM((rows * each, HD), f32), dma((5,))],
            size=100000,
            far=range(5),
        )
        share = call(
            functools.partial(shares, row_steps, rows),
            shape((count, HD), f32),
            [distant(routes.T), distant(route_logits.T), heads, distant(w_gate), distant(w_up)],
            [
                pltpu.VMEM(routes.T.shape, jnp.int32),
                pltpu.VMEM(route_logits.T.shape, f32),
                dma((2,)),
            ],
            size=100000,
            far=range(5),
        )
        x = call(
            functools.partial(norm_both, flips),
            shape((2 * rows, half), bf16),
            [near(row_near[0]), got, near(row_near[1]), share, heads],
            size=100000,
            far=(3, 4),
        )

        def grown(heads, step):
            got = swap(heads, "wide", wide, step)
            return call(
                stack, shape((2 * heads.shape[0], HD), bf16), [heads, got], size=4 * heads.size
            )

        for step in steps[1:-2]:
            heads = grown(heads, step)
            x = call(
                stack_after,
                shape((2 * x.shape[0], half), bf16),
                [x, swap(x, "wide", wide, step), heads],
                size=8 * x.size,
                far=(2,),
            )
        line_steps = [steps[-2], steps[-1], steps[-2] ^ steps[-1]]
        last = cross(x, wide, line_steps[2])
        line = [cross(x, wide, line_steps[0]), swap(x, "wide", wide, line_steps[1])]
        wider = max(x.shape[0] * half // HD, heads.shape[0])
        sent_heads = call(widen, shape((wider, HD), bf16), [heads], size=4 * wider * HD)
        far_rows = swap(sent_heads, "wide", wide, steps[0])
        x, heads = call(
            functools.partial(stack_line, rows),
            [shape((count, half), bf16), shape((2 * heads.shape[0], HD), bf16)],
            [x, last, line[0], far_rows, line[1], heads],
            size=8 * count * half,
        )
        got_heads = swap(heads, "wide", wide, steps[-2])

        product = 2 * count * half * units
        other_x = swap(x, "narrow", 2, 1)
        whole = pltpu.VMEM((units, half), bf16)
        hidden, down_own, down_other = call(
            functools.partial(gate_all, flips),
            [shape((count, units), bf16), whole, whole],
            [
                x,
                other_x,
                near(w_gate),
                near(w_up),
                share,
                distant(w_down),
            ],
            [dma((2, CUTS))],
            flops=4 * product,
            size=6 * piece_bytes,
            far=(5,),
        )
        heads = call(
            stack_after,
            shape((2 * heads.shape[0], HD), bf16),
            [heads, got_heads, hidden],
            size=8 * heads.size,
            far=(2,),
        )
        given = call(
            down,
            shape((count, half), bf16),
            [hidden, near(down_other), heads],
            flops=product,
            size=piece_bytes,
            far=(2,),
        )
        taken = swap(given, "narrow", 2, 1)
        far_heads = swap(heads, "wide", wide, steps[-1])
        terms = call(
            down,
            shape((count, half), f32),
            [hidden, near(down_own), given],
            flops=product,
            size=piece_bytes,
            far=(2,),
        )

        caches = [near(key_cache), near(value_cache), lengths, assignment]
        slots = queries.shape[0]
        early_slots = list(range(slots // 2))
        late_slots = list(range(slots // 2, slots))
        early = hidden
        for step in reversed(steps[:-2]):
            kept = terms.shape[0] // 2
            terms, sent = call(
                combine,
                [shape((kept, half), f32), shape((kept, half), bf16)],
                [terms, taken, early],
                size=terms.size * 8,
                far=(2,),
            )
            taken = cross(sent, wide, step) if step in flips else swap(sent, "wide", wide, step)
            if early is hidden:
                early = call(
                    functools.partial(attend, head_steps, early_slots),
                    shape((len(early_slots) * heads_local, HD), f32),
                    [heads, far_heads, *caches, sent],
                    flops=2 * key_cache.size * GROUP,
                    size=2 * key_cache.size,
                    smem=(4, 5),
                    far=(6,),
                )
        block = shape((rows, half), bf16)
        terms, *sent = call(
            part_line,
            [shape((rows, half), f32), block, block, block],
            [terms, taken, early],
            size=terms.size * 8,
            far=(2,),
        )
        taken = [
            cross(sent[2], wide, line_steps[2]),
            cross(sent[0], wide, line_steps[0]),
            swap(sent[1], "wide", wide, line_steps[1]),
        ]
        context = call(
            functools.partial(attend_last, head_steps, late_slots, heads_local),
            shape(queries.shape, bf16),
            [heads, far_heads, *caches, sent[0], early],
            [
                pltpu.VMEM((len(late_slots) * heads_local, HD), f32),
                pltpu.VMEM((slots * heads_local, HD), f32),
            ],
            flops=2 * key_cache.size * GROUP,
            size=2 * key_cache.size,
            smem=(4, 5),
            far=(6,),
        )
        piece = call(
            functools.partial(finish, flips),
            block,
            [terms, *taken, tokens, distant(context)],
            size=terms.size * 8,
            far=(5,),
        )
        other = swap(piece, "narrow", 2, 1)
        mixed_out = call(
            functools.partial(join, flips),
            shape((rows, width), bf16),
            [piece, other],
            size=terms.size * 4,
        )
        return (context, mixed_out)

    return local


def solution(mesh):
    placed = (
        P(("groups", "wide"), "narrow"),
        P(("groups", "wide"), "narrow"),
        P(("groups", "wide"), "narrow"),
        P(("groups", "wide"), None, "narrow"),
        P(("groups", "wide"), None, "narrow"),
        P(("groups", "wide")),
        P(("groups", "wide")),
        P(("groups", "wide"), None),
        P(),
        P("groups", None),
        P("groups", None),
        P("narrow", None, "wide"),
        P("narrow", None, "wide"),
        P("narrow", "wide", None),
    )
    return jax.shard_map(
        make_local(mesh.shape["wide"]),
        mesh=mesh,
        in_specs=placed,
        out_specs=(P(("groups", "wide"), "narrow"), P(("groups", "wide"), None)),
        check_vma=False,
    )
```

```python
import functools
import math

import jax
import jax.numpy as jnp
from jax import lax
from jax.experimental import pallas as pl
from jax.experimental.pallas import tpu as pltpu
from jax.sharding import PartitionSpec as P

HQ = 48
KVH = 8
HD = 128
GROUP = HQ // KVH
SCALE = HD ** (-0.5)
TILE = 512
WIDE_TILE = 1536
CUTS = 4
MIB = 1024 * 1024


def steps_of(wide):
    bits = int(math.log2(wide))
    return [1 << i for i in range(bits - 2)] + [wide >> 1, wide >> 2]


def swap(block, axis, count, step):
    return lax.ppermute(block, axis, [(i, i ^ step) for i in range(count)])


def cross(block, wide, step):
    pairs = [(2 * i + c, 2 * (i ^ step) + 1 - c) for i in range(wide) for c in range(2)]
    return lax.ppermute(block, ("wide", "narrow"), pairs)


def side_of(flip):
    bit = (lax.axis_index("wide") // flip) % 2
    return lax.axis_index("narrow") ^ bit


def owner_of(place, me, steps):
    found = me
    for bit, step in enumerate(steps):
        found = found ^ (((place >> bit) & 1) * step)
    return found


def place_of(owner, me, steps):
    differ = owner ^ me
    found = 0
    for bit, step in enumerate(steps):
        shift = int(math.log2(step))
        found = found | (((differ >> shift) & 1) << bit)
    return found


def call(kernel, outs, ins, scratch=(), flops=0, size=0, limit=4, smem=(), far=()):
    spaces = [pltpu.SMEM if i in smem else pl.ANY if i in far else pltpu.VMEM for i in range(len(ins))]
    return pl.pallas_call(
        kernel,
        name=getattr(kernel, "func", kernel).__name__,
        out_shape=outs,
        in_specs=[pl.BlockSpec(memory_space=space) for space in spaces],
        out_specs=jax.tree.map(lambda _: pl.BlockSpec(memory_space=pltpu.VMEM), outs),
        scratch_shapes=list(scratch),
        compiler_params=pltpu.CompilerParams(vmem_limit_bytes=limit * MIB),
        cost_estimate=pl.CostEstimate(flops=flops, bytes_accessed=size, transcendentals=0),
    )(*ins)


def column_copies(source, target, sems, first):
    columns = target.shape[1] // CUTS
    return [
        pltpu.make_async_copy(
            source.at[0, :, pl.ds(pl.multiple_of(first + i * columns, columns), columns)],
            target.at[:, pl.ds(i * columns, columns)],
            sems.at[i],
        )
        for i in range(CUTS)
    ]


def shape(dims, dtype):
    return jax.ShapeDtypeStruct(dims, dtype)


def near(array):
    return pltpu.with_memory_space_constraint(array, pltpu.VMEM)


def distant(array):
    return pltpu.with_memory_space_constraint(array, pltpu.HBM)


def pack(far_query, far_key, far_value, far_tokens, far_gain, far_place, heads_ref, *held):
    *row_refs, query_ref, key_ref, value_ref, packed, sems = held
    near_refs = (query_ref, key_ref, value_ref)
    far_refs = (far_query, far_key, far_value, far_tokens, far_gain, far_place)
    copies = [
        pltpu.make_async_copy(far, ref, sems.at[i])
        for i, (far, ref) in enumerate(zip(far_refs, (*near_refs, *row_refs)))
    ]
    for copy in copies:
        copy.start()
    for copy in copies:
        copy.wait()
    rows = near_refs[0].shape[0]
    at = 0
    each = heads_ref.shape[0] // rows
    for ref in near_refs:
        block = ref[...].astype(jnp.float32)
        for head in range(ref.shape[1] // HD):
            packed[pl.ds(at, rows, stride=each), :] = block[:, head * HD : (head + 1) * HD]
            at += 1
    heads_ref[...] = packed[...].astype(jnp.bfloat16)


def norm_both(flip, own_ref, got_ref, gain_ref, share, heads, out_ref):
    half = out_ref.shape[1]
    values = stacked([own_ref, got_ref])
    scale = lax.rsqrt(jnp.mean(values * values, axis=-1, keepdims=True) + 1e-05)
    normed = values * scale * gain_ref[...]
    out_ref[...] = jnp.where(side_of(flip) == 0, normed[:, :half], normed[:, half:]).astype(jnp.bfloat16)


def stacked(refs):
    return jnp.concatenate([ref[...].astype(jnp.float32) for ref in refs], axis=0)


def stack(*refs):
    refs[-1][...] = stacked(refs[:-1]).astype(refs[-1].dtype)


def tag(rows_ref, place_ref, out_ref):
    count, half = rows_ref.shape
    slots = place_ref.shape[1]
    out_ref[:, :half] = rows_ref[...]
    out_ref[:, half:] = jnp.zeros((count, HD), jnp.bfloat16)
    names = jnp.broadcast_to(place_ref[...].astype(jnp.float32), (count, slots))
    out_ref[:, half : half + slots] = names.astype(jnp.bfloat16)


def halve(own_ref, got_ref, out_ref, first_ref, second_ref):
    count = own_ref.shape[0]
    out_ref[:count, :] = own_ref[...]
    out_ref[count:, :] = got_ref[:count, :]
    first_ref[...] = own_ref[...]
    second_ref[...] = got_ref[:count, :]


def stack_line(
    steps,
    each,
    own_ref,
    next_ref,
    far_ref,
    last_ref,
    first_ref,
    second_ref,
    own_heads,
    out_ref,
    heads_ref,
    asked_ref,
):
    half = out_ref.shape[1]
    rows = [own_ref, far_ref.at[:, :half], next_ref, last_ref]
    out_ref[...] = stacked(rows).astype(jnp.bfloat16)
    count = first_ref.shape[0]
    heads_ref[: 2 * count, :] = own_heads[...]
    heads_ref[2 * count : 3 * count, :] = first_ref[...]
    heads_ref[3 * count :, :] = second_ref[...]
    me = lax.axis_index("wide")
    slots = asked_ref.shape[0] // each
    shift = int(math.log2(slots))
    names = far_ref[:, half : half + HD].astype(jnp.float32)
    found = [jnp.zeros((each, HD), jnp.float32)] * slots
    for at in range(heads_ref.shape[0] // each):
        name = (owner_of(at >> shift, me, steps) << shift) | (at & (slots - 1))
        name = name.astype(jnp.float32)
        block = heads_ref[at * each : (at + 1) * each, :].astype(jnp.float32)
        for slot in range(slots):
            asked = names[0:1, slot : slot + 1] == name
            found[slot] = jnp.where(asked, block, found[slot])
    for slot in range(slots):
        asked_ref[slot * each : (slot + 1) * each, :] = found[slot].astype(jnp.bfloat16)


def widen(own_ref, out_ref):
    count = own_ref.shape[0]
    out_ref[:count, :] = own_ref[...]
    out_ref[count:, :] = jnp.zeros((out_ref.shape[0] - count, HD), out_ref.dtype)


def stack_after(own_ref, got_ref, after, out_ref):
    stack(own_ref, got_ref, out_ref)


def grow_both(own_ref, got_ref, own_heads, got_heads, *refs):
    refs[-2][...] = stacked([own_ref, got_ref]).astype(jnp.bfloat16)
    refs[-1][...] = stacked([own_heads, got_heads]).astype(jnp.bfloat16)


def shares(steps, rows, far_routes, far_logits, *refs):
    *_, out_ref, routes_ref, logits_ref, sems = refs
    copies = [
        pltpu.make_async_copy(far_routes, routes_ref, sems.at[0]),
        pltpu.make_async_copy(far_logits, logits_ref, sems.at[1]),
    ]
    for copy in copies:
        copy.start()
    for copy in copies:
        copy.wait()
    count = out_ref.shape[0]
    core = lax.axis_index("narrow")
    me = lax.axis_index("wide")
    logits = logits_ref[...]
    first = 1.0 / (1.0 + jnp.exp(logits[1:2] - logits[0:1]))
    second = 1.0 - first
    chosen = (routes_ref[...] == core).astype(jnp.float32)
    weight_row = chosen[0:1] * first + chosen[1:2] * second
    row = lax.broadcasted_iota(jnp.int32, (count, count), 0)
    column = lax.broadcasted_iota(jnp.int32, (count, count), 1)
    shift = int(math.log2(rows))
    token = (owner_of(row >> shift, me, steps) << shift) | (row & (rows - 1))
    weight = jnp.sum(jnp.where(token == column, weight_row, 0.0), axis=1, keepdims=True)
    out_ref[...] = jnp.broadcast_to(weight, out_ref.shape)


def gate_all(
    flip,
    x_ref,
    other_ref,
    gate_ref,
    up_ref,
    share_ref,
    far_down,
    hidden_out,
    down_own,
    down_other,
    sems,
):
    count, depth = x_ref.shape
    side = side_of(flip)
    other_copies = column_copies(far_down, down_other, sems.at[0], (1 - side) * depth)
    own_copies = column_copies(far_down, down_own, sems.at[1], side * depth)
    for copy in other_copies + own_copies:
        copy.start()
    tile = min(TILE, gate_ref.shape[2])
    own = pl.ds(pl.multiple_of(side * depth, depth), depth)
    other = pl.ds(pl.multiple_of((1 - side) * depth, depth), depth)

    weight = share_ref[:, 0:1]

    @pl.loop(0, gate_ref.shape[2] // tile)
    def _(i):
        columns = pl.ds(pl.multiple_of(i * tile, tile), tile)
        x, y = x_ref[...], other_ref[...]
        gate = jnp.dot(x, gate_ref[0, own, columns], preferred_element_type=jnp.float32)
        gate += jnp.dot(y, gate_ref[0, other, columns], preferred_element_type=jnp.float32)
        up = jnp.dot(x, up_ref[0, own, columns], preferred_element_type=jnp.float32)
        up += jnp.dot(y, up_ref[0, other, columns], preferred_element_type=jnp.float32)
        hidden_out[:, columns] = (weight * (gate * jax.nn.sigmoid(gate)) * up).astype(jnp.bfloat16)

    for copy in other_copies + own_copies:
        copy.wait()


def down(hidden_ref, down_ref, after, out_ref):
    @pl.loop(0, out_ref.shape[1] // WIDE_TILE)
    def _(i):
        columns = pl.ds(pl.multiple_of(i * WIDE_TILE, WIDE_TILE), WIDE_TILE)
        out_ref[:, columns] = jnp.dot(
            hidden_ref[...], down_ref[:, columns], preferred_element_type=jnp.float32
        ).astype(out_ref.dtype)


def part_line(terms_ref, taken_ref, kept_ref, far_ref, next_ref, last_ref):
    total = terms_ref[...] + taken_ref[...].astype(jnp.float32)
    rows = kept_ref.shape[0]
    kept_ref[...] = total[:rows]
    for i, ref in enumerate((far_ref, next_ref, last_ref)):
        ref[...] = total[(i + 1) * rows : (i + 2) * rows].astype(jnp.bfloat16)


def combine(*refs):
    terms_ref, *taken, after, kept_ref, sent_ref = refs
    total = terms_ref[...]
    for ref in taken:
        total = total + ref[...].astype(jnp.float32)
    kept = kept_ref.shape[0]
    kept_ref[...] = total[:kept].astype(kept_ref.dtype)
    sent_ref[...] = total[kept:].astype(jnp.bfloat16)


def finish(flip, kept_ref, other_kept, other_taken, taken_ref, tokens_ref, after, out_ref):
    half = kept_ref.shape[1]
    first = side_of(flip) == 0
    own = kept_ref[...].astype(jnp.float32) + taken_ref[...].astype(jnp.float32)
    other = other_kept[...].astype(jnp.float32) + other_taken[...].astype(jnp.float32)
    tokens = tokens_ref[...].astype(jnp.float32)
    left = tokens[:, :half] + jnp.where(first, own, other)
    right = tokens[:, half:] + jnp.where(first, other, own)
    out_ref[:, :half] = left.astype(jnp.bfloat16)
    out_ref[:, half:] = right.astype(jnp.bfloat16)


def attend(
    steps, taking, near_ref, far_ref, keys_ref, values_ref, lengths_ref, place_ref, after, out_ref
):
    slots, span, width = keys_ref.shape
    rows = slots
    kv_local = width // HD
    heads = kv_local * GROUP
    each = heads + 2 * kv_local
    me = lax.axis_index("wide")
    shift = int(math.log2(rows))
    half = near_ref.shape[0]
    head_of = lax.broadcasted_iota(jnp.int32, (heads, 1), 0)
    positions = lax.broadcasted_iota(jnp.int32, (heads, span), 1)

    def by_group(pieces):
        result = pieces[0]
        for g in range(1, kv_local):
            result = jnp.where(head_of >= g * GROUP, pieces[g], result)
        return result

    for order, slot in enumerate(taking):
        request = place_ref[slot]
        at = (place_of(request >> shift, me, steps) << shift) | (request & (rows - 1))
        at = at * each
        inside = pl.ds(pl.multiple_of(jnp.where(at < half, at, 0), each), each)
        far = far_ref[slot * each : (slot + 1) * each, :]
        block = jnp.where(at < half, near_ref[inside, :], far)
        query = block[:heads]
        own = block[heads:].astype(jnp.float32)
        own_key = by_group([own[g : g + 1] for g in range(kv_local)])
        own_value = by_group([own[kv_local + g : kv_local + g + 1] for g in range(kv_local)])
        own_score = jnp.sum(query.astype(jnp.float32) * own_key, axis=1, keepdims=True) * SCALE
        scores = by_group(
            [
                lax.dot_general(
                    query,
                    keys_ref[slot, :, g * HD : (g + 1) * HD],
                    (((1,), (1,)), ((), ())),
                    preferred_element_type=jnp.float32,
                )
                for g in range(kv_local)
            ]
        )
        scores = jnp.where(positions < lengths_ref[slot], scores * SCALE, -jnp.inf)
        row_max = jnp.maximum(jnp.max(scores, axis=1, keepdims=True), own_score)
        weights = jnp.exp(scores - row_max)
        own_weight = jnp.exp(own_score - row_max)
        total = jnp.sum(weights, axis=1, keepdims=True) + own_weight
        probs = (weights / total).astype(jnp.bfloat16)
        own_prob = (own_weight / total).astype(jnp.bfloat16).astype(jnp.float32)
        mixed = by_group(
            [
                jnp.dot(
                    probs,
                    values_ref[slot, :, g * HD : (g + 1) * HD],
                    preferred_element_type=jnp.float32,
                )
                for g in range(kv_local)
            ]
        )
        out_ref[order * heads : (order + 1) * heads, :] = mixed + own_prob * own_value


def lay_out(heads, pieces, out_ref, held):
    at = 0
    for piece in pieces:
        held[at : at + piece.shape[0], :] = piece[...]
        at += piece.shape[0]
    for head in range(heads):
        out_ref[:, head * HD : (head + 1) * HD] = held[
            pl.ds(head, out_ref.shape[0], stride=heads), :
        ].astype(jnp.bfloat16)


def attend_last(steps, taking, heads, *refs):
    *ins, early, out_ref, late, held = refs
    attend(steps, taking, *ins, late)
    lay_out(heads, [early, late], out_ref, held)


def make_local(wide):
    steps = steps_of(wide)
    head_steps = [*steps[1:-2], steps[0], steps[-1], steps[-2]]

    def local(
        queries,
        new_keys,
        new_values,
        key_cache,
        value_cache,
        lengths,
        assignment,
        tokens,
        norm_gain,
        routes,
        route_logits,
        w_gate,
        w_up,
        w_down,
    ):
        rows, width = tokens.shape
        half = width // 2
        units = w_gate.shape[2]
        count = rows * wide
        each = (queries.shape[1] + 2 * new_keys.shape[1]) // HD
        core = lax.axis_index("narrow")
        bf16, f32 = jnp.bfloat16, jnp.float32
        heads_local = queries.shape[1] // HD
        dma = pltpu.SemaphoreType.DMA
        piece_bytes = 2 * half * units

        got = cross(tokens, wide, steps[0])
        heads_in = [queries, new_keys, new_values]
        row_in = [tokens, norm_gain[None], assignment[None]]
        heads, *row_near = call(
            pack,
            [shape((rows * each, HD), bf16)] + [pltpu.VMEM(a.shape, a.dtype) for a in row_in],
            [distant(a) for a in heads_in + row_in],
            [pltpu.VMEM(a.shape, a.dtype) for a in heads_in]
            + [pltpu.VMEM((rows * each, HD), f32), dma((6,))],
            size=100000,
            far=range(6),
        )
        share = call(
            functools.partial(shares, steps, rows),
            shape((count, HD), f32),
            [distant(routes.T), distant(route_logits.T), heads, distant(w_gate), distant(w_up)],
            [
                pltpu.VMEM(routes.T.shape, jnp.int32),
                pltpu.VMEM(route_logits.T.shape, f32),
                dma((2,)),
            ],
            size=100000,
            far=range(5),
        )
        x = call(
            functools.partial(norm_both, steps[-2]),
            shape((2 * rows, half), bf16),
            [near(row_near[0]), got, near(row_near[1]), share, heads],
            size=100000,
            far=(3, 4),
        )

        def grown(heads, step):
            got = swap(heads, "wide", wide, step)
            return call(
                stack, shape((2 * heads.shape[0], HD), bf16), [heads, got], size=4 * heads.size
            )

        for step in steps[1:-2]:
            heads = grown(heads, step)
            x = call(
                stack_after,
                shape((2 * x.shape[0], half), bf16),
                [x, swap(x, "wide", wide, step), heads],
                size=8 * x.size,
                far=(2,),
            )
        line_steps = [steps[-2], steps[-1], steps[-2] ^ steps[-1]]
        last = cross(x, wide, line_steps[2])
        tagged = call(
            tag, shape((x.shape[0], half + HD), bf16), [x, near(row_near[2])], size=4 * x.size
        )
        line = [cross(tagged, wide, line_steps[0]), swap(x, "wide", wide, line_steps[1])]
        wider = max(x.shape[0] * half // HD, heads.shape[0])
        sent_heads = call(widen, shape((wider, HD), bf16), [heads], size=4 * wider * HD)
        far_rows = swap(sent_heads, "wide", wide, steps[0])
        part = shape(heads.shape, bf16)
        heads, *parts = call(
            halve,
            [shape((2 * heads.shape[0], HD), bf16), part, part],
            [heads, far_rows],
            size=8 * heads.size,
        )
        parts = [swap(part, "wide", wide, line_steps[1]) for part in parts]
        x, heads, asked = call(
            functools.partial(stack_line, head_steps[:-1], each),
            [
                shape((count, half), bf16),
                shape((2 * heads.shape[0], HD), bf16),
                shape((rows * each, HD), bf16),
            ],
            [x, line[1], line[0], last, *parts, heads],
            size=8 * count * half,
        )
        far_heads = swap(asked, "wide", wide, steps[-2])

        product = 2 * count * half * units
        other_x = swap(x, "narrow", 2, 1)
        whole = pltpu.VMEM((units, half), bf16)
        hidden, down_own, down_other = call(
            functools.partial(gate_all, steps[-2]),
            [shape((count, units), bf16), whole, whole],
            [
                x,
                other_x,
                near(w_gate),
                near(w_up),
                share,
                distant(w_down),
            ],
            [dma((2, CUTS))],
            flops=4 * product,
            size=6 * piece_bytes,
            far=(5,),
        )
        given = call(
            down,
            shape((count, half), bf16),
            [hidden, near(down_other), far_heads],
            flops=product,
            size=piece_bytes,
            far=(2,),
        )
        taken = swap(given, "narrow", 2, 1)
        terms = call(
            down,
            shape((count, half), f32),
            [hidden, near(down_own), given],
            flops=product,
            size=piece_bytes,
            far=(2,),
        )

        caches = [near(key_cache), near(value_cache), lengths, assignment]
        slots = queries.shape[0]
        early_slots = list(range(slots - 1))
        late_slots = list(range(slots - 1, slots))
        quarter = count // 4
        block = shape((quarter, half), bf16)
        terms, *sent = call(
            part_line,
            [shape((quarter, half), f32), block, block, block],
            [terms, taken],
            size=terms.size * 8,
        )
        taken = [
            cross(sent[0], wide, line_steps[0]),
            swap(sent[1], "wide", wide, line_steps[1]),
            cross(sent[2], wide, line_steps[2]),
        ]
        early = call(
            functools.partial(attend, head_steps, early_slots),
            shape((len(early_slots) * heads_local, HD), f32),
            [heads, far_heads, *caches, sent[1]],
            flops=2 * key_cache.size * GROUP,
            size=2 * key_cache.size,
            smem=(4, 5),
            far=(6,),
        )
        for step in reversed(steps[:-2]):
            kept = terms.shape[0] // 2
            terms, sent = call(
                combine,
                [shape((kept, half), bf16 if kept == rows else f32), shape((kept, half), bf16)],
                [terms, *taken, early],
                size=terms.size * 8,
                far=(1 + len(taken),),
            )
            taken = [swap(sent, "wide", wide, step)]
        context = call(
            functools.partial(attend_last, head_steps, late_slots, heads_local),
            shape(queries.shape, bf16),
            [heads, far_heads, *caches, terms, early],
            [
                pltpu.VMEM((len(late_slots) * heads_local, HD), f32),
                pltpu.VMEM((slots * heads_local, HD), f32),
            ],
            flops=2 * key_cache.size * GROUP,
            size=2 * key_cache.size,
            smem=(4, 5),
            far=(6,),
        )
        other_kept = swap(terms, "narrow", 2, 1)
        other_taken = cross(sent, wide, steps[0])
        mixed_out = call(
            functools.partial(finish, steps[-2]),
            shape((rows, width), bf16),
            [terms, other_kept, other_taken, *taken, tokens, distant(context)],
            size=terms.size * 8,
            far=(5,),
        )
        return (context, mixed_out)

    return local


def solution(mesh):
    placed = (
        P(("groups", "wide"), "narrow"),
        P(("groups", "wide"), "narrow"),
        P(("groups", "wide"), "narrow"),
        P(("groups", "wide"), None, "narrow"),
        P(("groups", "wide"), None, "narrow"),
        P(("groups", "wide")),
        P(("groups", "wide")),
        P(("groups", "wide"), None),
        P(),
        P("groups", None),
        P("groups", None),
        P("narrow", None, "wide"),
        P("narrow", None, "wide"),
        P("narrow", "wide", None),
    )
    return jax.shard_map(
        make_local(mesh.shape["wide"]),
        mesh=mesh,
        in_specs=placed,
        out_specs=(P(("groups", "wide"), "narrow"), P(("groups", "wide"), None)),
        check_vma=False,
    )
```

```python
import functools
import math

import jax
import jax.numpy as jnp
from jax import lax
from jax.experimental import pallas as pl
from jax.experimental.pallas import tpu as pltpu
from jax.sharding import PartitionSpec as P

HQ = 48
KVH = 8
HD = 128
GROUP = HQ // KVH
SCALE = HD ** (-0.5)
TILE = 512
WIDE_TILE = 1536
CUTS = 4
MIB = 1024 * 1024


def steps_of(wide):
    bits = int(math.log2(wide))
    return [1 << i for i in range(bits - 2)] + [wide >> 1, wide >> 2]


def swap(block, axis, count, step):
    return lax.ppermute(block, axis, [(i, i ^ step) for i in range(count)])


def cross(block, wide, step):
    pairs = [(2 * i + c, 2 * (i ^ step) + 1 - c) for i in range(wide) for c in range(2)]
    return lax.ppermute(block, ("wide", "narrow"), pairs)


def side_of(flip):
    bit = (lax.axis_index("wide") // flip) % 2
    return lax.axis_index("narrow") ^ bit


def owner_of(place, me, steps):
    found = me
    for bit, step in enumerate(steps):
        found = found ^ (((place >> bit) & 1) * step)
    return found


def place_of(owner, me, steps):
    differ = owner ^ me
    found = 0
    for bit, step in enumerate(steps):
        shift = int(math.log2(step))
        found = found | (((differ >> shift) & 1) << bit)
    return found


def call(kernel, outs, ins, scratch=(), flops=0, size=0, limit=4, smem=(), far=()):
    spaces = [pltpu.SMEM if i in smem else pl.ANY if i in far else pltpu.VMEM for i in range(len(ins))]
    return pl.pallas_call(
        kernel,
        name=getattr(kernel, "func", kernel).__name__,
        out_shape=outs,
        in_specs=[pl.BlockSpec(memory_space=space) for space in spaces],
        out_specs=jax.tree.map(lambda _: pl.BlockSpec(memory_space=pltpu.VMEM), outs),
        scratch_shapes=list(scratch),
        compiler_params=pltpu.CompilerParams(vmem_limit_bytes=limit * MIB),
        cost_estimate=pl.CostEstimate(flops=flops, bytes_accessed=size, transcendentals=0),
    )(*ins)


def column_copies(source, target, sems, first):
    columns = target.shape[1] // CUTS
    return [
        pltpu.make_async_copy(
            source.at[0, :, pl.ds(pl.multiple_of(first + i * columns, columns), columns)],
            target.at[:, pl.ds(i * columns, columns)],
            sems.at[i],
        )
        for i in range(CUTS)
    ]


def shape(dims, dtype):
    return jax.ShapeDtypeStruct(dims, dtype)


def near(array):
    return pltpu.with_memory_space_constraint(array, pltpu.VMEM)


def distant(array):
    return pltpu.with_memory_space_constraint(array, pltpu.HBM)


def pack(far_query, far_key, far_value, far_tokens, far_gain, heads_ref, *held):
    tokens_ref, gain_ref, *near_refs, packed, sems = held
    far_refs = (far_query, far_key, far_value, far_tokens, far_gain)
    copies = [
        pltpu.make_async_copy(far, ref, sems.at[i])
        for i, (far, ref) in enumerate(zip(far_refs, (*near_refs, tokens_ref, gain_ref)))
    ]
    for copy in copies:
        copy.start()
    for copy in copies:
        copy.wait()
    rows = near_refs[0].shape[0]
    at = 0
    each = heads_ref.shape[0] // rows
    for ref in near_refs:
        block = ref[...].astype(jnp.float32)
        for head in range(ref.shape[1] // HD):
            packed[pl.ds(at, rows, stride=each), :] = block[:, head * HD : (head + 1) * HD]
            at += 1
    heads_ref[...] = packed[...].astype(jnp.bfloat16)


def norm_both(flip, own_ref, got_ref, gain_ref, share, heads, out_ref):
    half = out_ref.shape[1]
    values = stacked([own_ref, got_ref])
    scale = lax.rsqrt(jnp.mean(values * values, axis=-1, keepdims=True) + 1e-05)
    normed = values * scale * gain_ref[...]
    out_ref[...] = jnp.where(side_of(flip) == 0, normed[:, :half], normed[:, half:]).astype(jnp.bfloat16)


def stacked(refs):
    return jnp.concatenate([ref[...].astype(jnp.float32) for ref in refs], axis=0)


def stack(*refs):
    refs[-1][...] = stacked(refs[:-1]).astype(refs[-1].dtype)


def stack_line(own_ref, last_ref, far_ref, got_heads, next_ref, own_heads, out_ref, heads_ref):
    count = own_heads.shape[0]
    heads_ref[:count, :] = own_heads[...]
    heads_ref[count:, :] = got_heads[:count, :]
    rows = [own_ref, far_ref, next_ref, last_ref]
    out_ref[...] = stacked(rows).astype(jnp.bfloat16)


def widen(own_ref, share, out_ref):
    count = own_ref.shape[0]
    out_ref[:count, :] = own_ref[...]
    out_ref[count:, :] = jnp.zeros((out_ref.shape[0] - count, HD), out_ref.dtype)


def stack_after(own_ref, got_ref, after, out_ref):
    stack(own_ref, got_ref, out_ref)


def grow_both(own_ref, got_ref, own_heads, got_heads, *refs):
    refs[-2][...] = stacked([own_ref, got_ref]).astype(jnp.bfloat16)
    refs[-1][...] = stacked([own_heads, got_heads]).astype(jnp.bfloat16)


def shares(steps, rows, far_routes, far_logits, *refs):
    *_, out_ref, routes_ref, logits_ref, sems = refs
    copies = [
        pltpu.make_async_copy(far_routes, routes_ref, sems.at[0]),
        pltpu.make_async_copy(far_logits, logits_ref, sems.at[1]),
    ]
    for copy in copies:
        copy.start()
    for copy in copies:
        copy.wait()
    count = out_ref.shape[0]
    core = lax.axis_index("narrow")
    me = lax.axis_index("wide")
    logits = logits_ref[...]
    first = 1.0 / (1.0 + jnp.exp(logits[1:2] - logits[0:1]))
    second = 1.0 - first
    chosen = (routes_ref[...] == core).astype(jnp.float32)
    weight_row = chosen[0:1] * first + chosen[1:2] * second
    row = lax.broadcasted_iota(jnp.int32, (count, count), 0)
    column = lax.broadcasted_iota(jnp.int32, (count, count), 1)
    shift = int(math.log2(rows))
    token = (owner_of(row >> shift, me, steps) << shift) | (row & (rows - 1))
    weight = jnp.sum(jnp.where(token == column, weight_row, 0.0), axis=1, keepdims=True)
    out_ref[...] = jnp.broadcast_to(weight, out_ref.shape)


def gate_all(
    flip,
    x_ref,
    other_ref,
    gate_ref,
    up_ref,
    share_ref,
    far_down,
    hidden_out,
    down_own,
    down_other,
    sems,
):
    count, depth = x_ref.shape
    side = side_of(flip)
    other_copies = column_copies(far_down, down_other, sems.at[0], (1 - side) * depth)
    own_copies = column_copies(far_down, down_own, sems.at[1], side * depth)
    for copy in other_copies + own_copies:
        copy.start()
    tile = min(TILE, gate_ref.shape[2])
    own = pl.ds(pl.multiple_of(side * depth, depth), depth)
    other = pl.ds(pl.multiple_of((1 - side) * depth, depth), depth)

    weight = share_ref[:, 0:1]

    @pl.loop(0, gate_ref.shape[2] // tile)
    def _(i):
        columns = pl.ds(pl.multiple_of(i * tile, tile), tile)
        x, y = x_ref[...], other_ref[...]
        gate = jnp.dot(x, gate_ref[0, own, columns], preferred_element_type=jnp.float32)
        gate += jnp.dot(y, gate_ref[0, other, columns], preferred_element_type=jnp.float32)
        up = jnp.dot(x, up_ref[0, own, columns], preferred_element_type=jnp.float32)
        up += jnp.dot(y, up_ref[0, other, columns], preferred_element_type=jnp.float32)
        hidden_out[:, columns] = (weight * (gate * jax.nn.sigmoid(gate)) * up).astype(jnp.bfloat16)

    for copy in other_copies + own_copies:
        copy.wait()


def down(hidden_ref, down_ref, after, out_ref):
    @pl.loop(0, out_ref.shape[1] // WIDE_TILE)
    def _(i):
        columns = pl.ds(pl.multiple_of(i * WIDE_TILE, WIDE_TILE), WIDE_TILE)
        out_ref[:, columns] = jnp.dot(
            hidden_ref[...], down_ref[:, columns], preferred_element_type=jnp.float32
        ).astype(out_ref.dtype)


def part_line(terms_ref, taken_ref, kept_ref, far_ref, next_ref, last_ref):
    total = terms_ref[...] + taken_ref[...].astype(jnp.float32)
    rows = kept_ref.shape[0]
    kept_ref[...] = total[:rows]
    for i, ref in enumerate((far_ref, next_ref, last_ref)):
        ref[...] = total[(i + 1) * rows : (i + 2) * rows].astype(jnp.bfloat16)


def combine(*refs):
    terms_ref, *taken, after, kept_ref, sent_ref = refs
    total = terms_ref[...]
    for ref in taken:
        total = total + ref[...].astype(jnp.float32)
    kept = kept_ref.shape[0]
    kept_ref[...] = total[:kept].astype(kept_ref.dtype)
    sent_ref[...] = total[kept:].astype(jnp.bfloat16)


def finish(flip, kept_ref, taken_ref, other_taken, other_kept, tokens_ref, after, out_ref):
    half = kept_ref.shape[1]
    first = side_of(flip) == 0
    own = kept_ref[...].astype(jnp.float32) + taken_ref[...].astype(jnp.float32)
    other = other_kept[...].astype(jnp.float32) + other_taken[...].astype(jnp.float32)
    tokens = tokens_ref[...].astype(jnp.float32)
    left = tokens[:, :half] + jnp.where(first, own, other)
    right = tokens[:, half:] + jnp.where(first, other, own)
    out_ref[:, :half] = left.astype(jnp.bfloat16)
    out_ref[:, half:] = right.astype(jnp.bfloat16)


def attend(
    steps, taking, near_ref, far_ref, keys_ref, values_ref, lengths_ref, place_ref, after, out_ref
):
    slots, span, width = keys_ref.shape
    rows = slots
    kv_local = width // HD
    heads = kv_local * GROUP
    each = heads + 2 * kv_local
    me = lax.axis_index("wide")
    shift = int(math.log2(rows))
    half = near_ref.shape[0]
    head_of = lax.broadcasted_iota(jnp.int32, (heads, 1), 0)
    positions = lax.broadcasted_iota(jnp.int32, (heads, span), 1)

    def by_group(pieces):
        result = pieces[0]
        for g in range(1, kv_local):
            result = jnp.where(head_of >= g * GROUP, pieces[g], result)
        return result

    for order, slot in enumerate(taking):
        request = place_ref[slot]
        at = (place_of(request >> shift, me, steps) << shift) | (request & (rows - 1))
        at = at * each
        inside = pl.ds(pl.multiple_of(jnp.where(at < half, at, at - half), each), each)
        block = jnp.where(at < half, near_ref[inside, :], far_ref[inside, :])
        query = block[:heads]
        own = block[heads:].astype(jnp.float32)
        own_key = by_group([own[g : g + 1] for g in range(kv_local)])
        own_value = by_group([own[kv_local + g : kv_local + g + 1] for g in range(kv_local)])
        own_score = jnp.sum(query.astype(jnp.float32) * own_key, axis=1, keepdims=True) * SCALE
        scores = by_group(
            [
                lax.dot_general(
                    query,
                    keys_ref[slot, :, g * HD : (g + 1) * HD],
                    (((1,), (1,)), ((), ())),
                    preferred_element_type=jnp.float32,
                )
                for g in range(kv_local)
            ]
        )
        scores = jnp.where(positions < lengths_ref[slot], scores * SCALE, -jnp.inf)
        row_max = jnp.maximum(jnp.max(scores, axis=1, keepdims=True), own_score)
        weights = jnp.exp(scores - row_max)
        own_weight = jnp.exp(own_score - row_max)
        total = jnp.sum(weights, axis=1, keepdims=True) + own_weight
        probs = (weights / total).astype(jnp.bfloat16)
        own_prob = (own_weight / total).astype(jnp.bfloat16).astype(jnp.float32)
        mixed = by_group(
            [
                jnp.dot(
                    probs,
                    values_ref[slot, :, g * HD : (g + 1) * HD],
                    preferred_element_type=jnp.float32,
                )
                for g in range(kv_local)
            ]
        )
        out_ref[order * heads : (order + 1) * heads, :] = mixed + own_prob * own_value


def lay_out(heads, pieces, out_ref, held):
    at = 0
    for piece in pieces:
        held[at : at + piece.shape[0], :] = piece[...]
        at += piece.shape[0]
    for head in range(heads):
        out_ref[:, head * HD : (head + 1) * HD] = held[
            pl.ds(head, out_ref.shape[0], stride=heads), :
        ].astype(jnp.bfloat16)


def attend_last(steps, taking, heads, *refs):
    *ins, early, out_ref, late, held = refs
    attend(steps, taking, *ins, late)
    lay_out(heads, [early, late], out_ref, held)


def make_local(wide):
    steps = steps_of(wide)
    head_steps = [*steps[1:-2], *steps[:1], *steps[-2:]]

    def local(
        queries,
        new_keys,
        new_values,
        key_cache,
        value_cache,
        lengths,
        assignment,
        tokens,
        norm_gain,
        routes,
        route_logits,
        w_gate,
        w_up,
        w_down,
    ):
        rows, width = tokens.shape
        half = width // 2
        units = w_gate.shape[2]
        count = rows * wide
        each = (queries.shape[1] + 2 * new_keys.shape[1]) // HD
        core = lax.axis_index("narrow")
        bf16, f32 = jnp.bfloat16, jnp.float32
        heads_local = queries.shape[1] // HD
        dma = pltpu.SemaphoreType.DMA
        piece_bytes = 2 * half * units

        got = cross(tokens, wide, steps[0])
        heads_in = [queries, new_keys, new_values]
        row_in = [tokens, norm_gain[None]]
        heads, *row_near = call(
            pack,
            [shape((rows * each, HD), bf16)] + [pltpu.VMEM(a.shape, a.dtype) for a in row_in],
            [distant(a) for a in heads_in + row_in],
            [pltpu.VMEM(a.shape, a.dtype) for a in heads_in]
            + [pltpu.VMEM((rows * each, HD), f32), dma((5,))],
            size=100000,
            far=range(5),
        )
        share = call(
            functools.partial(shares, steps, rows),
            shape((count, HD), f32),
            [distant(routes.T), distant(route_logits.T), heads, distant(w_gate), distant(w_up)],
            [
                pltpu.VMEM(routes.T.shape, jnp.int32),
                pltpu.VMEM(route_logits.T.shape, f32),
                dma((2,)),
            ],
            size=100000,
            far=range(5),
        )
        x = call(
            functools.partial(norm_both, steps[-2]),
            shape((2 * rows, half), bf16),
            [near(row_near[0]), got, near(row_near[1]), share, heads],
            size=100000,
            far=(3, 4),
        )

        def grown(heads, step):
            got = swap(heads, "wide", wide, step)
            return call(
                stack, shape((2 * heads.shape[0], HD), bf16), [heads, got], size=4 * heads.size
            )

        for step in steps[1:-2]:
            heads = grown(heads, step)
            x = call(
                stack_after,
                shape((2 * x.shape[0], half), bf16),
                [x, swap(x, "wide", wide, step), heads],
                size=8 * x.size,
                far=(2,),
            )
        line_steps = [steps[-2], steps[-1], steps[-2] ^ steps[-1]]
        last = cross(x, wide, line_steps[2])
        line = [cross(x, wide, line_steps[0]), swap(x, "wide", wide, line_steps[1])]
        wider = max(x.shape[0] * half // HD, heads.shape[0])
        sent_heads = call(
            widen, shape((wider, HD), bf16), [heads, share], size=4 * wider * HD, far=(1,)
        )
        far_rows = swap(sent_heads, "wide", wide, steps[0])
        x, heads = call(
            stack_line,
            [shape((count, half), bf16), shape((2 * heads.shape[0], HD), bf16)],
            [x, last, line[0], far_rows, line[1], heads],
            size=8 * count * half,
        )
        got_heads = swap(heads, "wide", wide, steps[-2])

        product = 2 * count * half * units
        other_x = swap(x, "narrow", 2, 1)
        whole = pltpu.VMEM((units, half), bf16)
        hidden, down_own, down_other = call(
            functools.partial(gate_all, steps[-2]),
            [shape((count, units), bf16), whole, whole],
            [
                x,
                other_x,
                near(w_gate),
                near(w_up),
                share,
                distant(w_down),
            ],
            [dma((2, CUTS))],
            flops=4 * product,
            size=6 * piece_bytes,
            far=(5,),
        )
        heads = call(
            stack_after,
            shape((2 * heads.shape[0], HD), bf16),
            [heads, got_heads, hidden],
            size=8 * heads.size,
            far=(2,),
        )
        given = call(
            down,
            shape((count, half), bf16),
            [hidden, near(down_other), heads],
            flops=product,
            size=piece_bytes,
            far=(2,),
        )
        taken = swap(given, "narrow", 2, 1)
        far_heads = swap(heads, "wide", wide, steps[-1])
        terms = call(
            down,
            shape((count, half), f32),
            [hidden, near(down_own), given],
            flops=product,
            size=piece_bytes,
            far=(2,),
        )

        caches = [near(key_cache), near(value_cache), lengths, assignment]
        slots = queries.shape[0]
        early_slots = list(range(slots - 1))
        late_slots = list(range(slots - 1, slots))
        quarter = count // 4
        block = shape((quarter, half), bf16)
        terms, *sent = call(
            part_line,
            [shape((quarter, half), f32), block, block, block],
            [terms, taken],
            size=terms.size * 8,
        )
        taken = [
            swap(sent[1], "wide", wide, line_steps[1]),
            cross(sent[2], wide, line_steps[2]),
            cross(sent[0], wide, line_steps[0]),
        ]
        early = call(
            functools.partial(attend, head_steps, early_slots),
            shape((len(early_slots) * heads_local, HD), f32),
            [heads, far_heads, *caches, sent[0]],
            flops=2 * key_cache.size * GROUP,
            size=2 * key_cache.size,
            smem=(4, 5),
            far=(6,),
        )
        for step in reversed(steps[:-2]):
            kept = terms.shape[0] // 2
            terms, sent = call(
                combine,
                [shape((kept, half), bf16 if kept == rows else f32), shape((kept, half), bf16)],
                [terms, *taken, early],
                size=terms.size * 8,
                far=(1 + len(taken),),
            )
            taken = [swap(sent, "wide", wide, step)]
        context = call(
            functools.partial(attend_last, head_steps, late_slots, heads_local),
            shape(queries.shape, bf16),
            [heads, far_heads, *caches, terms, early],
            [
                pltpu.VMEM((len(late_slots) * heads_local, HD), f32),
                pltpu.VMEM((slots * heads_local, HD), f32),
            ],
            flops=2 * key_cache.size * GROUP,
            size=2 * key_cache.size,
            smem=(4, 5),
            far=(6,),
        )
        other_kept = swap(terms, "narrow", 2, 1)
        other_taken = cross(sent, wide, steps[0])
        mixed_out = call(
            functools.partial(finish, steps[-2]),
            shape((rows, width), bf16),
            [terms, *taken, other_taken, other_kept, tokens, distant(context)],
            size=terms.size * 8,
            far=(5,),
        )
        return (context, mixed_out)

    return local


def solution(mesh):
    placed = (
        P(("groups", "wide"), "narrow"),
        P(("groups", "wide"), "narrow"),
        P(("groups", "wide"), "narrow"),
        P(("groups", "wide"), None, "narrow"),
        P(("groups", "wide"), None, "narrow"),
        P(("groups", "wide")),
        P(("groups", "wide")),
        P(("groups", "wide"), None),
        P(),
        P("groups", None),
        P("groups", None),
        P("narrow", None, "wide"),
        P("narrow", None, "wide"),
        P("narrow", "wide", None),
    )
    return jax.shard_map(
        make_local(mesh.shape["wide"]),
        mesh=mesh,
        in_specs=placed,
        out_specs=(P(("groups", "wide"), "narrow"), P(("groups", "wide"), None)),
        check_vma=False,
    )
```

```python
import functools
import math

import jax
import jax.numpy as jnp
from jax import lax
from jax.experimental import pallas as pl
from jax.experimental.pallas import tpu as pltpu
from jax.sharding import PartitionSpec as P

HQ = 48
KVH = 8
HD = 128
GROUP = HQ // KVH
SCALE = HD ** (-0.5)
TILE = 512
WIDE_TILE = 1536
CUTS = 4
MIB = 1024 * 1024


def steps_of(wide):
    bits = int(math.log2(wide))
    return [1 << i for i in range(bits - 2)] + [wide >> 1, wide >> 2]


def swap(block, axis, count, step):
    return lax.ppermute(block, axis, [(i, i ^ step) for i in range(count)])


def cross(block, wide, step):
    pairs = [(2 * i + c, 2 * (i ^ step) + 1 - c) for i in range(wide) for c in range(2)]
    return lax.ppermute(block, ("wide", "narrow"), pairs)


def side_of(flip):
    bit = (lax.axis_index("wide") // flip) % 2
    return lax.axis_index("narrow") ^ bit


def owner_of(place, me, steps):
    found = me
    for bit, step in enumerate(steps):
        found = found ^ (((place >> bit) & 1) * step)
    return found


def place_of(owner, me, steps):
    differ = owner ^ me
    found = 0
    for bit, step in enumerate(steps):
        shift = int(math.log2(step))
        found = found | (((differ >> shift) & 1) << bit)
    return found


def call(kernel, outs, ins, scratch=(), flops=0, size=0, limit=4, smem=(), far=()):
    spaces = [pltpu.SMEM if i in smem else pl.ANY if i in far else pltpu.VMEM for i in range(len(ins))]
    return pl.pallas_call(
        kernel,
        name=getattr(kernel, "func", kernel).__name__,
        out_shape=outs,
        in_specs=[pl.BlockSpec(memory_space=space) for space in spaces],
        out_specs=jax.tree.map(lambda _: pl.BlockSpec(memory_space=pltpu.VMEM), outs),
        scratch_shapes=list(scratch),
        compiler_params=pltpu.CompilerParams(vmem_limit_bytes=limit * MIB),
        cost_estimate=pl.CostEstimate(flops=flops, bytes_accessed=size, transcendentals=0),
    )(*ins)


def column_copies(source, target, sems, first):
    columns = target.shape[1] // CUTS
    return [
        pltpu.make_async_copy(
            source.at[0, :, pl.ds(pl.multiple_of(first + i * columns, columns), columns)],
            target.at[:, pl.ds(i * columns, columns)],
            sems.at[i],
        )
        for i in range(CUTS)
    ]


def shape(dims, dtype):
    return jax.ShapeDtypeStruct(dims, dtype)


def near(array):
    return pltpu.with_memory_space_constraint(array, pltpu.VMEM)


def distant(array):
    return pltpu.with_memory_space_constraint(array, pltpu.HBM)


def pack(far_query, far_key, far_value, far_tokens, far_gain, heads_ref, *held):
    tokens_ref, gain_ref, *near_refs, packed, sems = held
    far_refs = (far_query, far_key, far_value, far_tokens, far_gain)
    copies = [
        pltpu.make_async_copy(far, ref, sems.at[i])
        for i, (far, ref) in enumerate(zip(far_refs, (*near_refs, tokens_ref, gain_ref)))
    ]
    for copy in copies:
        copy.start()
    for copy in copies:
        copy.wait()
    rows = near_refs[0].shape[0]
    at = 0
    each = heads_ref.shape[0] // rows
    for ref in near_refs:
        block = ref[...].astype(jnp.float32)
        for head in range(ref.shape[1] // HD):
            packed[pl.ds(at, rows, stride=each), :] = block[:, head * HD : (head + 1) * HD]
            at += 1
    heads_ref[...] = packed[...].astype(jnp.bfloat16)


def norm_both(flip, own_ref, got_ref, gain_ref, share, heads, out_ref):
    half = out_ref.shape[1]
    values = stacked([own_ref, got_ref])
    scale = lax.rsqrt(jnp.mean(values * values, axis=-1, keepdims=True) + 1e-05)
    normed = values * scale * gain_ref[...]
    out_ref[...] = jnp.where(side_of(flip) == 0, normed[:, :half], normed[:, half:]).astype(jnp.bfloat16)


def stacked(refs):
    return jnp.concatenate([ref[...].astype(jnp.float32) for ref in refs], axis=0)


def stack(*refs):
    refs[-1][...] = stacked(refs[:-1]).astype(refs[-1].dtype)


def stack_line(own_ref, last_ref, far_ref, got_heads, next_ref, own_heads, out_ref, heads_ref):
    count = own_heads.shape[0]
    heads_ref[:count, :] = own_heads[...]
    heads_ref[count:, :] = got_heads[:count, :]
    rows = [own_ref, far_ref, next_ref, last_ref]
    out_ref[...] = stacked(rows).astype(jnp.bfloat16)


def widen(own_ref, out_ref):
    count = own_ref.shape[0]
    out_ref[:count, :] = own_ref[...]
    out_ref[count:, :] = jnp.zeros((out_ref.shape[0] - count, HD), out_ref.dtype)


def stack_after(own_ref, got_ref, after, out_ref):
    stack(own_ref, got_ref, out_ref)


def grow_both(own_ref, got_ref, own_heads, got_heads, *refs):
    refs[-2][...] = stacked([own_ref, got_ref]).astype(jnp.bfloat16)
    refs[-1][...] = stacked([own_heads, got_heads]).astype(jnp.bfloat16)


def shares(steps, rows, far_routes, far_logits, *refs):
    *_, out_ref, routes_ref, logits_ref, sems = refs
    copies = [
        pltpu.make_async_copy(far_routes, routes_ref, sems.at[0]),
        pltpu.make_async_copy(far_logits, logits_ref, sems.at[1]),
    ]
    for copy in copies:
        copy.start()
    for copy in copies:
        copy.wait()
    count = out_ref.shape[0]
    core = lax.axis_index("narrow")
    me = lax.axis_index("wide")
    logits = logits_ref[...]
    first = 1.0 / (1.0 + jnp.exp(logits[1:2] - logits[0:1]))
    second = 1.0 - first
    chosen = (routes_ref[...] == core).astype(jnp.float32)
    weight_row = chosen[0:1] * first + chosen[1:2] * second
    row = lax.broadcasted_iota(jnp.int32, (count, count), 0)
    column = lax.broadcasted_iota(jnp.int32, (count, count), 1)
    shift = int(math.log2(rows))
    token = (owner_of(row >> shift, me, steps) << shift) | (row & (rows - 1))
    weight = jnp.sum(jnp.where(token == column, weight_row, 0.0), axis=1, keepdims=True)
    out_ref[...] = jnp.broadcast_to(weight, out_ref.shape)


def gate_all(
    flip,
    x_ref,
    other_ref,
    gate_ref,
    up_ref,
    share_ref,
    far_down,
    hidden_out,
    down_own,
    down_other,
    sems,
):
    count, depth = x_ref.shape
    side = side_of(flip)
    other_copies = column_copies(far_down, down_other, sems.at[0], (1 - side) * depth)
    own_copies = column_copies(far_down, down_own, sems.at[1], side * depth)
    for copy in other_copies + own_copies:
        copy.start()
    tile = min(TILE, gate_ref.shape[2])
    own = pl.ds(pl.multiple_of(side * depth, depth), depth)
    other = pl.ds(pl.multiple_of((1 - side) * depth, depth), depth)

    weight = share_ref[:, 0:1]

    @pl.loop(0, gate_ref.shape[2] // tile)
    def _(i):
        columns = pl.ds(pl.multiple_of(i * tile, tile), tile)
        x, y = x_ref[...], other_ref[...]
        gate = jnp.dot(x, gate_ref[0, own, columns], preferred_element_type=jnp.float32)
        gate += jnp.dot(y, gate_ref[0, other, columns], preferred_element_type=jnp.float32)
        up = jnp.dot(x, up_ref[0, own, columns], preferred_element_type=jnp.float32)
        up += jnp.dot(y, up_ref[0, other, columns], preferred_element_type=jnp.float32)
        hidden_out[:, columns] = (weight * (gate * jax.nn.sigmoid(gate)) * up).astype(jnp.bfloat16)

    for copy in other_copies + own_copies:
        copy.wait()


def down(hidden_ref, down_ref, after, out_ref):
    @pl.loop(0, out_ref.shape[1] // WIDE_TILE)
    def _(i):
        columns = pl.ds(pl.multiple_of(i * WIDE_TILE, WIDE_TILE), WIDE_TILE)
        out_ref[:, columns] = jnp.dot(
            hidden_ref[...], down_ref[:, columns], preferred_element_type=jnp.float32
        ).astype(out_ref.dtype)


def part_line(terms_ref, taken_ref, kept_ref, far_ref, next_ref, last_ref):
    total = terms_ref[...] + taken_ref[...].astype(jnp.float32)
    rows = kept_ref.shape[0]
    kept_ref[...] = total[:rows]
    for i, ref in enumerate((far_ref, next_ref, last_ref)):
        ref[...] = total[(i + 1) * rows : (i + 2) * rows].astype(jnp.bfloat16)


def combine(*refs):
    terms_ref, *taken, after, kept_ref, sent_ref = refs
    total = terms_ref[...]
    for ref in taken:
        total = total + ref[...].astype(jnp.float32)
    kept = kept_ref.shape[0]
    kept_ref[...] = total[:kept].astype(kept_ref.dtype)
    sent_ref[...] = total[kept:].astype(jnp.bfloat16)


def finish(flip, kept_ref, taken_ref, other_kept, other_taken, tokens_ref, after, out_ref):
    half = kept_ref.shape[1]
    first = side_of(flip) == 0
    own = kept_ref[...].astype(jnp.float32) + taken_ref[...].astype(jnp.float32)
    other = other_kept[...].astype(jnp.float32) + other_taken[...].astype(jnp.float32)
    tokens = tokens_ref[...].astype(jnp.float32)
    left = tokens[:, :half] + jnp.where(first, own, other)
    right = tokens[:, half:] + jnp.where(first, other, own)
    out_ref[:, :half] = left.astype(jnp.bfloat16)
    out_ref[:, half:] = right.astype(jnp.bfloat16)


def attend(
    steps, taking, near_ref, far_ref, keys_ref, values_ref, lengths_ref, place_ref, after, out_ref
):
    slots, span, width = keys_ref.shape
    rows = slots
    kv_local = width // HD
    heads = kv_local * GROUP
    each = heads + 2 * kv_local
    me = lax.axis_index("wide")
    shift = int(math.log2(rows))
    half = near_ref.shape[0]
    head_of = lax.broadcasted_iota(jnp.int32, (heads, 1), 0)
    positions = lax.broadcasted_iota(jnp.int32, (heads, span), 1)

    def by_group(pieces):
        result = pieces[0]
        for g in range(1, kv_local):
            result = jnp.where(head_of >= g * GROUP, pieces[g], result)
        return result

    for order, slot in enumerate(taking):
        request = place_ref[slot]
        at = (place_of(request >> shift, me, steps) << shift) | (request & (rows - 1))
        at = at * each
        inside = pl.ds(pl.multiple_of(jnp.where(at < half, at, at - half), each), each)
        block = jnp.where(at < half, near_ref[inside, :], far_ref[inside, :])
        query = block[:heads]
        own = block[heads:].astype(jnp.float32)
        own_key = by_group([own[g : g + 1] for g in range(kv_local)])
        own_value = by_group([own[kv_local + g : kv_local + g + 1] for g in range(kv_local)])
        own_score = jnp.sum(query.astype(jnp.float32) * own_key, axis=1, keepdims=True) * SCALE
        scores = by_group(
            [
                lax.dot_general(
                    query,
                    keys_ref[slot, :, g * HD : (g + 1) * HD],
                    (((1,), (1,)), ((), ())),
                    preferred_element_type=jnp.float32,
                )
                for g in range(kv_local)
            ]
        )
        scores = jnp.where(positions < lengths_ref[slot], scores * SCALE, -jnp.inf)
        row_max = jnp.maximum(jnp.max(scores, axis=1, keepdims=True), own_score)
        weights = jnp.exp(scores - row_max)
        own_weight = jnp.exp(own_score - row_max)
        total = jnp.sum(weights, axis=1, keepdims=True) + own_weight
        probs = (weights / total).astype(jnp.bfloat16)
        own_prob = (own_weight / total).astype(jnp.bfloat16).astype(jnp.float32)
        mixed = by_group(
            [
                jnp.dot(
                    probs,
                    values_ref[slot, :, g * HD : (g + 1) * HD],
                    preferred_element_type=jnp.float32,
                )
                for g in range(kv_local)
            ]
        )
        out_ref[order * heads : (order + 1) * heads, :] = mixed + own_prob * own_value


def lay_out(heads, pieces, out_ref, held):
    at = 0
    for piece in pieces:
        held[at : at + piece.shape[0], :] = piece[...]
        at += piece.shape[0]
    for head in range(heads):
        out_ref[:, head * HD : (head + 1) * HD] = held[
            pl.ds(head, out_ref.shape[0], stride=heads), :
        ].astype(jnp.bfloat16)


def attend_last(steps, taking, heads, *refs):
    *ins, early, out_ref, late, held = refs
    attend(steps, taking, *ins, late)
    lay_out(heads, [early, late], out_ref, held)


def make_local(wide):
    steps = steps_of(wide)
    head_steps = [*steps[1:-2], *steps[:1], *steps[-2:]]

    def local(
        queries,
        new_keys,
        new_values,
        key_cache,
        value_cache,
        lengths,
        assignment,
        tokens,
        norm_gain,
        routes,
        route_logits,
        w_gate,
        w_up,
        w_down,
    ):
        rows, width = tokens.shape
        half = width // 2
        units = w_gate.shape[2]
        count = rows * wide
        each = (queries.shape[1] + 2 * new_keys.shape[1]) // HD
        core = lax.axis_index("narrow")
        bf16, f32 = jnp.bfloat16, jnp.float32
        heads_local = queries.shape[1] // HD
        dma = pltpu.SemaphoreType.DMA
        piece_bytes = 2 * half * units

        got = cross(tokens, wide, steps[0])
        heads_in = [queries, new_keys, new_values]
        row_in = [tokens, norm_gain[None]]
        heads, *row_near = call(
            pack,
            [shape((rows * each, HD), bf16)] + [pltpu.VMEM(a.shape, a.dtype) for a in row_in],
            [distant(a) for a in heads_in + row_in],
            [pltpu.VMEM(a.shape, a.dtype) for a in heads_in]
            + [pltpu.VMEM((rows * each, HD), f32), dma((5,))],
            size=100000,
            far=range(5),
        )
        share = call(
            functools.partial(shares, steps, rows),
            shape((count, HD), f32),
            [distant(routes.T), distant(route_logits.T), heads, distant(w_gate), distant(w_up)],
            [
                pltpu.VMEM(routes.T.shape, jnp.int32),
                pltpu.VMEM(route_logits.T.shape, f32),
                dma((2,)),
            ],
            size=100000,
            far=range(5),
        )
        x = call(
            functools.partial(norm_both, steps[-1]),
            shape((2 * rows, half), bf16),
            [near(row_near[0]), got, near(row_near[1]), share, heads],
            size=100000,
            far=(3, 4),
        )

        def grown(heads, step):
            got = swap(heads, "wide", wide, step)
            return call(
                stack, shape((2 * heads.shape[0], HD), bf16), [heads, got], size=4 * heads.size
            )

        for step in steps[1:-2]:
            heads = grown(heads, step)
            x = call(
                stack_after,
                shape((2 * x.shape[0], half), bf16),
                [x, swap(x, "wide", wide, step), heads],
                size=8 * x.size,
                far=(2,),
            )
        line_steps = [steps[-2], steps[-1], steps[-2] ^ steps[-1]]
        last = cross(x, wide, line_steps[2])
        line = [swap(x, "wide", wide, line_steps[0]), cross(x, wide, line_steps[1])]
        wider = max(x.shape[0] * half // HD, heads.shape[0])
        sent_heads = call(widen, shape((wider, HD), bf16), [heads], size=4 * wider * HD)
        far_rows = swap(sent_heads, "wide", wide, steps[0])
        x, heads = call(
            stack_line,
            [shape((count, half), bf16), shape((2 * heads.shape[0], HD), bf16)],
            [x, last, line[0], far_rows, line[1], heads],
            size=8 * count * half,
        )
        got_heads = swap(heads, "wide", wide, steps[-2])

        product = 2 * count * half * units
        other_x = swap(x, "narrow", 2, 1)
        whole = pltpu.VMEM((units, half), bf16)
        hidden, down_own, down_other = call(
            functools.partial(gate_all, steps[-1]),
            [shape((count, units), bf16), whole, whole],
            [
                x,
                other_x,
                near(w_gate),
                near(w_up),
                share,
                distant(w_down),
            ],
            [dma((2, CUTS))],
            flops=4 * product,
            size=6 * piece_bytes,
            far=(5,),
        )
        heads = call(
            stack_after,
            shape((2 * heads.shape[0], HD), bf16),
            [heads, got_heads, hidden],
            size=8 * heads.size,
            far=(2,),
        )
        given = call(
            down,
            shape((count, half), bf16),
            [hidden, near(down_other), heads],
            flops=product,
            size=piece_bytes,
            far=(2,),
        )
        taken = swap(given, "narrow", 2, 1)
        far_heads = swap(heads, "wide", wide, steps[-1])
        terms = call(
            down,
            shape((count, half), f32),
            [hidden, near(down_own), given],
            flops=product,
            size=piece_bytes,
            far=(2,),
        )

        caches = [near(key_cache), near(value_cache), lengths, assignment]
        slots = queries.shape[0]
        early_slots = list(range(slots - 1))
        late_slots = list(range(slots - 1, slots))
        quarter = count // 4
        block = shape((quarter, half), bf16)
        terms, *sent = call(
            part_line,
            [shape((quarter, half), f32), block, block, block],
            [terms, taken],
            size=terms.size * 8,
        )
        taken = [
            cross(sent[1], wide, line_steps[1]),
            cross(sent[2], wide, line_steps[2]),
            swap(sent[0], "wide", wide, line_steps[0]),
        ]
        early = call(
            functools.partial(attend, head_steps, early_slots),
            shape((len(early_slots) * heads_local, HD), f32),
            [heads, far_heads, *caches, sent[0]],
            flops=2 * key_cache.size * GROUP,
            size=2 * key_cache.size,
            smem=(4, 5),
            far=(6,),
        )
        for step in reversed(steps[:-2]):
            kept = terms.shape[0] // 2
            terms, sent = call(
                combine,
                [shape((kept, half), bf16 if kept == rows else f32), shape((kept, half), bf16)],
                [terms, *taken, early],
                size=terms.size * 8,
                far=(1 + len(taken),),
            )
            taken = [swap(sent, "wide", wide, step)]
        context = call(
            functools.partial(attend_last, head_steps, late_slots, heads_local),
            shape(queries.shape, bf16),
            [heads, far_heads, *caches, sent, early],
            [
                pltpu.VMEM((len(late_slots) * heads_local, HD), f32),
                pltpu.VMEM((slots * heads_local, HD), f32),
            ],
            flops=2 * key_cache.size * GROUP,
            size=2 * key_cache.size,
            smem=(4, 5),
            far=(6,),
        )
        other_kept = swap(terms, "narrow", 2, 1)
        other_taken = cross(sent, wide, steps[0])
        mixed_out = call(
            functools.partial(finish, steps[-1]),
            shape((rows, width), bf16),
            [terms, *taken, other_kept, other_taken, tokens, distant(context)],
            size=terms.size * 8,
            far=(5,),
        )
        return (context, mixed_out)

    return local


def solution(mesh):
    placed = (
        P(("groups", "wide"), "narrow"),
        P(("groups", "wide"), "narrow"),
        P(("groups", "wide"), "narrow"),
        P(("groups", "wide"), None, "narrow"),
        P(("groups", "wide"), None, "narrow"),
        P(("groups", "wide")),
        P(("groups", "wide")),
        P(("groups", "wide"), None),
        P(),
        P("groups", None),
        P("groups", None),
        P("narrow", None, "wide"),
        P("narrow", None, "wide"),
        P("narrow", "wide", None),
    )
    return jax.shard_map(
        make_local(mesh.shape["wide"]),
        mesh=mesh,
        in_specs=placed,
        out_specs=(P(("groups", "wide"), "narrow"), P(("groups", "wide"), None)),
        check_vma=False,
    )
```

```python
import functools
import math

import jax
import jax.numpy as jnp
from jax import lax
from jax.experimental import pallas as pl
from jax.experimental.pallas import tpu as pltpu
from jax.sharding import PartitionSpec as P

HQ = 48
KVH = 8
HD = 128
GROUP = HQ // KVH
SCALE = HD ** (-0.5)
TILE = 512
WIDE_TILE = 1536
CUTS = 4
MIB = 1024 * 1024


def steps_of(wide):
    bits = int(math.log2(wide))
    return [1 << i for i in range(bits - 2)] + [wide >> 1, wide >> 2]


def swap(block, axis, count, step):
    return lax.ppermute(block, axis, [(i, i ^ step) for i in range(count)])


def cross(block, wide, step):
    pairs = [(2 * i + c, 2 * (i ^ step) + 1 - c) for i in range(wide) for c in range(2)]
    return lax.ppermute(block, ("wide", "narrow"), pairs)


def side_of(flip):
    bit = (lax.axis_index("wide") // flip) % 2
    return lax.axis_index("narrow") ^ bit


def owner_of(place, me, steps):
    found = me
    for bit, step in enumerate(steps):
        found = found ^ (((place >> bit) & 1) * step)
    return found


def place_of(owner, me, steps):
    differ = owner ^ me
    found = 0
    for bit, step in enumerate(steps):
        shift = int(math.log2(step))
        found = found | (((differ >> shift) & 1) << bit)
    return found


def call(kernel, outs, ins, scratch=(), flops=0, size=0, limit=4, smem=(), far=()):
    spaces = [pltpu.SMEM if i in smem else pl.ANY if i in far else pltpu.VMEM for i in range(len(ins))]
    return pl.pallas_call(
        kernel,
        name=getattr(kernel, "func", kernel).__name__,
        out_shape=outs,
        in_specs=[pl.BlockSpec(memory_space=space) for space in spaces],
        out_specs=jax.tree.map(lambda _: pl.BlockSpec(memory_space=pltpu.VMEM), outs),
        scratch_shapes=list(scratch),
        compiler_params=pltpu.CompilerParams(vmem_limit_bytes=limit * MIB),
        cost_estimate=pl.CostEstimate(flops=flops, bytes_accessed=size, transcendentals=0),
    )(*ins)


def column_copies(source, target, sems, first):
    columns = target.shape[1] // CUTS
    return [
        pltpu.make_async_copy(
            source.at[0, :, pl.ds(pl.multiple_of(first + i * columns, columns), columns)],
            target.at[:, pl.ds(i * columns, columns)],
            sems.at[i],
        )
        for i in range(CUTS)
    ]


def shape(dims, dtype):
    return jax.ShapeDtypeStruct(dims, dtype)


def near(array):
    return pltpu.with_memory_space_constraint(array, pltpu.VMEM)


def distant(array):
    return pltpu.with_memory_space_constraint(array, pltpu.HBM)


def pack(far_query, far_key, far_value, far_tokens, far_gain, heads_ref, *held):
    tokens_ref, gain_ref, *near_refs, packed, sems = held
    far_refs = (far_query, far_key, far_value, far_tokens, far_gain)
    copies = [
        pltpu.make_async_copy(far, ref, sems.at[i])
        for i, (far, ref) in enumerate(zip(far_refs, (*near_refs, tokens_ref, gain_ref)))
    ]
    for copy in copies:
        copy.start()
    for copy in copies:
        copy.wait()
    rows = near_refs[0].shape[0]
    at = 0
    each = heads_ref.shape[0] // rows
    for ref in near_refs:
        block = ref[...].astype(jnp.float32)
        for head in range(ref.shape[1] // HD):
            packed[pl.ds(at, rows, stride=each), :] = block[:, head * HD : (head + 1) * HD]
            at += 1
    heads_ref[...] = packed[...].astype(jnp.bfloat16)


def norm_both(flip, own_ref, got_ref, gain_ref, share, heads, out_ref):
    half = out_ref.shape[1]
    values = stacked([own_ref, got_ref])
    scale = lax.rsqrt(jnp.mean(values * values, axis=-1, keepdims=True) + 1e-05)
    normed = values * scale * gain_ref[...]
    out_ref[...] = jnp.where(side_of(flip) == 0, normed[:, :half], normed[:, half:]).astype(jnp.bfloat16)


def stacked(refs):
    return jnp.concatenate([ref[...].astype(jnp.float32) for ref in refs], axis=0)


def stack(*refs):
    refs[-1][...] = stacked(refs[:-1]).astype(refs[-1].dtype)


def stack_line(own_ref, last_ref, far_ref, got_heads, next_ref, own_heads, out_ref, heads_ref):
    count = own_heads.shape[0]
    heads_ref[:count, :] = own_heads[...]
    heads_ref[count:, :] = got_heads[:count, :]
    rows = [own_ref, far_ref, next_ref, last_ref]
    out_ref[...] = stacked(rows).astype(jnp.bfloat16)


def widen(own_ref, out_ref):
    count = own_ref.shape[0]
    out_ref[:count, :] = own_ref[...]
    out_ref[count:, :] = jnp.zeros((out_ref.shape[0] - count, HD), out_ref.dtype)


def stack_after(own_ref, got_ref, after, out_ref):
    stack(own_ref, got_ref, out_ref)


def grow_both(own_ref, got_ref, own_heads, got_heads, *refs):
    refs[-2][...] = stacked([own_ref, got_ref]).astype(jnp.bfloat16)
    refs[-1][...] = stacked([own_heads, got_heads]).astype(jnp.bfloat16)


def shares(steps, rows, far_routes, far_logits, *refs):
    *_, out_ref, routes_ref, logits_ref, sems = refs
    copies = [
        pltpu.make_async_copy(far_routes, routes_ref, sems.at[0]),
        pltpu.make_async_copy(far_logits, logits_ref, sems.at[1]),
    ]
    for copy in copies:
        copy.start()
    for copy in copies:
        copy.wait()
    count = out_ref.shape[0]
    core = lax.axis_index("narrow")
    me = lax.axis_index("wide")
    logits = logits_ref[...]
    first = 1.0 / (1.0 + jnp.exp(logits[1:2] - logits[0:1]))
    second = 1.0 - first
    chosen = (routes_ref[...] == core).astype(jnp.float32)
    weight_row = chosen[0:1] * first + chosen[1:2] * second
    row = lax.broadcasted_iota(jnp.int32, (count, count), 0)
    column = lax.broadcasted_iota(jnp.int32, (count, count), 1)
    shift = int(math.log2(rows))
    token = (owner_of(row >> shift, me, steps) << shift) | (row & (rows - 1))
    weight = jnp.sum(jnp.where(token == column, weight_row, 0.0), axis=1, keepdims=True)
    out_ref[...] = jnp.broadcast_to(weight, out_ref.shape)


def gate_all(
    flip,
    x_ref,
    other_ref,
    gate_ref,
    up_ref,
    share_ref,
    far_down,
    hidden_out,
    down_own,
    down_other,
    sems,
):
    count, depth = x_ref.shape
    side = side_of(flip)
    other_copies = column_copies(far_down, down_other, sems.at[0], (1 - side) * depth)
    own_copies = column_copies(far_down, down_own, sems.at[1], side * depth)
    for copy in other_copies + own_copies:
        copy.start()
    tile = min(TILE, gate_ref.shape[2])
    own = pl.ds(pl.multiple_of(side * depth, depth), depth)
    other = pl.ds(pl.multiple_of((1 - side) * depth, depth), depth)

    weight = share_ref[:, 0:1]

    @pl.loop(0, gate_ref.shape[2] // tile)
    def _(i):
        columns = pl.ds(pl.multiple_of(i * tile, tile), tile)
        x, y = x_ref[...], other_ref[...]
        gate = jnp.dot(x, gate_ref[0, own, columns], preferred_element_type=jnp.float32)
        gate += jnp.dot(y, gate_ref[0, other, columns], preferred_element_type=jnp.float32)
        up = jnp.dot(x, up_ref[0, own, columns], preferred_element_type=jnp.float32)
        up += jnp.dot(y, up_ref[0, other, columns], preferred_element_type=jnp.float32)
        hidden_out[:, columns] = (weight * (gate * jax.nn.sigmoid(gate)) * up).astype(jnp.bfloat16)

    for copy in other_copies + own_copies:
        copy.wait()


def down(hidden_ref, down_ref, after, out_ref):
    @pl.loop(0, out_ref.shape[1] // WIDE_TILE)
    def _(i):
        columns = pl.ds(pl.multiple_of(i * WIDE_TILE, WIDE_TILE), WIDE_TILE)
        out_ref[:, columns] = jnp.dot(
            hidden_ref[...], down_ref[:, columns], preferred_element_type=jnp.float32
        ).astype(out_ref.dtype)


def part_line(terms_ref, taken_ref, kept_ref, far_ref, next_ref, last_ref):
    total = terms_ref[...] + taken_ref[...].astype(jnp.float32)
    rows = kept_ref.shape[0]
    kept_ref[...] = total[:rows]
    for i, ref in enumerate((far_ref, next_ref, last_ref)):
        ref[...] = total[(i + 1) * rows : (i + 2) * rows].astype(jnp.bfloat16)


def combine(*refs):
    terms_ref, *taken, after, kept_ref, sent_ref = refs
    total = terms_ref[...]
    for ref in taken:
        total = total + ref[...].astype(jnp.float32)
    kept = kept_ref.shape[0]
    kept_ref[...] = total[:kept].astype(kept_ref.dtype)
    sent_ref[...] = total[kept:].astype(jnp.bfloat16)


def finish(flip, kept_ref, taken_ref, other_kept, other_taken, tokens_ref, after, out_ref):
    half = kept_ref.shape[1]
    first = side_of(flip) == 0
    own = kept_ref[...].astype(jnp.float32) + taken_ref[...].astype(jnp.float32)
    other = other_kept[...].astype(jnp.float32) + other_taken[...].astype(jnp.float32)
    tokens = tokens_ref[...].astype(jnp.float32)
    left = tokens[:, :half] + jnp.where(first, own, other)
    right = tokens[:, half:] + jnp.where(first, other, own)
    out_ref[:, :half] = left.astype(jnp.bfloat16)
    out_ref[:, half:] = right.astype(jnp.bfloat16)


def attend(
    steps, taking, near_ref, far_ref, keys_ref, values_ref, lengths_ref, place_ref, after, out_ref
):
    slots, span, width = keys_ref.shape
    rows = slots
    kv_local = width // HD
    heads = kv_local * GROUP
    each = heads + 2 * kv_local
    me = lax.axis_index("wide")
    shift = int(math.log2(rows))
    half = near_ref.shape[0]
    head_of = lax.broadcasted_iota(jnp.int32, (heads, 1), 0)
    positions = lax.broadcasted_iota(jnp.int32, (heads, span), 1)

    def by_group(pieces):
        result = pieces[0]
        for g in range(1, kv_local):
            result = jnp.where(head_of >= g * GROUP, pieces[g], result)
        return result

    for order, slot in enumerate(taking):
        request = place_ref[slot]
        at = (place_of(request >> shift, me, steps) << shift) | (request & (rows - 1))
        at = at * each
        inside = pl.ds(pl.multiple_of(jnp.where(at < half, at, at - half), each), each)
        block = jnp.where(at < half, near_ref[inside, :], far_ref[inside, :])
        query = block[:heads]
        own = block[heads:].astype(jnp.float32)
        own_key = by_group([own[g : g + 1] for g in range(kv_local)])
        own_value = by_group([own[kv_local + g : kv_local + g + 1] for g in range(kv_local)])
        own_score = jnp.sum(query.astype(jnp.float32) * own_key, axis=1, keepdims=True) * SCALE
        scores = by_group(
            [
                lax.dot_general(
                    query,
                    keys_ref[slot, :, g * HD : (g + 1) * HD],
                    (((1,), (1,)), ((), ())),
                    preferred_element_type=jnp.float32,
                )
                for g in range(kv_local)
            ]
        )
        scores = jnp.where(positions < lengths_ref[slot], scores * SCALE, -jnp.inf)
        row_max = jnp.maximum(jnp.max(scores, axis=1, keepdims=True), own_score)
        weights = jnp.exp(scores - row_max)
        own_weight = jnp.exp(own_score - row_max)
        total = jnp.sum(weights, axis=1, keepdims=True) + own_weight
        probs = (weights / total).astype(jnp.bfloat16)
        own_prob = (own_weight / total).astype(jnp.bfloat16).astype(jnp.float32)
        mixed = by_group(
            [
                jnp.dot(
                    probs,
                    values_ref[slot, :, g * HD : (g + 1) * HD],
                    preferred_element_type=jnp.float32,
                )
                for g in range(kv_local)
            ]
        )
        out_ref[order * heads : (order + 1) * heads, :] = mixed + own_prob * own_value


def lay_out(heads, pieces, out_ref, held):
    at = 0
    for piece in pieces:
        held[at : at + piece.shape[0], :] = piece[...]
        at += piece.shape[0]
    for head in range(heads):
        out_ref[:, head * HD : (head + 1) * HD] = held[
            pl.ds(head, out_ref.shape[0], stride=heads), :
        ].astype(jnp.bfloat16)


def attend_last(steps, taking, heads, *refs):
    *ins, early, out_ref, late, held = refs
    attend(steps, taking, *ins, late)
    lay_out(heads, [early, late], out_ref, held)


def make_local(wide):
    steps = steps_of(wide)
    head_steps = [*steps[1:-2], steps[-1], steps[-2], steps[0]]

    def local(
        queries,
        new_keys,
        new_values,
        key_cache,
        value_cache,
        lengths,
        assignment,
        tokens,
        norm_gain,
        routes,
        route_logits,
        w_gate,
        w_up,
        w_down,
    ):
        rows, width = tokens.shape
        half = width // 2
        units = w_gate.shape[2]
        count = rows * wide
        each = (queries.shape[1] + 2 * new_keys.shape[1]) // HD
        core = lax.axis_index("narrow")
        bf16, f32 = jnp.bfloat16, jnp.float32
        heads_local = queries.shape[1] // HD
        dma = pltpu.SemaphoreType.DMA
        piece_bytes = 2 * half * units

        got = cross(tokens, wide, steps[0])
        heads_in = [queries, new_keys, new_values]
        row_in = [tokens, norm_gain[None]]
        heads, *row_near = call(
            pack,
            [shape((rows * each, HD), bf16)] + [pltpu.VMEM(a.shape, a.dtype) for a in row_in],
            [distant(a) for a in heads_in + row_in],
            [pltpu.VMEM(a.shape, a.dtype) for a in heads_in]
            + [pltpu.VMEM((rows * each, HD), f32), dma((5,))],
            size=100000,
            far=range(5),
        )
        share = call(
            functools.partial(shares, steps, rows),
            shape((count, HD), f32),
            [distant(routes.T), distant(route_logits.T), heads, distant(w_gate), distant(w_up)],
            [
                pltpu.VMEM(routes.T.shape, jnp.int32),
                pltpu.VMEM(route_logits.T.shape, f32),
                dma((2,)),
            ],
            size=100000,
            far=range(5),
        )
        x = call(
            functools.partial(norm_both, steps[-2]),
            shape((2 * rows, half), bf16),
            [near(row_near[0]), got, near(row_near[1]), share, heads],
            size=100000,
            far=(3, 4),
        )

        def grown(heads, step):
            got = swap(heads, "wide", wide, step)
            return call(
                stack, shape((2 * heads.shape[0], HD), bf16), [heads, got], size=4 * heads.size
            )

        for step in steps[1:-2]:
            heads = grown(heads, step)
            x = call(
                stack_after,
                shape((2 * x.shape[0], half), bf16),
                [x, swap(x, "wide", wide, step), heads],
                size=8 * x.size,
                far=(2,),
            )
        line_steps = [steps[-2], steps[-1], steps[-2] ^ steps[-1]]
        last = cross(x, wide, line_steps[2])
        line = [cross(x, wide, line_steps[0]), swap(x, "wide", wide, line_steps[1])]
        wider = max(x.shape[0] * half // HD, heads.shape[0])
        sent_heads = call(widen, shape((wider, HD), bf16), [heads], size=4 * wider * HD)
        far_rows = swap(sent_heads, "wide", wide, steps[-1])
        x, heads = call(
            stack_line,
            [shape((count, half), bf16), shape((2 * heads.shape[0], HD), bf16)],
            [x, last, line[0], far_rows, line[1], heads],
            size=8 * count * half,
        )
        got_heads = swap(heads, "wide", wide, steps[-2])

        product = 2 * count * half * units
        other_x = swap(x, "narrow", 2, 1)
        whole = pltpu.VMEM((units, half), bf16)
        hidden, down_own, down_other = call(
            functools.partial(gate_all, steps[-2]),
            [shape((count, units), bf16), whole, whole],
            [
                x,
                other_x,
                near(w_gate),
                near(w_up),
                share,
                distant(w_down),
            ],
            [dma((2, CUTS))],
            flops=4 * product,
            size=6 * piece_bytes,
            far=(5,),
        )
        heads = call(
            stack_after,
            shape((2 * heads.shape[0], HD), bf16),
            [heads, got_heads, hidden],
            size=8 * heads.size,
            far=(2,),
        )
        given = call(
            down,
            shape((count, half), bf16),
            [hidden, near(down_other), heads],
            flops=product,
            size=piece_bytes,
            far=(2,),
        )
        taken = swap(given, "narrow", 2, 1)
        far_heads = swap(heads, "wide", wide, steps[0])
        terms = call(
            down,
            shape((count, half), f32),
            [hidden, near(down_own), given],
            flops=product,
            size=piece_bytes,
            far=(2,),
        )

        caches = [near(key_cache), near(value_cache), lengths, assignment]
        slots = queries.shape[0]
        early_slots = list(range(slots - 1))
        late_slots = list(range(slots - 1, slots))
        quarter = count // 4
        block = shape((quarter, half), bf16)
        terms, *sent = call(
            part_line,
            [shape((quarter, half), f32), block, block, block],
            [terms, taken],
            size=terms.size * 8,
        )
        taken = [
            swap(sent[1], "wide", wide, line_steps[1]),
            cross(sent[2], wide, line_steps[2]),
            cross(sent[0], wide, line_steps[0]),
        ]
        early = call(
            functools.partial(attend, head_steps, early_slots),
            shape((len(early_slots) * heads_local, HD), f32),
            [heads, far_heads, *caches, sent[0]],
            flops=2 * key_cache.size * GROUP,
            size=2 * key_cache.size,
            smem=(4, 5),
            far=(6,),
        )
        for step in reversed(steps[:-2]):
            kept = terms.shape[0] // 2
            terms, sent = call(
                combine,
                [shape((kept, half), bf16 if kept == rows else f32), shape((kept, half), bf16)],
                [terms, *taken, early],
                size=terms.size * 8,
                far=(1 + len(taken),),
            )
            taken = [swap(sent, "wide", wide, step)]
        context = call(
            functools.partial(attend_last, head_steps, late_slots, heads_local),
            shape(queries.shape, bf16),
            [heads, far_heads, *caches, sent, early],
            [
                pltpu.VMEM((len(late_slots) * heads_local, HD), f32),
                pltpu.VMEM((slots * heads_local, HD), f32),
            ],
            flops=2 * key_cache.size * GROUP,
            size=2 * key_cache.size,
            smem=(4, 5),
            far=(6,),
        )
        other_kept = swap(terms, "narrow", 2, 1)
        other_taken = cross(sent, wide, steps[0])
        mixed_out = call(
            functools.partial(finish, steps[-2]),
            shape((rows, width), bf16),
            [terms, *taken, other_kept, other_taken, tokens, distant(context)],
            size=terms.size * 8,
            far=(5,),
        )
        return (context, mixed_out)

    return local


def solution(mesh):
    placed = (
        P(("groups", "wide"), "narrow"),
        P(("groups", "wide"), "narrow"),
        P(("groups", "wide"), "narrow"),
        P(("groups", "wide"), None, "narrow"),
        P(("groups", "wide"), None, "narrow"),
        P(("groups", "wide")),
        P(("groups", "wide")),
        P(("groups", "wide"), None),
        P(),
        P("groups", None),
        P("groups", None),
        P("narrow", None, "wide"),
        P("narrow", None, "wide"),
        P("narrow", "wide", None),
    )
    return jax.shard_map(
        make_local(mesh.shape["wide"]),
        mesh=mesh,
        in_specs=placed,
        out_specs=(P(("groups", "wide"), "narrow"), P(("groups", "wide"), None)),
        check_vma=False,
    )
```

```python
import functools
import math

import jax
import jax.numpy as jnp
from jax import lax
from jax.experimental import pallas as pl
from jax.experimental.pallas import tpu as pltpu
from jax.sharding import PartitionSpec as P

HQ = 48
KVH = 8
HD = 128
GROUP = HQ // KVH
SCALE = HD ** (-0.5)
TILE = 512
WIDE_TILE = 1536
CUTS = 4
MIB = 1024 * 1024


def steps_of(wide):
    bits = int(math.log2(wide))
    return [1 << i for i in range(bits - 2)] + [wide >> 1, wide >> 2]


def swap(block, axis, count, step):
    return lax.ppermute(block, axis, [(i, i ^ step) for i in range(count)])


def cross(block, wide, step):
    pairs = [(2 * i + c, 2 * (i ^ step) + 1 - c) for i in range(wide) for c in range(2)]
    return lax.ppermute(block, ("wide", "narrow"), pairs)


def side_of(flip):
    bit = (lax.axis_index("wide") // flip) % 2
    return lax.axis_index("narrow") ^ bit


def owner_of(place, me, steps):
    found = me
    for bit, step in enumerate(steps):
        found = found ^ (((place >> bit) & 1) * step)
    return found


def place_of(owner, me, steps):
    differ = owner ^ me
    found = 0
    for bit, step in enumerate(steps):
        shift = int(math.log2(step))
        found = found | (((differ >> shift) & 1) << bit)
    return found


def call(kernel, outs, ins, scratch=(), flops=0, size=0, limit=4, smem=(), far=()):
    spaces = [pltpu.SMEM if i in smem else pl.ANY if i in far else pltpu.VMEM for i in range(len(ins))]
    return pl.pallas_call(
        kernel,
        name=getattr(kernel, "func", kernel).__name__,
        out_shape=outs,
        in_specs=[pl.BlockSpec(memory_space=space) for space in spaces],
        out_specs=jax.tree.map(lambda _: pl.BlockSpec(memory_space=pltpu.VMEM), outs),
        scratch_shapes=list(scratch),
        compiler_params=pltpu.CompilerParams(vmem_limit_bytes=limit * MIB),
        cost_estimate=pl.CostEstimate(flops=flops, bytes_accessed=size, transcendentals=0),
    )(*ins)


def column_copies(source, target, sems, first):
    columns = target.shape[1] // CUTS
    return [
        pltpu.make_async_copy(
            source.at[0, :, pl.ds(pl.multiple_of(first + i * columns, columns), columns)],
            target.at[:, pl.ds(i * columns, columns)],
            sems.at[i],
        )
        for i in range(CUTS)
    ]


def shape(dims, dtype):
    return jax.ShapeDtypeStruct(dims, dtype)


def near(array):
    return pltpu.with_memory_space_constraint(array, pltpu.VMEM)


def distant(array):
    return pltpu.with_memory_space_constraint(array, pltpu.HBM)


def pack(far_query, far_key, far_value, far_tokens, far_gain, heads_ref, *held):
    tokens_ref, gain_ref, *near_refs, packed, sems = held
    far_refs = (far_query, far_key, far_value, far_tokens, far_gain)
    copies = [
        pltpu.make_async_copy(far, ref, sems.at[i])
        for i, (far, ref) in enumerate(zip(far_refs, (*near_refs, tokens_ref, gain_ref)))
    ]
    for copy in copies:
        copy.start()
    for copy in copies:
        copy.wait()
    rows = near_refs[0].shape[0]
    at = 0
    each = heads_ref.shape[0] // rows
    for ref in near_refs:
        block = ref[...].astype(jnp.float32)
        for head in range(ref.shape[1] // HD):
            packed[pl.ds(at, rows, stride=each), :] = block[:, head * HD : (head + 1) * HD]
            at += 1
    heads_ref[...] = packed[...].astype(jnp.bfloat16)


def norm_both(flip, own_ref, got_ref, gain_ref, share, heads, out_ref):
    half = out_ref.shape[1]
    values = stacked([own_ref, got_ref])
    scale = lax.rsqrt(jnp.mean(values * values, axis=-1, keepdims=True) + 1e-05)
    normed = values * scale * gain_ref[...]
    out_ref[...] = jnp.where(side_of(flip) == 0, normed[:, :half], normed[:, half:]).astype(jnp.bfloat16)


def stacked(refs):
    return jnp.concatenate([ref[...].astype(jnp.float32) for ref in refs], axis=0)


def stack(*refs):
    refs[-1][...] = stacked(refs[:-1]).astype(refs[-1].dtype)


def stack_line(own_ref, last_ref, far_ref, got_heads, next_ref, own_heads, out_ref, heads_ref):
    count = own_heads.shape[0]
    heads_ref[:count, :] = own_heads[...]
    heads_ref[count:, :] = got_heads[:count, :]
    rows = [own_ref, far_ref, next_ref, last_ref]
    out_ref[...] = stacked(rows).astype(jnp.bfloat16)


def widen(own_ref, out_ref):
    count = own_ref.shape[0]
    out_ref[:count, :] = own_ref[...]
    out_ref[count:, :] = jnp.zeros((out_ref.shape[0] - count, HD), out_ref.dtype)


def stack_after(own_ref, got_ref, after, out_ref):
    stack(own_ref, got_ref, out_ref)


def grow_both(own_ref, got_ref, own_heads, got_heads, *refs):
    refs[-2][...] = stacked([own_ref, got_ref]).astype(jnp.bfloat16)
    refs[-1][...] = stacked([own_heads, got_heads]).astype(jnp.bfloat16)


def shares(steps, rows, far_routes, far_logits, *refs):
    *_, out_ref, routes_ref, logits_ref, sems = refs
    copies = [
        pltpu.make_async_copy(far_routes, routes_ref, sems.at[0]),
        pltpu.make_async_copy(far_logits, logits_ref, sems.at[1]),
    ]
    for copy in copies:
        copy.start()
    for copy in copies:
        copy.wait()
    count = out_ref.shape[0]
    core = lax.axis_index("narrow")
    me = lax.axis_index("wide")
    logits = logits_ref[...]
    first = 1.0 / (1.0 + jnp.exp(logits[1:2] - logits[0:1]))
    second = 1.0 - first
    chosen = (routes_ref[...] == core).astype(jnp.float32)
    weight_row = chosen[0:1] * first + chosen[1:2] * second
    row = lax.broadcasted_iota(jnp.int32, (count, count), 0)
    column = lax.broadcasted_iota(jnp.int32, (count, count), 1)
    shift = int(math.log2(rows))
    token = (owner_of(row >> shift, me, steps) << shift) | (row & (rows - 1))
    weight = jnp.sum(jnp.where(token == column, weight_row, 0.0), axis=1, keepdims=True)
    out_ref[...] = jnp.broadcast_to(weight, out_ref.shape)


def gate_all(
    flip,
    x_ref,
    other_ref,
    gate_ref,
    up_ref,
    share_ref,
    far_down,
    hidden_out,
    down_own,
    down_other,
    sems,
):
    count, depth = x_ref.shape
    side = side_of(flip)
    other_copies = column_copies(far_down, down_other, sems.at[0], (1 - side) * depth)
    own_copies = column_copies(far_down, down_own, sems.at[1], side * depth)
    for copy in other_copies + own_copies:
        copy.start()
    tile = min(TILE, gate_ref.shape[2])
    own = pl.ds(pl.multiple_of(side * depth, depth), depth)
    other = pl.ds(pl.multiple_of((1 - side) * depth, depth), depth)

    weight = share_ref[:, 0:1]

    @pl.loop(0, gate_ref.shape[2] // tile)
    def _(i):
        columns = pl.ds(pl.multiple_of(i * tile, tile), tile)
        x, y = x_ref[...], other_ref[...]
        gate = jnp.dot(x, gate_ref[0, own, columns], preferred_element_type=jnp.float32)
        gate += jnp.dot(y, gate_ref[0, other, columns], preferred_element_type=jnp.float32)
        up = jnp.dot(x, up_ref[0, own, columns], preferred_element_type=jnp.float32)
        up += jnp.dot(y, up_ref[0, other, columns], preferred_element_type=jnp.float32)
        hidden_out[:, columns] = (weight * (gate * jax.nn.sigmoid(gate)) * up).astype(jnp.bfloat16)

    for copy in other_copies + own_copies:
        copy.wait()


def down(hidden_ref, down_ref, after, out_ref):
    @pl.loop(0, out_ref.shape[1] // WIDE_TILE)
    def _(i):
        columns = pl.ds(pl.multiple_of(i * WIDE_TILE, WIDE_TILE), WIDE_TILE)
        out_ref[:, columns] = jnp.dot(
            hidden_ref[...], down_ref[:, columns], preferred_element_type=jnp.float32
        ).astype(out_ref.dtype)


def part_line(terms_ref, taken_ref, kept_ref, far_ref, next_ref, last_ref):
    total = terms_ref[...] + taken_ref[...].astype(jnp.float32)
    rows = kept_ref.shape[0]
    kept_ref[...] = total[:rows]
    for i, ref in enumerate((far_ref, next_ref, last_ref)):
        ref[...] = total[(i + 1) * rows : (i + 2) * rows].astype(jnp.bfloat16)


def combine(*refs):
    terms_ref, *taken, after, kept_ref, sent_ref = refs
    total = terms_ref[...]
    for ref in taken:
        total = total + ref[...].astype(jnp.float32)
    kept = kept_ref.shape[0]
    kept_ref[...] = total[:kept].astype(kept_ref.dtype)
    sent_ref[...] = total[kept:].astype(jnp.bfloat16)


def finish(flip, kept_ref, taken_ref, other_taken, other_kept, tokens_ref, after, out_ref):
    half = kept_ref.shape[1]
    first = side_of(flip) == 0
    own = kept_ref[...].astype(jnp.float32) + taken_ref[...].astype(jnp.float32)
    other = other_kept[...].astype(jnp.float32) + other_taken[...].astype(jnp.float32)
    tokens = tokens_ref[...].astype(jnp.float32)
    left = tokens[:, :half] + jnp.where(first, own, other)
    right = tokens[:, half:] + jnp.where(first, other, own)
    out_ref[:, :half] = left.astype(jnp.bfloat16)
    out_ref[:, half:] = right.astype(jnp.bfloat16)


def attend(
    steps, taking, near_ref, far_ref, keys_ref, values_ref, lengths_ref, place_ref, after, out_ref
):
    slots, span, width = keys_ref.shape
    rows = slots
    kv_local = width // HD
    heads = kv_local * GROUP
    each = heads + 2 * kv_local
    me = lax.axis_index("wide")
    shift = int(math.log2(rows))
    half = near_ref.shape[0]
    head_of = lax.broadcasted_iota(jnp.int32, (heads, 1), 0)
    positions = lax.broadcasted_iota(jnp.int32, (heads, span), 1)

    def by_group(pieces):
        result = pieces[0]
        for g in range(1, kv_local):
            result = jnp.where(head_of >= g * GROUP, pieces[g], result)
        return result

    for order, slot in enumerate(taking):
        request = place_ref[slot]
        at = (place_of(request >> shift, me, steps) << shift) | (request & (rows - 1))
        at = at * each
        inside = pl.ds(pl.multiple_of(jnp.where(at < half, at, at - half), each), each)
        block = jnp.where(at < half, near_ref[inside, :], far_ref[inside, :])
        query = block[:heads]
        own = block[heads:].astype(jnp.float32)
        own_key = by_group([own[g : g + 1] for g in range(kv_local)])
        own_value = by_group([own[kv_local + g : kv_local + g + 1] for g in range(kv_local)])
        own_score = jnp.sum(query.astype(jnp.float32) * own_key, axis=1, keepdims=True) * SCALE
        scores = by_group(
            [
                lax.dot_general(
                    query,
                    keys_ref[slot, :, g * HD : (g + 1) * HD],
                    (((1,), (1,)), ((), ())),
                    preferred_element_type=jnp.float32,
                )
                for g in range(kv_local)
            ]
        )
        scores = jnp.where(positions < lengths_ref[slot], scores * SCALE, -jnp.inf)
        row_max = jnp.maximum(jnp.max(scores, axis=1, keepdims=True), own_score)
        weights = jnp.exp(scores - row_max)
        own_weight = jnp.exp(own_score - row_max)
        total = jnp.sum(weights, axis=1, keepdims=True) + own_weight
        probs = (weights / total).astype(jnp.bfloat16)
        own_prob = (own_weight / total).astype(jnp.bfloat16).astype(jnp.float32)
        mixed = by_group(
            [
                jnp.dot(
                    probs,
                    values_ref[slot, :, g * HD : (g + 1) * HD],
                    preferred_element_type=jnp.float32,
                )
                for g in range(kv_local)
            ]
        )
        out_ref[order * heads : (order + 1) * heads, :] = mixed + own_prob * own_value


def lay_out(heads, pieces, out_ref, held):
    at = 0
    for piece in pieces:
        held[at : at + piece.shape[0], :] = piece[...]
        at += piece.shape[0]
    for head in range(heads):
        out_ref[:, head * HD : (head + 1) * HD] = held[
            pl.ds(head, out_ref.shape[0], stride=heads), :
        ].astype(jnp.bfloat16)


def attend_last(steps, taking, heads, *refs):
    *ins, early, out_ref, late, held = refs
    attend(steps, taking, *ins, late)
    lay_out(heads, [early, late], out_ref, held)


def make_local(wide):
    steps = steps_of(wide)
    head_steps = [*steps[1:-2], *steps[:1], *steps[-2:]]

    def local(
        queries,
        new_keys,
        new_values,
        key_cache,
        value_cache,
        lengths,
        assignment,
        tokens,
        norm_gain,
        routes,
        route_logits,
        w_gate,
        w_up,
        w_down,
    ):
        rows, width = tokens.shape
        half = width // 2
        units = w_gate.shape[2]
        count = rows * wide
        each = (queries.shape[1] + 2 * new_keys.shape[1]) // HD
        core = lax.axis_index("narrow")
        bf16, f32 = jnp.bfloat16, jnp.float32
        heads_local = queries.shape[1] // HD
        dma = pltpu.SemaphoreType.DMA
        piece_bytes = 2 * half * units

        got = cross(tokens, wide, steps[0])
        heads_in = [queries, new_keys, new_values]
        row_in = [tokens, norm_gain[None]]
        heads, *row_near = call(
            pack,
            [shape((rows * each, HD), bf16)] + [pltpu.VMEM(a.shape, a.dtype) for a in row_in],
            [distant(a) for a in heads_in + row_in],
            [pltpu.VMEM(a.shape, a.dtype) for a in heads_in]
            + [pltpu.VMEM((rows * each, HD), f32), dma((5,))],
            size=100000,
            far=range(5),
        )
        share = call(
            functools.partial(shares, steps, rows),
            shape((count, HD), f32),
            [distant(routes.T), distant(route_logits.T), heads, distant(w_gate), distant(w_up)],
            [
                pltpu.VMEM(routes.T.shape, jnp.int32),
                pltpu.VMEM(route_logits.T.shape, f32),
                dma((2,)),
            ],
            size=100000,
            far=range(5),
        )
        x = call(
            functools.partial(norm_both, steps[-1]),
            shape((2 * rows, half), bf16),
            [near(row_near[0]), got, near(row_near[1]), share, heads],
            size=100000,
            far=(3, 4),
        )

        def grown(heads, step):
            got = swap(heads, "wide", wide, step)
            return call(
                stack, shape((2 * heads.shape[0], HD), bf16), [heads, got], size=4 * heads.size
            )

        for step in steps[1:-2]:
            heads = grown(heads, step)
            x = call(
                stack_after,
                shape((2 * x.shape[0], half), bf16),
                [x, swap(x, "wide", wide, step), heads],
                size=8 * x.size,
                far=(2,),
            )
        line_steps = [steps[-2], steps[-1], steps[-2] ^ steps[-1]]
        last = cross(x, wide, line_steps[2])
        line = [swap(x, "wide", wide, line_steps[0]), cross(x, wide, line_steps[1])]
        wider = max(x.shape[0] * half // HD, heads.shape[0])
        sent_heads = call(widen, shape((wider, HD), bf16), [heads], size=4 * wider * HD)
        far_rows = swap(sent_heads, "wide", wide, steps[0])
        x, heads = call(
            stack_line,
            [shape((count, half), bf16), shape((2 * heads.shape[0], HD), bf16)],
            [x, last, line[0], far_rows, line[1], heads],
            size=8 * count * half,
        )
        got_heads = swap(heads, "wide", wide, steps[-2])

        product = 2 * count * half * units
        other_x = swap(x, "narrow", 2, 1)
        whole = pltpu.VMEM((units, half), bf16)
        hidden, down_own, down_other = call(
            functools.partial(gate_all, steps[-1]),
            [shape((count, units), bf16), whole, whole],
            [
                x,
                other_x,
                near(w_gate),
                near(w_up),
                share,
                distant(w_down),
            ],
            [dma((2, CUTS))],
            flops=4 * product,
            size=6 * piece_bytes,
            far=(5,),
        )
        heads = call(
            stack_after,
            shape((2 * heads.shape[0], HD), bf16),
            [heads, got_heads, hidden],
            size=8 * heads.size,
            far=(2,),
        )
        given = call(
            down,
            shape((count, half), bf16),
            [hidden, near(down_other), heads],
            flops=product,
            size=piece_bytes,
            far=(2,),
        )
        taken = swap(given, "narrow", 2, 1)
        far_heads = swap(heads, "wide", wide, steps[-1])
        terms = call(
            down,
            shape((count, half), f32),
            [hidden, near(down_own), given],
            flops=product,
            size=piece_bytes,
            far=(2,),
        )

        caches = [near(key_cache), near(value_cache), lengths, assignment]
        slots = queries.shape[0]
        early_slots = list(range(slots - 1))
        late_slots = list(range(slots - 1, slots))
        quarter = count // 4
        block = shape((quarter, half), bf16)
        terms, *sent = call(
            part_line,
            [shape((quarter, half), f32), block, block, block],
            [terms, taken],
            size=terms.size * 8,
        )
        taken = [
            cross(sent[1], wide, line_steps[1]),
            cross(sent[2], wide, line_steps[2]),
            swap(sent[0], "wide", wide, line_steps[0]),
        ]
        early = call(
            functools.partial(attend, head_steps, early_slots),
            shape((len(early_slots) * heads_local, HD), f32),
            [heads, far_heads, *caches, sent[0]],
            flops=2 * key_cache.size * GROUP,
            size=2 * key_cache.size,
            smem=(4, 5),
            far=(6,),
        )
        for step in reversed(steps[:-2]):
            kept = terms.shape[0] // 2
            terms, sent = call(
                combine,
                [shape((kept, half), bf16 if kept == rows else f32), shape((kept, half), bf16)],
                [terms, *taken, early],
                size=terms.size * 8,
                far=(1 + len(taken),),
            )
            taken = [swap(sent, "wide", wide, step)]
        context = call(
            functools.partial(attend_last, head_steps, late_slots, heads_local),
            shape(queries.shape, bf16),
            [heads, far_heads, *caches, terms, early],
            [
                pltpu.VMEM((len(late_slots) * heads_local, HD), f32),
                pltpu.VMEM((slots * heads_local, HD), f32),
            ],
            flops=2 * key_cache.size * GROUP,
            size=2 * key_cache.size,
            smem=(4, 5),
            far=(6,),
        )
        other_kept = swap(terms, "narrow", 2, 1)
        other_taken = cross(sent, wide, steps[0])
        mixed_out = call(
            functools.partial(finish, steps[-1]),
            shape((rows, width), bf16),
            [terms, *taken, other_taken, other_kept, tokens, distant(context)],
            size=terms.size * 8,
            far=(5,),
        )
        return (context, mixed_out)

    return local


def solution(mesh):
    placed = (
        P(("groups", "wide"), "narrow"),
        P(("groups", "wide"), "narrow"),
        P(("groups", "wide"), "narrow"),
        P(("groups", "wide"), None, "narrow"),
        P(("groups", "wide"), None, "narrow"),
        P(("groups", "wide")),
        P(("groups", "wide")),
        P(("groups", "wide"), None),
        P(),
        P("groups", None),
        P("groups", None),
        P("narrow", None, "wide"),
        P("narrow", None, "wide"),
        P("narrow", "wide", None),
    )
    return jax.shard_map(
        make_local(mesh.shape["wide"]),
        mesh=mesh,
        in_specs=placed,
        out_specs=(P(("groups", "wide"), "narrow"), P(("groups", "wide"), None)),
        check_vma=False,
    )
```

```python
import functools
import math

import jax
import jax.numpy as jnp
from jax import lax
from jax.experimental import pallas as pl
from jax.experimental.pallas import tpu as pltpu
from jax.sharding import PartitionSpec as P

HQ = 48
KVH = 8
HD = 128
GROUP = HQ // KVH
SCALE = HD ** (-0.5)
TILE = 512
WIDE_TILE = 3072
CUTS = 4
MIB = 1024 * 1024


def steps_of(wide):
    bits = int(math.log2(wide))
    return [1 << i for i in range(bits - 2)] + [wide >> 1, wide >> 2]


def swap(block, axis, count, step):
    return lax.ppermute(block, axis, [(i, i ^ step) for i in range(count)])


def cross(block, wide, step):
    pairs = [(2 * i + c, 2 * (i ^ step) + 1 - c) for i in range(wide) for c in range(2)]
    return lax.ppermute(block, ("wide", "narrow"), pairs)


def side_of(flip):
    bit = (lax.axis_index("wide") // flip) % 2
    return lax.axis_index("narrow") ^ bit


def owner_of(place, me, steps):
    found = me
    for bit, step in enumerate(steps):
        found = found ^ (((place >> bit) & 1) * step)
    return found


def place_of(owner, me, steps):
    differ = owner ^ me
    found = 0
    for bit, step in enumerate(steps):
        shift = int(math.log2(step))
        found = found | (((differ >> shift) & 1) << bit)
    return found


def call(kernel, outs, ins, scratch=(), flops=0, size=0, limit=4, smem=(), far=()):
    spaces = [pltpu.SMEM if i in smem else pl.ANY if i in far else pltpu.VMEM for i in range(len(ins))]
    return pl.pallas_call(
        kernel,
        name=getattr(kernel, "func", kernel).__name__,
        out_shape=outs,
        in_specs=[pl.BlockSpec(memory_space=space) for space in spaces],
        out_specs=jax.tree.map(lambda _: pl.BlockSpec(memory_space=pltpu.VMEM), outs),
        scratch_shapes=list(scratch),
        compiler_params=pltpu.CompilerParams(vmem_limit_bytes=limit * MIB),
        cost_estimate=pl.CostEstimate(flops=flops, bytes_accessed=size, transcendentals=0),
    )(*ins)


def column_copies(source, target, sems, first):
    columns = target.shape[1] // CUTS
    return [
        pltpu.make_async_copy(
            source.at[0, :, pl.ds(pl.multiple_of(first + i * columns, columns), columns)],
            target.at[:, pl.ds(i * columns, columns)],
            sems.at[i],
        )
        for i in range(CUTS)
    ]


def shape(dims, dtype):
    return jax.ShapeDtypeStruct(dims, dtype)


def near(array):
    return pltpu.with_memory_space_constraint(array, pltpu.VMEM)


def distant(array):
    return pltpu.with_memory_space_constraint(array, pltpu.HBM)


def pack(far_query, far_key, far_value, far_tokens, far_gain, heads_ref, *held):
    tokens_ref, gain_ref, *near_refs, packed, sems = held
    far_refs = (far_query, far_key, far_value, far_tokens, far_gain)
    copies = [
        pltpu.make_async_copy(far, ref, sems.at[i])
        for i, (far, ref) in enumerate(zip(far_refs, (*near_refs, tokens_ref, gain_ref)))
    ]
    for copy in copies:
        copy.start()
    for copy in copies:
        copy.wait()
    rows = near_refs[0].shape[0]
    at = 0
    each = heads_ref.shape[0] // rows
    for ref in near_refs:
        block = ref[...].astype(jnp.float32)
        for head in range(ref.shape[1] // HD):
            packed[pl.ds(at, rows, stride=each), :] = block[:, head * HD : (head + 1) * HD]
            at += 1
    heads_ref[...] = packed[...].astype(jnp.bfloat16)


def norm_both(flip, own_ref, got_ref, gain_ref, share, heads, out_ref):
    half = out_ref.shape[1]
    values = stacked([own_ref, got_ref])
    scale = lax.rsqrt(jnp.mean(values * values, axis=-1, keepdims=True) + 1e-05)
    normed = values * scale * gain_ref[...]
    out_ref[...] = jnp.where(side_of(flip) == 0, normed[:, :half], normed[:, half:]).astype(jnp.bfloat16)


def stacked(refs):
    return jnp.concatenate([ref[...].astype(jnp.float32) for ref in refs], axis=0)


def stack(*refs):
    refs[-1][...] = stacked(refs[:-1]).astype(refs[-1].dtype)


def stack_line(own_ref, last_ref, far_ref, got_heads, next_ref, own_heads, out_ref, heads_ref):
    count = own_heads.shape[0]
    heads_ref[:count, :] = own_heads[...]
    heads_ref[count:, :] = got_heads[:count, :]
    rows = [own_ref, far_ref, next_ref, last_ref]
    out_ref[...] = stacked(rows).astype(jnp.bfloat16)


def widen(own_ref, out_ref):
    count = own_ref.shape[0]
    out_ref[:count, :] = own_ref[...]
    out_ref[count:, :] = jnp.zeros((out_ref.shape[0] - count, HD), out_ref.dtype)


def stack_after(own_ref, got_ref, after, out_ref):
    stack(own_ref, got_ref, out_ref)


def grow_both(own_ref, got_ref, own_heads, got_heads, *refs):
    refs[-2][...] = stacked([own_ref, got_ref]).astype(jnp.bfloat16)
    refs[-1][...] = stacked([own_heads, got_heads]).astype(jnp.bfloat16)


def shares(steps, rows, far_routes, far_logits, *refs):
    *_, out_ref, routes_ref, logits_ref, sems = refs
    copies = [
        pltpu.make_async_copy(far_routes, routes_ref, sems.at[0]),
        pltpu.make_async_copy(far_logits, logits_ref, sems.at[1]),
    ]
    for copy in copies:
        copy.start()
    for copy in copies:
        copy.wait()
    count = out_ref.shape[0]
    core = lax.axis_index("narrow")
    me = lax.axis_index("wide")
    logits = logits_ref[...]
    first = 1.0 / (1.0 + jnp.exp(logits[1:2] - logits[0:1]))
    second = 1.0 - first
    chosen = (routes_ref[...] == core).astype(jnp.float32)
    weight_row = chosen[0:1] * first + chosen[1:2] * second
    row = lax.broadcasted_iota(jnp.int32, (count, count), 0)
    column = lax.broadcasted_iota(jnp.int32, (count, count), 1)
    shift = int(math.log2(rows))
    token = (owner_of(row >> shift, me, steps) << shift) | (row & (rows - 1))
    weight = jnp.sum(jnp.where(token == column, weight_row, 0.0), axis=1, keepdims=True)
    out_ref[...] = jnp.broadcast_to(weight, out_ref.shape)


def gate_all(
    flip,
    x_ref,
    other_ref,
    gate_ref,
    up_ref,
    share_ref,
    far_down,
    hidden_out,
    down_own,
    down_other,
    sems,
):
    count, depth = x_ref.shape
    side = side_of(flip)
    other_copies = column_copies(far_down, down_other, sems.at[0], (1 - side) * depth)
    own_copies = column_copies(far_down, down_own, sems.at[1], side * depth)
    for copy in other_copies + own_copies:
        copy.start()
    tile = min(TILE, gate_ref.shape[2])
    own = pl.ds(pl.multiple_of(side * depth, depth), depth)
    other = pl.ds(pl.multiple_of((1 - side) * depth, depth), depth)

    weight = share_ref[:, 0:1]

    @pl.loop(0, gate_ref.shape[2] // tile)
    def _(i):
        columns = pl.ds(pl.multiple_of(i * tile, tile), tile)
        x, y = x_ref[...], other_ref[...]
        gate = jnp.dot(x, gate_ref[0, own, columns], preferred_element_type=jnp.float32)
        gate += jnp.dot(y, gate_ref[0, other, columns], preferred_element_type=jnp.float32)
        up = jnp.dot(x, up_ref[0, own, columns], preferred_element_type=jnp.float32)
        up += jnp.dot(y, up_ref[0, other, columns], preferred_element_type=jnp.float32)
        hidden_out[:, columns] = (weight * (gate * jax.nn.sigmoid(gate)) * up).astype(jnp.bfloat16)

    for copy in other_copies + own_copies:
        copy.wait()


def down(hidden_ref, down_ref, after, out_ref):
    @pl.loop(0, out_ref.shape[1] // WIDE_TILE)
    def _(i):
        columns = pl.ds(pl.multiple_of(i * WIDE_TILE, WIDE_TILE), WIDE_TILE)
        out_ref[:, columns] = jnp.dot(
            hidden_ref[...], down_ref[:, columns], preferred_element_type=jnp.float32
        ).astype(out_ref.dtype)


def part_line(terms_ref, taken_ref, kept_ref, far_ref, next_ref, last_ref):
    total = terms_ref[...] + taken_ref[...].astype(jnp.float32)
    rows = kept_ref.shape[0]
    kept_ref[...] = total[:rows]
    for i, ref in enumerate((far_ref, next_ref, last_ref)):
        ref[...] = total[(i + 1) * rows : (i + 2) * rows].astype(jnp.bfloat16)


def combine(*refs):
    terms_ref, *taken, after, kept_ref, sent_ref = refs
    total = terms_ref[...]
    for ref in taken:
        total = total + ref[...].astype(jnp.float32)
    kept = kept_ref.shape[0]
    kept_ref[...] = total[:kept].astype(kept_ref.dtype)
    sent_ref[...] = total[kept:].astype(jnp.bfloat16)


def finish(flip, kept_ref, taken_ref, other_kept, other_taken, tokens_ref, after, out_ref):
    half = kept_ref.shape[1]
    first = side_of(flip) == 0
    own = kept_ref[...].astype(jnp.float32) + taken_ref[...].astype(jnp.float32)
    other = other_kept[...].astype(jnp.float32) + other_taken[...].astype(jnp.float32)
    tokens = tokens_ref[...].astype(jnp.float32)
    left = tokens[:, :half] + jnp.where(first, own, other)
    right = tokens[:, half:] + jnp.where(first, other, own)
    out_ref[:, :half] = left.astype(jnp.bfloat16)
    out_ref[:, half:] = right.astype(jnp.bfloat16)


def attend(
    steps, taking, near_ref, far_ref, keys_ref, values_ref, lengths_ref, place_ref, after, out_ref
):
    slots, span, width = keys_ref.shape
    rows = slots
    kv_local = width // HD
    heads = kv_local * GROUP
    each = heads + 2 * kv_local
    me = lax.axis_index("wide")
    shift = int(math.log2(rows))
    half = near_ref.shape[0]
    head_of = lax.broadcasted_iota(jnp.int32, (heads, 1), 0)
    positions = lax.broadcasted_iota(jnp.int32, (heads, span), 1)

    def by_group(pieces):
        result = pieces[0]
        for g in range(1, kv_local):
            result = jnp.where(head_of >= g * GROUP, pieces[g], result)
        return result

    for order, slot in enumerate(taking):
        request = place_ref[slot]
        at = (place_of(request >> shift, me, steps) << shift) | (request & (rows - 1))
        at = at * each
        inside = pl.ds(pl.multiple_of(jnp.where(at < half, at, at - half), each), each)
        block = jnp.where(at < half, near_ref[inside, :], far_ref[inside, :])
        query = block[:heads]
        own = block[heads:].astype(jnp.float32)
        own_key = by_group([own[g : g + 1] for g in range(kv_local)])
        own_value = by_group([own[kv_local + g : kv_local + g + 1] for g in range(kv_local)])
        own_score = jnp.sum(query.astype(jnp.float32) * own_key, axis=1, keepdims=True) * SCALE
        scores = by_group(
            [
                lax.dot_general(
                    query,
                    keys_ref[slot, :, g * HD : (g + 1) * HD],
                    (((1,), (1,)), ((), ())),
                    preferred_element_type=jnp.float32,
                )
                for g in range(kv_local)
            ]
        )
        scores = jnp.where(positions < lengths_ref[slot], scores * SCALE, -jnp.inf)
        row_max = jnp.maximum(jnp.max(scores, axis=1, keepdims=True), own_score)
        weights = jnp.exp(scores - row_max)
        own_weight = jnp.exp(own_score - row_max)
        total = jnp.sum(weights, axis=1, keepdims=True) + own_weight
        probs = (weights / total).astype(jnp.bfloat16)
        own_prob = (own_weight / total).astype(jnp.bfloat16).astype(jnp.float32)
        mixed = by_group(
            [
                jnp.dot(
                    probs,
                    values_ref[slot, :, g * HD : (g + 1) * HD],
                    preferred_element_type=jnp.float32,
                )
                for g in range(kv_local)
            ]
        )
        out_ref[order * heads : (order + 1) * heads, :] = mixed + own_prob * own_value


def lay_out(heads, pieces, out_ref, held):
    at = 0
    for piece in pieces:
        held[at : at + piece.shape[0], :] = piece[...]
        at += piece.shape[0]
    for head in range(heads):
        out_ref[:, head * HD : (head + 1) * HD] = held[
            pl.ds(head, out_ref.shape[0], stride=heads), :
        ].astype(jnp.bfloat16)


def attend_last(steps, taking, heads, *refs):
    *ins, early, out_ref, late, held = refs
    attend(steps, taking, *ins, late)
    lay_out(heads, [early, late], out_ref, held)


def make_local(wide):
    steps = steps_of(wide)
    head_steps = [*steps[1:-2], *steps[:1], *steps[-2:]]

    def local(
        queries,
        new_keys,
        new_values,
        key_cache,
        value_cache,
        lengths,
        assignment,
        tokens,
        norm_gain,
        routes,
        route_logits,
        w_gate,
        w_up,
        w_down,
    ):
        rows, width = tokens.shape
        half = width // 2
        units = w_gate.shape[2]
        count = rows * wide
        each = (queries.shape[1] + 2 * new_keys.shape[1]) // HD
        core = lax.axis_index("narrow")
        bf16, f32 = jnp.bfloat16, jnp.float32
        heads_local = queries.shape[1] // HD
        dma = pltpu.SemaphoreType.DMA
        piece_bytes = 2 * half * units

        got = cross(tokens, wide, steps[0])
        heads_in = [queries, new_keys, new_values]
        row_in = [tokens, norm_gain[None]]
        heads, *row_near = call(
            pack,
            [shape((rows * each, HD), bf16)] + [pltpu.VMEM(a.shape, a.dtype) for a in row_in],
            [distant(a) for a in heads_in + row_in],
            [pltpu.VMEM(a.shape, a.dtype) for a in heads_in]
            + [pltpu.VMEM((rows * each, HD), f32), dma((5,))],
            size=100000,
            far=range(5),
        )
        share = call(
            functools.partial(shares, steps, rows),
            shape((count, HD), f32),
            [distant(routes.T), distant(route_logits.T), heads, distant(w_gate), distant(w_up)],
            [
                pltpu.VMEM(routes.T.shape, jnp.int32),
                pltpu.VMEM(route_logits.T.shape, f32),
                dma((2,)),
            ],
            size=100000,
            far=range(5),
        )
        x = call(
            functools.partial(norm_both, steps[-2]),
            shape((2 * rows, half), bf16),
            [near(row_near[0]), got, near(row_near[1]), share, heads],
            size=100000,
            far=(3, 4),
        )

        def grown(heads, step):
            got = swap(heads, "wide", wide, step)
            return call(
                stack, shape((2 * heads.shape[0], HD), bf16), [heads, got], size=4 * heads.size
            )

        for step in steps[1:-2]:
            heads = grown(heads, step)
            x = call(
                stack_after,
                shape((2 * x.shape[0], half), bf16),
                [x, swap(x, "wide", wide, step), heads],
                size=8 * x.size,
                far=(2,),
            )
        line_steps = [steps[-2], steps[-1], steps[-2] ^ steps[-1]]
        last = cross(x, wide, line_steps[2])
        line = [cross(x, wide, line_steps[0]), swap(x, "wide", wide, line_steps[1])]
        wider = max(x.shape[0] * half // HD, heads.shape[0])
        sent_heads = call(widen, shape((wider, HD), bf16), [heads], size=4 * wider * HD)
        far_rows = swap(sent_heads, "wide", wide, steps[0])
        x, heads = call(
            stack_line,
            [shape((count, half), bf16), shape((2 * heads.shape[0], HD), bf16)],
            [x, last, line[0], far_rows, line[1], heads],
            size=8 * count * half,
        )
        got_heads = swap(heads, "wide", wide, steps[-2])

        product = 2 * count * half * units
        other_x = swap(x, "narrow", 2, 1)
        whole = pltpu.VMEM((units, half), bf16)
        hidden, down_own, down_other = call(
            functools.partial(gate_all, steps[-2]),
            [shape((count, units), bf16), whole, whole],
            [
                x,
                other_x,
                near(w_gate),
                near(w_up),
                share,
                distant(w_down),
            ],
            [dma((2, CUTS))],
            flops=4 * product,
            size=6 * piece_bytes,
            far=(5,),
        )
        heads = call(
            stack_after,
            shape((2 * heads.shape[0], HD), bf16),
            [heads, got_heads, hidden],
            size=8 * heads.size,
            far=(2,),
        )
        given = call(
            down,
            shape((count, half), bf16),
            [hidden, near(down_other), heads],
            flops=product,
            size=piece_bytes,
            far=(2,),
        )
        taken = swap(given, "narrow", 2, 1)
        far_heads = swap(heads, "wide", wide, steps[-1])
        terms = call(
            down,
            shape((count, half), f32),
            [hidden, near(down_own), given],
            flops=product,
            size=piece_bytes,
            far=(2,),
        )

        caches = [near(key_cache), near(value_cache), lengths, assignment]
        slots = queries.shape[0]
        early_slots = list(range(slots - 1))
        late_slots = list(range(slots - 1, slots))
        quarter = count // 4
        block = shape((quarter, half), bf16)
        terms, *sent = call(
            part_line,
            [shape((quarter, half), f32), block, block, block],
            [terms, taken],
            size=terms.size * 8,
        )
        taken = [
            swap(sent[1], "wide", wide, line_steps[1]),
            cross(sent[2], wide, line_steps[2]),
            cross(sent[0], wide, line_steps[0]),
        ]
        early = call(
            functools.partial(attend, head_steps, early_slots),
            shape((len(early_slots) * heads_local, HD), f32),
            [heads, far_heads, *caches, sent[0]],
            flops=2 * key_cache.size * GROUP,
            size=2 * key_cache.size,
            smem=(4, 5),
            far=(6,),
        )
        for step in reversed(steps[:-2]):
            kept = terms.shape[0] // 2
            terms, sent = call(
                combine,
                [shape((kept, half), bf16 if kept == rows else f32), shape((kept, half), bf16)],
                [terms, *taken, early],
                size=terms.size * 8,
                far=(1 + len(taken),),
            )
            taken = [swap(sent, "wide", wide, step)]
        context = call(
            functools.partial(attend_last, head_steps, late_slots, heads_local),
            shape(queries.shape, bf16),
            [heads, far_heads, *caches, sent, early],
            [
                pltpu.VMEM((len(late_slots) * heads_local, HD), f32),
                pltpu.VMEM((slots * heads_local, HD), f32),
            ],
            flops=2 * key_cache.size * GROUP,
            size=2 * key_cache.size,
            smem=(4, 5),
            far=(6,),
        )
        other_kept = swap(terms, "narrow", 2, 1)
        other_taken = cross(sent, wide, steps[0])
        mixed_out = call(
            functools.partial(finish, steps[-2]),
            shape((rows, width), bf16),
            [terms, *taken, other_kept, other_taken, tokens, distant(context)],
            size=terms.size * 8,
            far=(5,),
        )
        return (context, mixed_out)

    return local


def solution(mesh):
    placed = (
        P(("groups", "wide"), "narrow"),
        P(("groups", "wide"), "narrow"),
        P(("groups", "wide"), "narrow"),
        P(("groups", "wide"), None, "narrow"),
        P(("groups", "wide"), None, "narrow"),
        P(("groups", "wide")),
        P(("groups", "wide")),
        P(("groups", "wide"), None),
        P(),
        P("groups", None),
        P("groups", None),
        P("narrow", None, "wide"),
        P("narrow", None, "wide"),
        P("narrow", "wide", None),
    )
    return jax.shard_map(
        make_local(mesh.shape["wide"]),
        mesh=mesh,
        in_specs=placed,
        out_specs=(P(("groups", "wide"), "narrow"), P(("groups", "wide"), None)),
        check_vma=False,
    )
```
